512 devices in a mesh: gx: 128 (over z, y, core), gz: 4 (over x).
Axes of the slice: x: 4, y: 4, z: 16, core: 2. Of those that a mesh axis runs over, the one named last changes fastest.
Arguments:
- level_set: float32 [8192, 4096], P(('gx', 'gz')), may hold values from -60 to 60
- neighbours: int32 [8192, 6], P(('gx', 'gz')), may hold values from -1 to 8191, as said below
- live_count: int32 [512], P(('gx', 'gz')), may hold values from 4 to 16, as said below
- dense_target: int32 [8192], P(('gx', 'gz')), may hold values from -1 to 31, as said below
Outputs:
- level_set_out: float32 [8192, 4096], P(('gx', 'gz'))
- force_grid: float32 [512, 3, 16, 256], P('gx', None, 'gz')
The draws below stay inside these ranges and needn't reach their ends.
Inputs may be any that keep to these rules, and one draw needn't show every extreme that they name: `live_count`: some device holds 16 live bricks. `neighbours`: -1 or the global slot of a live brick on a device of the same gz index whose gx index differs from the own by 1 to 3, by 0, or by exactly 128 / 2 counted round; rows of dead slots are all -1; the entries of one device that name bricks of one other gx index number at most 4, and every device reaches that for some gx index. `dense_target`: -1 exactly on dead slots.
All inputs are finite; a program needn't handle non-finite values.
Results may differ from the reference program's by a relative error of at most 0.0003.
Values sent between devices are 32-bit elements; how exact they have to be, the bound alone decides.
A program may use at most 64 MiB of HBM per device.

```python
import math
import jax
import jax.numpy as jnp
import numpy as np
from jax import lax

SIDE = 16
B_DEV = 16
CAP_H = 4
REACH = 3
DN_DEV = 4
STEPS = 3
N_GX = 128
N_GZ = 4


def live_counts(key):
    base = jax.random.fold_in(key, 101)
    key_full, key_low, key_top = jax.random.split(base, 3)
    devices = N_GX * N_GZ
    full_load = jax.random.randint(key_full, (devices,), 0, 3) == 0
    low_load = jax.random.randint(key_low, (devices,), B_DEV // 4, B_DEV // 2 + 1)
    counts = jnp.where(full_load, B_DEV, low_load)
    busiest = jax.random.randint(key_top, (), 0, devices)
    counts = jnp.where(jnp.arange(devices) == busiest, B_DEV, counts)
    return counts.astype(jnp.int32)


def draw_live_count(key, part):
    return live_counts(key)


def near_column(column, magnitude, sign_bit):
    step = jnp.where(sign_bit == 0, magnitude, -magnitude)
    ahead = column + step
    inside = jnp.logical_and(ahead >= 0, ahead < N_GX)
    return jnp.where(inside, ahead, column - step)


def draw_neighbours(key, part):
    counts = live_counts(key)
    key = jax.random.fold_in(key, 7)
    key_kind, key_mag, key_sign, key_first, key_firsts, key_pick = jax.random.split(key, 6)
    devices = N_GX * N_GZ
    slots_all = devices * B_DEV
    row_ids = jnp.arange(slots_all)
    device_of = row_ids // B_DEV
    slot_of = row_ids % B_DEV
    is_live = slot_of < counts[device_of]
    column = device_of // N_GZ
    layer = device_of % N_GZ
    kinds = jax.random.randint(key_kind, (slots_all, 6), 0, 10)
    magnitude = jax.random.randint(key_mag, (slots_all, 6), 1, REACH + 1)
    sign_bit = jax.random.randint(key_sign, (slots_all, 6), 0, 2)
    first_mag = jax.random.randint(key_first, (devices,), 1, REACH + 1)
    first_sign = jax.random.randint(key_firsts, (devices,), 0, 2)
    sides = jnp.arange(6)[None, :]
    forced = jnp.logical_and(slot_of[:, None] == 0, sides < CAP_H)
    forced_far = jnp.logical_and(slot_of[:, None] == 0, sides == CAP_H)
    magnitude = jnp.where(forced, first_mag[device_of][:, None], magnitude)
    sign_bit = jnp.where(forced, first_sign[device_of][:, None], sign_bit)
    peer_col = near_column(column[:, None], magnitude, sign_bit)
    peer_col = jnp.where(forced_far, (column[:, None] + N_GX // 2) % N_GX, peer_col)
    pinned = jnp.logical_or(forced, forced_far)
    remote = jnp.logical_and(jnp.logical_or(kinds >= 2, pinned), is_live[:, None])
    matches = jnp.logical_and(peer_col.reshape(devices, -1)[:, :, None] == jnp.arange(N_GX)[None, None, :], remote.reshape(devices, -1)[:, :, None]).astype(jnp.int32)
    arrival = jnp.sum(jnp.cumsum(matches, 1) * matches, -1) - 1
    keep = jnp.logical_and(remote, arrival.reshape(slots_all, 6) < CAP_H)
    owner_dev = jnp.where(keep, peer_col * N_GZ + layer[:, None], device_of[:, None])
    picked = jax.random.randint(key_pick, (slots_all, 6), 0, 1 << 20) % counts[owner_dev]
    values = owner_dev * B_DEV + picked
    absent = jnp.logical_and(kinds == 0, jnp.logical_not(pinned))
    usable = jnp.logical_and(is_live[:, None], jnp.logical_not(absent))
    return jnp.where(usable, values, -1).astype(jnp.int32)


def draw_dense_target(key, part):
    counts = live_counts(key)
    key = jax.random.fold_in(key, 9)
    slots_all = N_GX * N_GZ * B_DEV
    row_ids = jnp.arange(slots_all)
    is_live = row_ids % B_DEV < counts[row_ids // B_DEV]
    targets = jax.random.randint(key, (slots_all,), 0, DN_DEV * 8)
    return jnp.where(is_live, targets, -1).astype(jnp.int32)


def draw_level_set(key, part):
    key = jax.random.fold_in(key, 11)
    key_dir, key_off, key_rough = jax.random.split(key, 3)
    bricks = N_GX * N_GZ * B_DEV
    cell_ids = jnp.arange(SIDE * SIDE * SIDE)
    centre = (SIDE - 1) / 2.0
    coord_x = (cell_ids // (SIDE * SIDE)).astype(jnp.float32) - centre
    coord_y = (cell_ids // SIDE % SIDE).astype(jnp.float32) - centre
    coord_z = (cell_ids % SIDE).astype(jnp.float32) - centre
    normals = jnp.clip(jax.random.normal(key_dir, (bricks, 3), jnp.float32), -3.0, 3.0) * 0.7
    offsets = jax.random.uniform(key_off, (bricks, 1), jnp.float32, -5.0, 5.0)
    roughness = jnp.clip(jax.random.normal(key_rough, (bricks, SIDE * SIDE * SIDE), jnp.float32), -3.0, 3.0) * 0.4
    return normals[:, 0:1] * coord_x[None, :] + normals[:, 1:2] * coord_y[None, :] + normals[:, 2:3] * coord_z[None, :] + offsets + roughness


def setup_inputs(seed: int = 0) -> dict:
    seeds = jax.random.split(jax.random.key(seed), 5)
    return {
        "level_set": draw_level_set(jax.random.fold_in(seeds[4], 71), 0),
        "neighbours": draw_neighbours(jax.random.fold_in(seeds[4], 71), 0),
        "live_count": draw_live_count(jax.random.fold_in(seeds[4], 71), 0),
        "dense_target": draw_dense_target(jax.random.fold_in(seeds[4], 71), 0),
    }


STEP_SIZE = 0.3
WENO_EPS = 1e-06
BAND_WIDTH = 1.5
OPPOSITE = np.array([1, 0, 3, 2, 5, 4], np.int32)

def to_strips(values, axis_id):
    leading = values.shape[:-1]
    block_cube = values.reshape(leading + (SIDE, SIDE, SIDE))
    if axis_id == 1:
        block_cube = jnp.swapaxes(block_cube, -3, -2)
    elif axis_id == 2:
        block_cube = jnp.moveaxis(block_cube, -1, -3)
    return block_cube.reshape(leading + (SIDE, SIDE * SIDE))

def from_strips(strips, axis_id):
    leading = strips.shape[:-2]
    block_cube = strips.reshape(leading + (SIDE, SIDE, SIDE))
    if axis_id == 1:
        block_cube = jnp.swapaxes(block_cube, -3, -2)
    elif axis_id == 2:
        block_cube = jnp.moveaxis(block_cube, -3, -1)
    return block_cube.reshape(leading + (SIDE * SIDE * SIDE,))

def face_table(surface, layers):
    pieces = []
    for axis_id in range(3):
        strips = to_strips(surface, axis_id)
        pieces.append(strips[:, :layers])
        pieces.append(strips[:, SIDE - layers:])
    stacked = jnp.stack(pieces, 1)
    return stacked.reshape(surface.shape[0] * 6, layers * SIDE * SIDE)

def square(values):
    return values * values

def weno(first, second, middle, fourth, fifth):
    stencil_one = first / 3.0 - 7.0 * second / 6.0 + 11.0 * middle / 6.0
    stencil_two = -second / 6.0 + 5.0 * middle / 6.0 + fourth / 3.0
    stencil_three = middle / 3.0 + 5.0 * fourth / 6.0 - fifth / 6.0
    smooth_one = 13.0 / 12.0 * square(first - 2.0 * second + middle) + 0.25 * square(first - 4.0 * second + 3.0 * middle)
    smooth_two = 13.0 / 12.0 * square(second - 2.0 * middle + fourth) + 0.25 * square(second - fourth)
    smooth_three = 13.0 / 12.0 * square(middle - 2.0 * fourth + fifth) + 0.25 * square(3.0 * middle - 4.0 * fourth + fifth)
    weight_one = 0.1 / square(WENO_EPS + smooth_one)
    weight_two = 0.6 / square(WENO_EPS + smooth_two)
    weight_three = 0.3 / square(WENO_EPS + smooth_three)
    combined = weight_one * stencil_one + weight_two * stencil_two + weight_three * stencil_three
    return combined / (weight_one + weight_two + weight_three)

def extend(strips, ghost_low, ghost_high, missing_low, missing_high):
    low_side = jnp.where(missing_low[:, None, None], jnp.broadcast_to(strips[:, :1], ghost_low.shape), ghost_low)
    high_side = jnp.where(missing_high[:, None, None], jnp.broadcast_to(strips[:, SIDE - 1:], ghost_high.shape), ghost_high)
    return jnp.concatenate([low_side, strips, high_side], 1)

def reinit_step(surface, start, ghosts, missing):
    sign_speed = start / jnp.sqrt(start * start + 1.0)
    grad_sq = jnp.zeros_like(surface)
    for axis_id in range(3):
        strips = to_strips(surface, axis_id)
        extended = extend(strips, ghosts[:, 2 * axis_id], ghosts[:, 2 * axis_id + 1], missing[:, 2 * axis_id], missing[:, 2 * axis_id + 1])
        differences = extended[:, 1:] - extended[:, :-1]
        upwind_left = weno(differences[:, 0:SIDE], differences[:, 1:SIDE + 1], differences[:, 2:SIDE + 2], differences[:, 3:SIDE + 3], differences[:, 4:SIDE + 4])
        upwind_right = weno(differences[:, 5:SIDE + 5], differences[:, 4:SIDE + 4], differences[:, 3:SIDE + 3], differences[:, 2:SIDE + 2], differences[:, 1:SIDE + 1])
        outward = jnp.maximum(square(jnp.maximum(upwind_left, 0.0)), square(jnp.minimum(upwind_right, 0.0)))
        inward = jnp.maximum(square(jnp.minimum(upwind_left, 0.0)), square(jnp.maximum(upwind_right, 0.0)))
        chosen = jnp.where(to_strips(start, axis_id) > 0.0, outward, inward)
        grad_sq = grad_sq + from_strips(chosen, axis_id)
    return surface - STEP_SIZE * sign_speed * (jnp.sqrt(grad_sq) - 1.0)

def force_of(surface, rim_layers, missing):
    laplace = jnp.zeros_like(surface)
    gradient = []
    for axis_id in range(3):
        strips = to_strips(surface, axis_id)
        extended = extend(strips, rim_layers[:, 2 * axis_id], rim_layers[:, 2 * axis_id + 1], missing[:, 2 * axis_id], missing[:, 2 * axis_id + 1])
        laplace = laplace + from_strips(extended[:, 2:] - 2.0 * extended[:, 1:-1] + extended[:, :-2], axis_id)
        gradient.append(from_strips(0.5 * (extended[:, 2:] - extended[:, :-2]), axis_id))
    smeared_delta = jnp.where(jnp.abs(surface) < BAND_WIDTH, (1.0 + jnp.cos(math.pi * surface / BAND_WIDTH)) / (2.0 * BAND_WIDTH), 0.0)
    forces = jnp.stack(gradient, 1) * (laplace * smeared_delta)[:, None, :]
    half_side = SIDE // 2
    coarsened = forces.reshape(surface.shape[0], 3, half_side, 2, half_side, 2, half_side, 2).mean(axis=(3, 5, 7))
    return coarsened.reshape(surface.shape[0], 3 * half_side ** 3)

def place_octants(gathered, dense_count):
    half_side = SIDE // 2
    shaped = gathered.reshape(dense_count, 2, 2, 2, 3, half_side, half_side, half_side)
    moved = jnp.transpose(shaped, (0, 4, 3, 7, 1, 5, 2, 6))
    return moved.reshape(dense_count, 3, SIDE, SIDE * SIDE)

def reference(level_set, neighbours, live_count, dense_target):
    brick_count = level_set.shape[0]
    row_ids = jnp.arange(brick_count)
    is_live = row_ids % B_DEV < live_count[row_ids // B_DEV]
    missing = neighbours < 0
    face_rows = jnp.where(missing, 0, neighbours) * 6 + OPPOSITE[None, :]

    def by_group(values):
        return values.reshape((N_GX, -1) + values.shape[1:])
    surface = level_set
    for pseudo_step in range(STEPS):
        faces_all = face_table(surface, 3)
        ghosts = faces_all[face_rows].reshape(brick_count, 6, 3, SIDE * SIDE)
        surface = lax.map(lambda items: reinit_step(items[0], items[1], items[2], items[3]), (by_group(surface), by_group(level_set), by_group(ghosts), by_group(missing))).reshape(brick_count, -1)
    faces_one = face_table(surface, 1)
    rim_layers = faces_one[face_rows].reshape(brick_count, 6, 1, SIDE * SIDE)
    coarsened = lax.map(lambda items: force_of(items[0], items[1], items[2]), (by_group(surface), by_group(rim_layers), by_group(missing))).reshape(brick_count, -1)
    level_set_out = jnp.where(is_live[:, None], surface, 0.0)
    selector = (by_group(dense_target)[:, :, None] == jnp.arange(DN_DEV * 8)[None, None, :]).astype(jnp.float32)
    gathered = jnp.einsum('cmk,cmv->ckv', selector, by_group(coarsened), precision=lax.Precision.HIGHEST)
    force_grid = place_octants(gathered.reshape(N_GX * DN_DEV * 8, -1), N_GX * DN_DEV)
    return (level_set_out, force_grid)
```

```python
import functools
import math

import jax
import jax.numpy as jnp
from jax import lax
from jax.experimental import pallas as pl
from jax.experimental.pallas import tpu as pltpu
from jax.sharding import PartitionSpec as P

SIDE = 16
SLOTS = 16
DENSE = 4
STEPS = 3
ROUNDS = STEPS + 1
BAND_WIDTH = 1.5
MESH = pl.DeviceIdType.MESH

PEERS = (0, 1, 2, 4, 5, 6, 7)
AXIS_ROWS = 512


def facing(peer):
    return 7 if peer == 7 else 6 - peer


def exchange(values, width, masks):
    count = len(values)
    bits = count.bit_length() - 1
    rolled = [v if j == 0 else pltpu.roll(v, j * width, 1) for j, v in enumerate(values)]
    moved = [rolled[-i % count] for i in range(count)]
    for bit in range(bits):
        moved = [jnp.where(masks[bit], moved[(i - (1 << bit)) % count], moved[i]) for i in range(count)]
    return [v if i == 0 else pltpu.roll(v, 128 - i * width, 1) for i, v in enumerate(moved)]


def lane_masks(rows, width, bits):
    lanes = lax.broadcasted_iota(jnp.int32, (rows, 128), 1)
    return [(lanes & (width << bit)) != 0 for bit in range(bits)]


def weno_axis(u, first, last, sigma, store):
    d = {j: u[j] - u[j - 1] for j in range(first - 2, last + 3)}
    e = {j: d[j + 1] - d[j] for j in range(first - 2, last + 2)}
    s = {j: e[j] - e[j - 1] for j in range(first - 1, last + 2)}
    t = {j: s[j + 1] - s[j] for j in range(first - 1, last + 1)}
    r1, r2, r3 = {}, {}, {}
    for j in range(first - 1, last + 2):
        base = (13.0 / 3.0) * (s[j] * s[j]) + 4e-6
        if j <= last - 1:
            lean = (e[j] + e[j]) + s[j]
            r = pltpu.reciprocal(base + lean * lean, approx=True)
            r1[j] = r * r
        if first <= j <= last:
            lean = e[j] + e[j - 1]
            r = pltpu.reciprocal(base + lean * lean, approx=True)
            r2[j] = 6.0 * (r * r)
        if j >= first + 1:
            lean = s[j] - (e[j - 1] + e[j - 1])
            r = pltpu.reciprocal(base + lean * lean, approx=True)
            r3[j] = r * r
    for i in range(first, last):
        half = 0.5 * t[i]
        left = 3.0 * d[i] + (e[i] + 0.5 * e[i - 1])
        right = left - half
        w3 = 3.0 * r3[i + 1]
        den = (r1[i - 1] + r2[i]) + w3
        num = r1[i - 1] * t[i - 1] + w3 * half
        left = left - num * pltpu.reciprocal(den, approx=True)
        w3 = 3.0 * r1[i]
        den = (r3[i + 2] + r2[i + 1]) + w3
        num = r3[i + 2] * t[i + 1] + w3 * half
        right = right + num * pltpu.reciprocal(den, approx=True)
        m = jnp.maximum(jnp.maximum(sigma(i) * left, -sigma(i) * right), 0.0)
        store(i, m * m)


def split3(x):
    hi = x.astype(jnp.bfloat16)
    rest = x - hi.astype(jnp.float32)
    mid = rest.astype(jnp.bfloat16)
    low = (rest - mid.astype(jnp.float32)).astype(jnp.bfloat16)
    return hi, mid, low


def as_one(mask):
    return jnp.where(mask, 1.0, 0.0).astype(jnp.bfloat16)


def dot_rows(a, b):
    return lax.dot_general(a, b, (((0,), (0,)), ((), ())), preferred_element_type=jnp.float32)


def dot(a, b):
    return lax.dot_general(a, b, (((1,), (0,)), ((), ())), preferred_element_type=jnp.float32)


def kernel(n_gx, n_gz, nb, live, target, start, level_out, part_out,
           u, faces, ghost, sigma, grad, speed, missing, near_col, far_col, force, request, heard,
           sends, recvs, fsend, frecv,
           request_sent, request_got, sent, got, fsent, fgot):
    me = lax.axis_index("gx")
    layer = lax.axis_index("gz")

    def peer_id(peer):
        step = n_gx // 2 if peer == 7 else peer - 3
        return {"gx": lax.rem(me + step + n_gx, n_gx)}

    barrier = pltpu.get_barrier_semaphore()
    for peer in PEERS:
        pl.semaphore_signal(barrier, inc=1, device_id=peer_id(peer), device_id_type=MESH)
    for turn in range(1, n_gz):
        pl.semaphore_signal(barrier, inc=1, device_id={"gz": lax.rem(layer + turn, n_gz)}, device_id_type=MESH)

    square_rows = lax.broadcasted_iota(jnp.int32, (128, 128), 0)
    square_lanes = lax.broadcasted_iota(jnp.int32, (128, 128), 1)
    entry = [jnp.broadcast_to(nb[:, side:side + 1], (16, 128)) for side in range(6)]
    entry = jnp.concatenate(entry + [jnp.full((32, 128), -1, jnp.int32)], 0)
    held = entry >= 0
    away = (entry >> (SLOTS * n_gz).bit_length() - 1) - me + 3
    kind = jnp.minimum(away & (n_gx - 1), 7)
    remote = jnp.logical_and(held, kind != 3)
    face = ((square_rows >> 4) ^ 1) * 16 + (entry & 15)
    mine = as_one(jnp.logical_and(remote, kind == square_lanes))
    before = dot(as_one(square_lanes < square_rows), mine)
    rank = dot((before * mine.astype(jnp.float32)).astype(jnp.bfloat16), jnp.ones((128, 128), jnp.bfloat16))
    slot = kind.astype(jnp.float32) * 8.0 + rank
    slot = jnp.where(remote, slot, -16.0)
    lane_ids = square_lanes.astype(jnp.float32)
    face = face.astype(jnp.float32)
    asked = dot_rows(as_one(slot == lane_ids), face.astype(jnp.bfloat16))
    asked = asked + dot_rows(as_one(slot + 4.0 == lane_ids), (face + 128.0).astype(jnp.bfloat16))
    request[...] = asked[:64].reshape(8, 8, 128)
    far_col[...] = slot[:96]
    near_col[...] = jnp.where(jnp.logical_and(held, kind == 3), face, -16.0)[:96]
    missing[...] = jnp.where(held, 0.0, 1.0)[:96]
    faces[96:, :] = jnp.zeros((32, 768), jnp.float32)

    pl.semaphore_wait(barrier, len(PEERS) + n_gz - 1)
    for peer in PEERS:
        pltpu.make_async_remote_copy(
            src_ref=request.at[peer], dst_ref=heard.at[facing(peer)],
            send_sem=request_sent.at[peer], recv_sem=request_got.at[facing(peer)],
            device_id=peer_id(peer), device_id_type=MESH).start()

    coarse_masks = lane_masks(16, 16, 3)
    fine_masks = lane_masks(16, 1, 4)

    def rows_of(axis, position, tile):
        return pl.ds(axis * AXIS_ROWS + position * 32 + tile * 16, 16)

    def keep_face(axis, position, tile, value):
        if 3 <= position < 13:
            return
        side = 2 * axis + (position >= 13)
        at = ((position % 13) * 2 + tile) * 128
        faces[side * 16:side * 16 + 16, at:at + 128] = value

    def spread(tile, x_of):
        ys = []
        for ytile in range(2):
            ys += exchange([x_of(i, ytile) for i in range(8)], 16, coarse_masks)
        for y in range(16):
            u[rows_of(1, y, tile), :] = ys[y]
            keep_face(1, y, tile, ys[y])
        zs = exchange(ys, 1, fine_masks)
        for z in range(16):
            u[rows_of(2, z, tile), :] = zs[z]
            keep_face(2, z, tile, zs[z])
        return ys, zs

    for tile in range(2):
        tops = {}
        for i in range(8):
            for ytile in range(2):
                x = tile * 8 + i
                value = start[:, x * 256 + ytile * 128:x * 256 + ytile * 128 + 128]
                u[rows_of(0, x, ytile), :] = value
                keep_face(0, x, ytile, value)
                sigma[rows_of(0, x, ytile), :] = jnp.where(value > 0.0, 1.0, -1.0)
                speed[rows_of(0, x, ytile), :] = 0.1 * value * lax.rsqrt(value * value + 1.0)
                tops[i, ytile] = value
        ys, zs = spread(tile, lambda i, ytile: tops[i, ytile])
        for p in range(16):
            sigma[rows_of(1, p, tile), :] = jnp.where(ys[p] > 0.0, 1.0, -1.0)
            sigma[rows_of(2, p, tile), :] = jnp.where(zs[p] > 0.0, 1.0, -1.0)

    for peer in PEERS:
        pltpu.make_async_remote_copy(
            src_ref=request.at[peer], dst_ref=heard.at[peer],
            send_sem=request_sent.at[peer], recv_sem=request_got.at[peer],
            device_id=peer_id(peer), device_id_type=MESH).wait()

    def copy_of(turn, peer, into):
        return pltpu.make_async_remote_copy(
            src_ref=sends.at[turn, peer], dst_ref=recvs.at[turn, into],
            send_sem=sent.at[turn, peer], recv_sem=got.at[turn, into],
            device_id=peer_id(peer), device_id_type=MESH)

    def serve(turn):
        hi, mid, low = split3(faces[...])
        cols = heard[...].reshape(64, 128)
        left = as_one(cols == lane_ids[:64])
        right = as_one(cols == lane_ids[:64] + 128.0)
        both = jnp.concatenate([left, left], 1)
        out = dot(both, jnp.concatenate([hi[:, :384], mid[:, :384]], 0))
        both = jnp.concatenate([right, right], 1)
        out = out + dot(both, jnp.concatenate([hi[:, 384:], mid[:, 384:]], 0))
        both = jnp.concatenate([left, right], 1)
        out = out + dot(both, jnp.concatenate([low[:, :384], low[:, 384:]], 0))
        sends[turn] = out.reshape(8, 8, 384)
        for peer in PEERS:
            copy_of(turn, peer, facing(peer)).start()
        near = as_one(near_col[...] == lane_ids[:96])
        out = dot(jnp.concatenate([near, near], 1), jnp.concatenate([hi, mid], 0)) + dot(near, low)
        for side in range(6):
            for part in range(6):
                at = (side * 6 + part) * 16
                ghost[at:at + 16, :] = out[side * 16:side * 16 + 16, part * 128:part * 128 + 128]

    def fetch(turn):
        for peer in PEERS:
            copy_of(turn, peer, peer).wait()
        hi, mid, low = split3(jnp.concatenate([recvs[turn, c] if c in PEERS else jnp.zeros((8, 384), jnp.float32)
                                               for c in range(8)], 0))
        arrived = jnp.concatenate([hi, mid, low, jnp.zeros_like(low)], 0)
        fold = jnp.where(lane_ids[:96] >= 64.0, lane_ids[:96] - 64.0, lane_ids[:96])
        for half in range(2):
            pick = as_one(far_col[...] + 4.0 * half == fold)
            out = dot(jnp.concatenate([pick, pick], 1), arrived)
            for side in range(6):
                for part in range(3):
                    at = (side * 6 + half * 3 + part) * 16
                    ghost[at:at + 16, :] += out[side * 16:side * 16 + 16, part * 128:part * 128 + 128]

    def column_rows(axis, position, column):
        return pl.ds(axis * AXIS_ROWS + position * 32 + column * 8, 8)

    def ghosts_at(axis, high, layer_id, column, edge):
        values = ghost[pl.ds((2 * axis + high) * 96 + layer_id * 32 + column * 8, 8), :]
        gone = missing[pl.ds((2 * axis + high) * 16 + (column % 2) * 8, 8), :]
        return jnp.where(gone > 0.0, edge, values)

    def weno_part(index, low, high):
        axis, column = index // 4, index % 4
        load = lambda i: u[column_rows(axis, i, column), :]
        signs = lambda i: sigma[column_rows(axis, i, column), :]

        def store(i, value):
            grad[column_rows(axis, i, column), :] = value

        if low == 3:
            values = {i: load(i) for i in range(16)}
            weno_axis(values, 3, 13, signs, store)
            return
        values = {i: load(i) for i in range(6)}
        for i in range(3):
            values[i - 3] = ghosts_at(axis, 0, i, column, values[0])
        weno_axis(values, 0, 3, signs, store)
        values = {i: load(i) for i in range(10, 16)}
        for i in range(3):
            values[16 + i] = ghosts_at(axis, 1, i, column, values[15])
        weno_axis(values, 13, 16, signs, store)

    def step(turn, carry):
        serve(turn)

        def inner(index, c):
            weno_part(index, 3, 13)
            return c

        def outer(index, c):
            weno_part(index, 0, 16)
            return c

        lax.fori_loop(0, 12, inner, 0)
        fetch(turn)
        lax.fori_loop(0, 12, outer, 0)

        for tile in range(2):
            sums = exchange([grad[rows_of(2, z, tile), :] for z in range(16)], 1, fine_masks)
            sums = [sums[y] + grad[rows_of(1, y, tile), :] for y in range(16)]
            fresh = {}
            for ytile in range(2):
                xs = exchange(sums[ytile * 8:ytile * 8 + 8], 16, coarse_masks)
                for i in range(8):
                    rows = rows_of(0, tile * 8 + i, ytile)
                    steep = jnp.sqrt(xs[i] + grad[rows, :])
                    value = u[rows, :] - speed[rows, :] * (steep - 3.0)
                    u[rows, :] = value
                    keep_face(0, tile * 8 + i, ytile, value)
                    fresh[i, ytile] = value
            spread(tile, lambda i, ytile: fresh[i, ytile])
        return carry

    lax.fori_loop(0, STEPS, step, 0)

    serve(STEPS)
    keep = lax.broadcasted_iota(jnp.int32, (16, 128), 0) < live[0]
    for x in range(16):
        for ytile in range(2):
            at = x * 256 + ytile * 128
            level_out[:, at:at + 128] = jnp.where(keep, u[rows_of(0, x, ytile), :], 0.0)
    fetch(STEPS)

    def rim(axis, high, tile, edge):
        values = ghost[pl.ds((2 * axis + high) * 96 + (2 - 2 * high) * 32 + tile * 16, 16), :]
        return jnp.where(missing[pl.ds((2 * axis + high) * 16, 16), :] > 0.0, edge, values)

    def beside(axis, position, tile):
        here = u[rows_of(axis, position, tile), :]
        low = rim(axis, 0, tile, here) if position == 0 else u[rows_of(axis, position - 1, tile), :]
        high = rim(axis, 1, tile, here) if position == 15 else u[rows_of(axis, position + 1, tile), :]
        return (high + low) - (here + here), high - low, here

    for tile in range(2):
        lap_y, grad_x = [], []
        for ytile in range(2):
            parts = [beside(0, tile * 8 + i, ytile) for i in range(8)]
            lap_y += exchange([p[0] for p in parts], 16, coarse_masks)
            grad_x += exchange([p[1] for p in parts], 16, coarse_masks)
        parts = [beside(1, y, tile) for y in range(16)]
        laps = exchange([lap_y[y] + parts[y][0] for y in range(16)], 1, fine_masks)
        grad_x = exchange(grad_x, 1, fine_masks)
        grad_y = exchange([p[1] for p in parts], 1, fine_masks)
        held = None
        for z in range(16):
            lap, grad_z, here = beside(2, z, tile)
            lap = lap + laps[z]
            v2 = jnp.minimum(here * here, BAND_WIDTH * BAND_WIDTH) * ((math.pi / 3.0) ** 2)
            wave = 1.0 / 479001600.0
            for power in (-1.0 / 3628800.0, 1.0 / 40320.0, -1.0 / 720.0, 1.0 / 24.0, -0.5, 1.0):
                wave = wave * v2 + power
            lap = jnp.where(jnp.abs(here) < BAND_WIDTH, lap * (wave * wave * (2.0 / 3.0)), 0.0)
            forces = [lap * grad_x[z], lap * grad_y[z], lap * grad_z]
            if z % 2 == 0:
                held = forces
            else:
                for a in range(3):
                    force[a, pl.ds(z // 2 * 16, 16), tile * 128:tile * 128 + 128] = held[a] + forces[a]

    r = lax.broadcasted_iota(jnp.int32, (256, 256), 0)
    l = lax.broadcasted_iota(jnp.int32, (256, 256), 1)
    same = jnp.logical_and((r >> 5) == ((l >> 4) & 7), ((r >> 1) & 7) == (l & 7))
    average = jnp.where(same, 1.0 / 16.0, 0.0).astype(jnp.bfloat16)
    lanes = lax.broadcasted_iota(jnp.int32, (16, 256), 1)
    brick_rows = lax.broadcasted_iota(jnp.int32, (16, 256), 0)
    lane_bricks = lax.broadcasted_iota(jnp.int32, (64, 128), 1)
    by_row = jnp.zeros((16, 256), jnp.int32)
    by_lane = jnp.full((64, 128), -1, jnp.int32)
    for b in range(16):
        by_row = jnp.where(brick_rows == b, target[b], by_row)
        by_lane = jnp.where((lane_bricks & 15) == b, target[b], by_lane)
    octant = jnp.logical_and(((by_row >> 2) & 1) == (lanes >> 7), ((by_row >> 1) & 1) == ((lanes >> 3) & 1))
    octant = jnp.where(octant, 1.0, 0.0)
    out_rows = lax.broadcasted_iota(jnp.int32, (64, 128), 0)
    pick = jnp.logical_and((by_lane >> 3) == (out_rows & 3), (by_lane & 1) == (out_rows >> 5))
    pick = jnp.logical_and(pick, (lane_bricks >> 4) == ((out_rows >> 2) & 7))
    pick = jnp.where(pick, 1.0, 0.0).astype(jnp.bfloat16)
    share = 64 // n_gz
    for a in range(3):
        hi, mid, low = split3(force[a])
        block = dot(hi, average) + (dot(mid, average) + dot(low, average))
        block = (block.reshape(8, 16, 256) * octant[None]).reshape(128, 256)
        hi, mid, low = split3(block)
        result = dot(pick, hi) + (dot(pick, mid) + dot(pick, low))
        for g in range(n_gz):
            fsend[g, a] = result[g * share:(g + 1) * share]

    def part_copy(turn):
        to = lax.rem(layer + turn, n_gz)
        return pltpu.make_async_remote_copy(
            src_ref=fsend.at[to], dst_ref=frecv.at[turn - 1],
            send_sem=fsent.at[turn - 1], recv_sem=fgot.at[turn - 1],
            device_id={"gz": to}, device_id_type=MESH)

    for turn in range(1, n_gz):
        part_copy(turn).start()
    total = fsend[layer]
    for turn in range(1, n_gz):
        part_copy(turn).wait()
        total = total + frecv[turn - 1]
    part_out[...] = total


def shards(n_gx, n_gz, level_set, neighbours, live_count, dense_target):
    share = 64 // n_gz
    smem = pl.BlockSpec(memory_space=pltpu.SMEM)
    vmem = pl.BlockSpec(memory_space=pltpu.VMEM)
    dma, f32 = pltpu.SemaphoreType.DMA, jnp.float32
    level, part = pl.pallas_call(
        functools.partial(kernel, n_gx, n_gz),
        out_shape=(jax.ShapeDtypeStruct(level_set.shape, f32), jax.ShapeDtypeStruct((3, share, 256), f32)),
        in_specs=[vmem, smem, smem, vmem],
        out_specs=(vmem, vmem),
        scratch_shapes=[
            pltpu.VMEM((3 * AXIS_ROWS, 128), f32),
            pltpu.VMEM((128, 768), f32),
            pltpu.VMEM((36 * 16, 128), f32),
            pltpu.VMEM((3 * AXIS_ROWS, 128), f32),
            pltpu.VMEM((3 * AXIS_ROWS, 128), f32),
            pltpu.VMEM((AXIS_ROWS, 128), f32),
            pltpu.VMEM((96, 128), f32),
            pltpu.VMEM((96, 128), f32),
            pltpu.VMEM((96, 128), f32),
            pltpu.VMEM((3, 128, 256), f32),
            pltpu.VMEM((8, 8, 128), f32),
            pltpu.VMEM((8, 8, 128), f32),
            pltpu.VMEM((ROUNDS, 8, 8, 384), f32),
            pltpu.VMEM((ROUNDS, 8, 8, 384), f32),
            pltpu.VMEM((n_gz, 3, share, 256), f32),
            pltpu.VMEM((n_gz - 1, 3, share, 256), f32),
            dma((8,)), dma((8,)), dma((ROUNDS, 8)), dma((ROUNDS, 8)), dma((n_gz - 1,)), dma((n_gz - 1,)),
        ],
        compiler_params=pltpu.CompilerParams(
            collective_id=0, has_side_effects=True, vmem_limit_bytes=24 << 20),
    )(neighbours, live_count, dense_target, level_set)
    part = part.reshape(3, SIDE // n_gz, DENSE, 256)
    return level, jnp.transpose(part, (2, 0, 1, 3))


def solution(mesh):
    placed = (P(("gx", "gz"), None), P(("gx", "gz"), None), P(("gx", "gz")), P(("gx", "gz")))
    return jax.shard_map(
        functools.partial(shards, mesh.shape["gx"], mesh.shape["gz"]),
        mesh=mesh,
        in_specs=placed,
        out_specs=(P(("gx", "gz"), None), P("gx", None, "gz", None)),
        check_vma=False,
    )
```

```python
import functools
import math

import jax
import jax.numpy as jnp
from jax import lax
from jax.experimental import pallas as pl
from jax.experimental.pallas import tpu as pltpu
from jax.sharding import PartitionSpec as P

SIDE = 16
SLOTS = 16
DENSE = 4
STEPS = 3
ROUNDS = STEPS + 1
BAND_WIDTH = 1.5
MESH = pl.DeviceIdType.MESH

PEERS = (7, 0, 6, 1, 5, 2, 4)
NEAR = (0, 6, 1, 5, 2, 4)
FAR = 7
AXIS_ROWS = 512


def facing(peer):
    return 7 if peer == 7 else 6 - peer


def exchange(values, width, masks):
    count = len(values)
    bits = count.bit_length() - 1
    rolled = [v if j == 0 else pltpu.roll(v, j * width, 1) for j, v in enumerate(values)]
    moved = [rolled[-i % count] for i in range(count)]
    for bit in range(bits):
        moved = [jnp.where(masks[bit], moved[(i - (1 << bit)) % count], moved[i]) for i in range(count)]
    return [v if i == 0 else pltpu.roll(v, 128 - i * width, 1) for i, v in enumerate(moved)]


def lane_masks(rows, width, bits):
    lanes = lax.broadcasted_iota(jnp.int32, (rows, 128), 1)
    return [(lanes & (width << bit)) != 0 for bit in range(bits)]


def weno_axis(u, first, last, sigma, store):
    d = {j: u[j] - u[j - 1] for j in range(first - 2, last + 3)}
    e = {j: d[j + 1] - d[j] for j in range(first - 2, last + 2)}
    s = {j: e[j] - e[j - 1] for j in range(first - 1, last + 2)}
    t = {j: s[j + 1] - s[j] for j in range(first - 1, last + 1)}
    r1, r2, r3 = {}, {}, {}
    for j in range(first - 1, last + 2):
        base = (13.0 / 3.0) * (s[j] * s[j]) + 4e-6
        if j <= last - 1:
            lean = (e[j] + e[j]) + s[j]
            r = pltpu.reciprocal(base + lean * lean, approx=True)
            r1[j] = r * r
        if first <= j <= last:
            lean = e[j] + e[j - 1]
            r = pltpu.reciprocal(base + lean * lean, approx=True)
            r2[j] = 6.0 * (r * r)
        if j >= first + 1:
            lean = s[j] - (e[j - 1] + e[j - 1])
            r = pltpu.reciprocal(base + lean * lean, approx=True)
            r3[j] = r * r
    for i in range(first, last):
        half = 0.5 * t[i]
        left = 3.0 * d[i] + (e[i] + 0.5 * e[i - 1])
        right = left - half
        w3 = 3.0 * r3[i + 1]
        den = (r1[i - 1] + r2[i]) + w3
        num = r1[i - 1] * t[i - 1] + w3 * half
        left = left - num * pltpu.reciprocal(den, approx=True)
        w3 = 3.0 * r1[i]
        den = (r3[i + 2] + r2[i + 1]) + w3
        num = r3[i + 2] * t[i + 1] + w3 * half
        right = right + num * pltpu.reciprocal(den, approx=True)
        m = jnp.maximum(jnp.maximum(sigma(i) * left, -sigma(i) * right), 0.0)
        store(i, m * m)


def split3(x):
    hi = x.astype(jnp.bfloat16)
    rest = x - hi.astype(jnp.float32)
    mid = rest.astype(jnp.bfloat16)
    low = (rest - mid.astype(jnp.float32)).astype(jnp.bfloat16)
    return hi, mid, low


def as_one(mask):
    return jnp.where(mask, 1.0, 0.0).astype(jnp.bfloat16)


def dot_rows(a, b):
    return lax.dot_general(a, b, (((0,), (0,)), ((), ())), preferred_element_type=jnp.float32)


def dot(a, b):
    return lax.dot_general(a, b, (((1,), (0,)), ((), ())), preferred_element_type=jnp.float32)


def kernel(n_gx, n_gz, table, live, target, level, level_out, part_out,
           nb, start, u, faces, ghost, sigma, grad, speed, missing, near_col, far_col, take, far_sigma, force, request, heard,
           sends, recvs, fsend, frecv,
           table_loaded, loaded, request_sent, request_got, sent, got, fsent, fgot):
    me = lax.axis_index("gx")
    layer = lax.axis_index("gz")

    def peer_id(peer):
        step = n_gx // 2 if peer == 7 else peer - 3
        return {"gx": lax.rem(me + step + n_gx, n_gx)}

    load = pltpu.make_async_copy(level, start, loaded)
    load.start()
    load_table = pltpu.make_async_copy(table, nb, table_loaded)
    load_table.start()
    barrier = pltpu.get_barrier_semaphore()
    for peer in PEERS:
        pl.semaphore_signal(barrier, inc=1, device_id=peer_id(peer), device_id_type=MESH)
    for turn in range(1, n_gz):
        pl.semaphore_signal(barrier, inc=1, device_id={"gz": lax.rem(layer + turn, n_gz)}, device_id_type=MESH)

    square_rows = lax.broadcasted_iota(jnp.int32, (128, 128), 0)
    square_lanes = lax.broadcasted_iota(jnp.int32, (128, 128), 1)
    load_table.wait()
    spots = [jnp.broadcast_to(nb[side:side + 1, :], (16, 16)) for side in range(6)]
    spots = jnp.concatenate(spots + [jnp.full((32, 16), -1, jnp.int32)], 0)
    own_spot = lax.broadcasted_iota(jnp.int32, (128, 16), 0) & 15
    own_spot = own_spot == lax.broadcasted_iota(jnp.int32, (128, 16), 1)
    entry = jnp.sum(jnp.where(own_spot, spots, 0).astype(jnp.float32), 1, keepdims=True)
    entry = jnp.broadcast_to(entry, (128, 128)).astype(jnp.int32)
    held = entry >= 0
    away = (entry >> (SLOTS * n_gz).bit_length() - 1) - me + 3
    kind = jnp.minimum(away & (n_gx - 1), 7)
    remote = jnp.logical_and(held, kind != 3)
    face = ((square_rows >> 4) ^ 1) * 16 + (entry & 15)
    mine = as_one(jnp.logical_and(remote, kind == square_lanes))
    before = dot(as_one(square_lanes < square_rows), mine)
    rank = dot((before * mine.astype(jnp.float32)).astype(jnp.bfloat16), jnp.ones((128, 128), jnp.bfloat16))
    slot = kind.astype(jnp.float32) * 8.0 + rank
    slot = jnp.where(remote, slot, -16.0)
    lane_ids = square_lanes.astype(jnp.float32)
    face = face.astype(jnp.float32)
    chosen = as_one(slot == lane_ids)
    asked = dot_rows(chosen, face.astype(jnp.bfloat16))
    asked = asked + dot_rows(as_one(slot + 4.0 == lane_ids), (face + 128.0).astype(jnp.bfloat16))
    request[...] = asked[:64].reshape(8, 8, 128)
    far_col[...] = slot[:96]
    take[...] = dot_rows(chosen, as_one(square_rows == square_lanes))[56:64]
    near_col[...] = jnp.where(jnp.logical_and(held, kind == 3), face, -16.0)[:96]
    missing[...] = jnp.where(held, 0.0, 1.0)[:96]
    faces[96:, :] = jnp.zeros((32, 1536), jnp.float32)

    pl.semaphore_wait(barrier, len(PEERS) + n_gz - 1)
    for peer in PEERS:
        pltpu.make_async_remote_copy(
            src_ref=request.at[peer], dst_ref=heard.at[facing(peer)],
            send_sem=request_sent.at[peer], recv_sem=request_got.at[facing(peer)],
            device_id=peer_id(peer), device_id_type=MESH).start()

    coarse_masks = lane_masks(16, 16, 3)
    fine_masks = lane_masks(16, 1, 4)

    def rows_of(axis, position, tile):
        return pl.ds(axis * AXIS_ROWS + position * 32 + tile * 16, 16)

    def keep_face(axis, position, tile, value):
        depth = min(position, 15 - position)
        if depth < 6:
            side = 2 * axis + (position >= 8)
            at = (depth * 2 + tile) * 128
            faces[side * 16:side * 16 + 16, at:at + 128] = value

    def spread(tile, x_of):
        ys = []
        for ytile in range(2):
            ys += exchange([x_of(i, ytile) for i in range(8)], 16, coarse_masks)
        for y in range(16):
            u[rows_of(1, y, tile), :] = ys[y]
            keep_face(1, y, tile, ys[y])
        zs = exchange(ys, 1, fine_masks)
        for z in range(16):
            u[rows_of(2, z, tile), :] = zs[z]
            keep_face(2, z, tile, zs[z])
        return ys, zs

    load.wait()
    for tile in range(2):
        tops = {}
        for i in range(8):
            for ytile in range(2):
                x = tile * 8 + i
                value = start[:, x * 256 + ytile * 128:x * 256 + ytile * 128 + 128]
                u[rows_of(0, x, ytile), :] = value
                keep_face(0, x, ytile, value)
                sigma[rows_of(0, x, ytile), :] = jnp.where(value > 0.0, 1.0, -1.0)
                speed[rows_of(0, x, ytile), :] = 0.1 * value * lax.rsqrt(value * value + 1.0)
                tops[i, ytile] = value
        ys, zs = spread(tile, lambda i, ytile: tops[i, ytile])
        for p in range(16):
            sigma[rows_of(1, p, tile), :] = jnp.where(ys[p] > 0.0, 1.0, -1.0)
            sigma[rows_of(2, p, tile), :] = jnp.where(zs[p] > 0.0, 1.0, -1.0)

    for peer in PEERS:
        pltpu.make_async_remote_copy(
            src_ref=request.at[peer], dst_ref=heard.at[peer],
            send_sem=request_sent.at[peer], recv_sem=request_got.at[peer],
            device_id=peer_id(peer), device_id_type=MESH).wait()

    def copy_of(turn, peer, into):
        return pltpu.make_async_remote_copy(
            src_ref=sends.at[turn, peer], dst_ref=recvs.at[turn, into],
            send_sem=sent.at[turn, peer], recv_sem=got.at[turn, into],
            device_id=peer_id(peer), device_id_type=MESH)

    def serve(turn):
        hi, mid, low = split3(faces[:, :768])
        cols = heard[...].reshape(64, 128)
        left = as_one(cols == lane_ids[:64])
        right = as_one(cols == lane_ids[:64] + 128.0)
        both = jnp.concatenate([left, left], 1)
        out = dot(both, jnp.concatenate([hi[:, :384], mid[:, :384]], 0))
        both = jnp.concatenate([right, right], 1)
        out = out + dot(both, jnp.concatenate([hi[:, 384:], mid[:, 384:]], 0))
        both = jnp.concatenate([left, right], 1)
        out = out + dot(both, jnp.concatenate([low[:, :384], low[:, 384:]], 0))
        sends[turn] = out.reshape(8, 8, 384)
        for peer in PEERS:
            copy_of(turn, peer, facing(peer)).start()
        near = as_one(near_col[...] == lane_ids[:96])
        out = dot(jnp.concatenate([near, near], 1), jnp.concatenate([hi, mid], 0)) + dot(near, low)
        for side in range(6):
            for part in range(6):
                at = (side * 6 + part) * 16
                ghost[at:at + 16, :] = out[side * 16:side * 16 + 16, part * 128:part * 128 + 128]

    def fetch_near(turn):
        for peer in NEAR:
            copy_of(turn, peer, peer).wait()
        none = jnp.zeros((8, 384), jnp.float32)
        hi, mid, low = split3(jnp.concatenate([recvs[turn, c] if c in NEAR else none for c in range(8)], 0))
        arrived = jnp.concatenate([hi, mid, low, jnp.zeros_like(low)], 0)
        fold = jnp.where(lane_ids[:96] >= 64.0, lane_ids[:96] - 64.0, lane_ids[:96])
        for half in range(2):
            pick = as_one(far_col[...] + 4.0 * half == fold)
            out = dot(jnp.concatenate([pick, pick], 1), arrived)
            for side in range(6):
                for part in range(3):
                    at = (side * 6 + half * 3 + part) * 16
                    ghost[at:at + 16, :] += out[side * 16:side * 16 + 16, part * 128:part * 128 + 128]

    def own_cells():
        hi, mid, low = split3(faces[...])
        one = take[...].astype(jnp.bfloat16)
        return dot(jnp.concatenate([one, one], 1), jnp.concatenate([hi, mid], 0)) + dot(one, low)

    def put_far(values):
        parts = [part.astype(jnp.float32) for part in split3(values)]
        parts = jnp.concatenate(parts + [jnp.zeros_like(values)], 0).astype(jnp.bfloat16)
        lanes = lax.broadcasted_iota(jnp.int32, (96, 32), 1)
        rows = jnp.where(lanes < 24, (lanes & 7) + 56, -1).astype(jnp.float32)
        return dot(as_one(far_col[:, :32] == rows), parts)

    def is_far(side):
        return far_col[side * 16:side * 16 + 16, :] >= 56.0

    def far_weno(turn, own):
        copy_of(turn, FAR, FAR).wait()
        came = recvs[turn, FAR]
        other = pltpu.roll(came, 4, 0)
        result = {}
        for tile in range(2):
            values = {}
            for depth in range(3):
                part = depth * 2 + tile
                from_ = came if part < 3 else other
                values[-1 - depth] = from_[:, part % 3 * 128:part % 3 * 128 + 128]
            for depth in range(6):
                at = (depth * 2 + tile) * 128
                values[depth] = own[:, at:at + 128]

            def signs(i):
                return far_sigma[:, (i * 2 + tile) * 128:(i * 2 + tile) * 128 + 128]

            def store(i, value):
                result[i * 2 + tile] = value

            weno_axis(values, 0, 3, signs, store)
        return put_far(jnp.concatenate([result[part] for part in range(6)], 1))

    def column_rows(axis, position, column):
        return pl.ds(axis * AXIS_ROWS + position * 32 + column * 8, 8)

    def ghosts_at(axis, high, depth, column, edge):
        values = ghost[pl.ds((2 * axis + high) * 96 + depth * 32 + column * 8, 8), :]
        gone = missing[pl.ds((2 * axis + high) * 16 + (column % 2) * 8, 8), :]
        return jnp.where(gone > 0.0, edge, values)

    def weno_part(index, low, high):
        axis, column = index // 4, index % 4
        load = lambda i: u[column_rows(axis, i, column), :]
        signs = lambda i: sigma[column_rows(axis, i, column), :]

        def store(i, value):
            grad[column_rows(axis, i, column), :] = value

        if low == 3:
            values = {i: load(i) for i in range(16)}
            weno_axis(values, 3, 13, signs, store)
            return
        values = {i: load(i) for i in range(6)}
        for i in range(3):
            values[-1 - i] = ghosts_at(axis, 0, i, column, values[0])
        weno_axis(values, 0, 3, signs, store)
        values = {i: load(i) for i in range(10, 16)}
        for i in range(3):
            values[16 + i] = ghosts_at(axis, 1, i, column, values[15])
        weno_axis(values, 13, 16, signs, store)

    first = own_cells()[:, :768]
    far_sigma[...] = jnp.where(first > 0.0, 1.0, -1.0)

    def step(turn, carry):
        serve(turn)

        def inner(index, c):
            weno_part(index, 3, 13)
            return c

        def outer(index, c):
            weno_part(index, 0, 16)
            return c

        lax.fori_loop(0, 12, inner, 0)
        own = own_cells()
        fetch_near(turn)
        lax.fori_loop(0, 12, outer, 0)
        fixed = far_weno(turn, own)

        def grad_at(axis, position, tile):
            value = grad[rows_of(axis, position, tile), :]
            depth = min(position, 15 - position)
            if depth >= 3:
                return value
            side = 2 * axis + (position >= 8)
            at = (depth * 2 + tile) * 128
            return jnp.where(is_far(side), fixed[side * 16:side * 16 + 16, at:at + 128], value)

        for tile in range(2):
            sums = exchange([grad_at(2, z, tile) for z in range(16)], 1, fine_masks)
            sums = [sums[y] + grad_at(1, y, tile) for y in range(16)]
            fresh = {}
            for ytile in range(2):
                xs = exchange(sums[ytile * 8:ytile * 8 + 8], 16, coarse_masks)
                for i in range(8):
                    rows = rows_of(0, tile * 8 + i, ytile)
                    steep = jnp.sqrt(xs[i] + grad_at(0, tile * 8 + i, ytile))
                    value = u[rows, :] - speed[rows, :] * (steep - 3.0)
                    u[rows, :] = value
                    keep_face(0, tile * 8 + i, ytile, value)
                    fresh[i, ytile] = value
            spread(tile, lambda i, ytile: fresh[i, ytile])
        return carry

    lax.fori_loop(0, STEPS, step, 0)

    serve(STEPS)
    keep = lax.broadcasted_iota(jnp.int32, (16, 128), 0) < live[0]
    for x in range(16):
        for ytile in range(2):
            at = x * 256 + ytile * 128
            level_out[:, at:at + 128] = jnp.where(keep, u[rows_of(0, x, ytile), :], 0.0)
    fetch_near(STEPS)
    copy_of(STEPS, FAR, FAR).wait()
    far_rim = put_far(recvs[STEPS, FAR, :, :256])

    def rim(axis, high, tile, edge):
        side = 2 * axis + high
        values = ghost[side * 96 + tile * 16:side * 96 + tile * 16 + 16, :]
        values = jnp.where(is_far(side), far_rim[side * 16:side * 16 + 16, tile * 128:tile * 128 + 128], values)
        return jnp.where(missing[side * 16:side * 16 + 16, :] > 0.0, edge, values)

    def beside(axis, position, tile):
        here = u[rows_of(axis, position, tile), :]
        low = rim(axis, 0, tile, here) if position == 0 else u[rows_of(axis, position - 1, tile), :]
        high = rim(axis, 1, tile, here) if position == 15 else u[rows_of(axis, position + 1, tile), :]
        return (high + low) - (here + here), high - low, here

    for tile in range(2):
        lap_y, grad_x = [], []
        for ytile in range(2):
            parts = [beside(0, tile * 8 + i, ytile) for i in range(8)]
            lap_y += exchange([p[0] for p in parts], 16, coarse_masks)
            grad_x += exchange([p[1] for p in parts], 16, coarse_masks)
        parts = [beside(1, y, tile) for y in range(16)]
        laps = exchange([lap_y[y] + parts[y][0] for y in range(16)], 1, fine_masks)
        grad_x = exchange(grad_x, 1, fine_masks)
        grad_y = exchange([p[1] for p in parts], 1, fine_masks)
        held = None
        for z in range(16):
            lap, grad_z, here = beside(2, z, tile)
            lap = lap + laps[z]
            v2 = jnp.minimum(here * here, BAND_WIDTH * BAND_WIDTH) * ((math.pi / 3.0) ** 2)
            wave = 1.0 / 479001600.0
            for power in (-1.0 / 3628800.0, 1.0 / 40320.0, -1.0 / 720.0, 1.0 / 24.0, -0.5, 1.0):
                wave = wave * v2 + power
            lap = jnp.where(jnp.abs(here) < BAND_WIDTH, lap * (wave * wave * (2.0 / 3.0)), 0.0)
            forces = [lap * grad_x[z], lap * grad_y[z], lap * grad_z]
            if z % 2 == 0:
                held = forces
            else:
                for a in range(3):
                    force[a, pl.ds(z // 2 * 16, 16), tile * 128:tile * 128 + 128] = held[a] + forces[a]

    r = lax.broadcasted_iota(jnp.int32, (256, 256), 0)
    l = lax.broadcasted_iota(jnp.int32, (256, 256), 1)
    same = jnp.logical_and((r >> 5) == ((l >> 4) & 7), ((r >> 1) & 7) == (l & 7))
    average = jnp.where(same, 1.0 / 16.0, 0.0).astype(jnp.bfloat16)
    lanes = lax.broadcasted_iota(jnp.int32, (16, 256), 1)
    brick_rows = lax.broadcasted_iota(jnp.int32, (16, 256), 0)
    lane_bricks = lax.broadcasted_iota(jnp.int32, (64, 128), 1)
    by_row = jnp.zeros((16, 256), jnp.int32)
    by_lane = jnp.full((64, 128), -1, jnp.int32)
    for b in range(16):
        by_row = jnp.where(brick_rows == b, target[b], by_row)
        by_lane = jnp.where((lane_bricks & 15) == b, target[b], by_lane)
    octant = jnp.logical_and(((by_row >> 2) & 1) == (lanes >> 7), ((by_row >> 1) & 1) == ((lanes >> 3) & 1))
    octant = jnp.where(octant, 1.0, 0.0)
    out_rows = lax.broadcasted_iota(jnp.int32, (64, 128), 0)
    pick = jnp.logical_and((by_lane >> 3) == (out_rows & 3), (by_lane & 1) == (out_rows >> 5))
    pick = jnp.logical_and(pick, (lane_bricks >> 4) == ((out_rows >> 2) & 7))
    pick = jnp.where(pick, 1.0, 0.0).astype(jnp.bfloat16)
    share = 64 // n_gz
    for a in range(3):
        hi, mid, low = split3(force[a])
        block = dot(hi, average) + (dot(mid, average) + dot(low, average))
        block = (block.reshape(8, 16, 256) * octant[None]).reshape(128, 256)
        hi, mid, low = split3(block)
        result = dot(pick, hi) + (dot(pick, mid) + dot(pick, low))
        for g in range(n_gz):
            fsend[g, a] = result[g * share:(g + 1) * share]

    def part_copy(turn):
        to = lax.rem(layer + turn, n_gz)
        return pltpu.make_async_remote_copy(
            src_ref=fsend.at[to], dst_ref=frecv.at[turn - 1],
            send_sem=fsent.at[turn - 1], recv_sem=fgot.at[turn - 1],
            device_id={"gz": to}, device_id_type=MESH)

    for turn in range(1, n_gz):
        part_copy(turn).start()
    total = fsend[layer]
    for turn in range(1, n_gz):
        part_copy(turn).wait()
        total = total + frecv[turn - 1]
    part_out[...] = total


def shards(n_gx, n_gz, level_set, neighbours, live_count, dense_target):
    share = 64 // n_gz
    smem = pl.BlockSpec(memory_space=pltpu.SMEM)
    vmem = pl.BlockSpec(memory_space=pltpu.VMEM)
    hbm = pl.BlockSpec(memory_space=pltpu.HBM)
    dma, f32 = pltpu.SemaphoreType.DMA, jnp.float32
    level, part = pl.pallas_call(
        functools.partial(kernel, n_gx, n_gz),
        out_shape=(jax.ShapeDtypeStruct(level_set.shape, f32), jax.ShapeDtypeStruct((3, share, 256), f32)),
        in_specs=[hbm, smem, smem, hbm],
        out_specs=(vmem, vmem),
        scratch_shapes=[
            pltpu.VMEM((6, SLOTS), jnp.int32),
            pltpu.VMEM(level_set.shape, f32),
            pltpu.VMEM((3 * AXIS_ROWS, 128), f32),
            pltpu.VMEM((128, 1536), f32),
            pltpu.VMEM((36 * 16, 128), f32),
            pltpu.VMEM((3 * AXIS_ROWS, 128), f32),
            pltpu.VMEM((3 * AXIS_ROWS, 128), f32),
            pltpu.VMEM((AXIS_ROWS, 128), f32),
            pltpu.VMEM((96, 128), f32),
            pltpu.VMEM((96, 128), f32),
            pltpu.VMEM((96, 128), f32),
            pltpu.VMEM((8, 128), f32),
            pltpu.VMEM((8, 768), f32),
            pltpu.VMEM((3, 128, 256), f32),
            pltpu.VMEM((8, 8, 128), f32),
            pltpu.VMEM((8, 8, 128), f32),
            pltpu.VMEM((ROUNDS, 8, 8, 384), f32),
            pltpu.VMEM((ROUNDS, 8, 8, 384), f32),
            pltpu.VMEM((n_gz, 3, share, 256), f32),
            pltpu.VMEM((n_gz - 1, 3, share, 256), f32),
            dma(()), dma(()), dma((8,)), dma((8,)), dma((ROUNDS, 8)), dma((ROUNDS, 8)), dma((n_gz - 1,)), dma((n_gz - 1,)),
        ],
        compiler_params=pltpu.CompilerParams(
            collective_id=0, has_side_effects=True, vmem_limit_bytes=60 << 20),
    )(neighbours.T, live_count, dense_target, level_set)
    part = part.reshape(3, SIDE // n_gz, DENSE, 256)
    return level, jnp.transpose(part, (2, 0, 1, 3))


def solution(mesh):
    placed = (P(("gx", "gz"), None), P(("gx", "gz"), None), P(("gx", "gz")), P(("gx", "gz")))
    return jax.shard_map(
        functools.partial(shards, mesh.shape["gx"], mesh.shape["gz"]),
        mesh=mesh,
        in_specs=placed,
        out_specs=(P(("gx", "gz"), None), P("gx", None, "gz", None)),
        check_vma=False,
    )
```

```python
import functools
import math

import jax
import jax.numpy as jnp
from jax import lax
from jax.experimental import pallas as pl
from jax.experimental.pallas import tpu as pltpu
from jax.sharding import PartitionSpec as P

SIDE = 16
SLOTS = 16
DENSE = 4
STEPS = 3
ROUNDS = STEPS + 1
BAND_WIDTH = 1.5
MESH = pl.DeviceIdType.MESH

PEERS = (7, 0, 6, 1, 5, 2, 4)
NEAR = (0, 6, 1, 5, 2, 4)
FAR = 7
AXIS_ROWS = 512


def facing(peer):
    return 7 if peer == 7 else 6 - peer


def exchange(values, width, masks):
    count = len(values)
    bits = count.bit_length() - 1
    rolled = [v if j == 0 else pltpu.roll(v, j * width, 1) for j, v in enumerate(values)]
    moved = [rolled[-i % count] for i in range(count)]
    for bit in range(bits):
        moved = [jnp.where(masks[bit], moved[(i - (1 << bit)) % count], moved[i]) for i in range(count)]
    return [v if i == 0 else pltpu.roll(v, 128 - i * width, 1) for i, v in enumerate(moved)]


def lane_masks(rows, width, bits):
    lanes = lax.broadcasted_iota(jnp.int32, (rows, 128), 1)
    return [(lanes & (width << bit)) != 0 for bit in range(bits)]


def weno_axis(u, first, last, sigma, store):
    d = {j: u[j] - u[j - 1] for j in range(first - 2, last + 3)}
    e = {j: d[j + 1] - d[j] for j in range(first - 2, last + 2)}
    s = {j: e[j] - e[j - 1] for j in range(first - 1, last + 2)}
    t = {j: s[j + 1] - s[j] for j in range(first - 1, last + 1)}
    r1, r2, r3 = {}, {}, {}
    for j in range(first - 1, last + 2):
        base = (13.0 / 3.0) * (s[j] * s[j]) + 4e-6
        if j <= last - 1:
            lean = (e[j] + e[j]) + s[j]
            r = pltpu.reciprocal(base + lean * lean, approx=True)
            r1[j] = r * r
        if first <= j <= last:
            lean = e[j] + e[j - 1]
            r = pltpu.reciprocal(base + lean * lean, approx=True)
            r2[j] = 6.0 * (r * r)
        if j >= first + 1:
            lean = s[j] - (e[j - 1] + e[j - 1])
            r = pltpu.reciprocal(base + lean * lean, approx=True)
            r3[j] = r * r
    for i in range(first, last):
        half = 0.5 * t[i]
        left = 3.0 * d[i] + (e[i] + 0.5 * e[i - 1])
        right = left - half
        w3 = 3.0 * r3[i + 1]
        den = (r1[i - 1] + r2[i]) + w3
        num = r1[i - 1] * t[i - 1] + w3 * half
        left = left - num * pltpu.reciprocal(den, approx=True)
        w3 = 3.0 * r1[i]
        den = (r3[i + 2] + r2[i + 1]) + w3
        num = r3[i + 2] * t[i + 1] + w3 * half
        right = right + num * pltpu.reciprocal(den, approx=True)
        m = jnp.maximum(jnp.maximum(sigma(i) * left, -sigma(i) * right), 0.0)
        store(i, m * m)


def split3(x):
    hi = x.astype(jnp.bfloat16)
    rest = x - hi.astype(jnp.float32)
    mid = rest.astype(jnp.bfloat16)
    low = (rest - mid.astype(jnp.float32)).astype(jnp.bfloat16)
    return hi, mid, low


def as_one(mask):
    return jnp.where(mask, 1.0, 0.0).astype(jnp.bfloat16)


def dot_rows(a, b):
    return lax.dot_general(a, b, (((0,), (0,)), ((), ())), preferred_element_type=jnp.float32)


def dot(a, b):
    return lax.dot_general(a, b, (((1,), (0,)), ((), ())), preferred_element_type=jnp.float32)


def kernel(n_gx, n_gz, table, live, target_in, level, level_out, part_out,
           nb, target, start, u, faces, ghost, sigma, grad, speed, missing, near_col, far_col, take, far_sigma, force, request, heard,
           sends, recvs, fsend, frecv,
           table_loaded, target_loaded, loaded, request_sent, request_got, sent, got, fsent, fgot):
    me = lax.axis_index("gx")
    layer = lax.axis_index("gz")

    def peer_id(peer):
        step = n_gx // 2 if peer == 7 else peer - 3
        return {"gx": lax.rem(me + step + n_gx, n_gx)}

    load = pltpu.make_async_copy(level, start, loaded)
    load.start()
    load_table = pltpu.make_async_copy(table, nb, table_loaded)
    load_table.start()
    load_target = pltpu.make_async_copy(target_in, target, target_loaded)
    load_target.start()
    barrier = pltpu.get_barrier_semaphore()
    for peer in PEERS:
        pl.semaphore_signal(barrier, inc=1, device_id=peer_id(peer), device_id_type=MESH)
    for turn in range(1, n_gz):
        pl.semaphore_signal(barrier, inc=1, device_id={"gz": lax.rem(layer + turn, n_gz)}, device_id_type=MESH)

    square_rows = lax.broadcasted_iota(jnp.int32, (128, 128), 0)
    square_lanes = lax.broadcasted_iota(jnp.int32, (128, 128), 1)
    load_table.wait()
    spots = [jnp.broadcast_to(nb[side:side + 1, :], (16, 16)) for side in range(6)]
    spots = jnp.concatenate(spots + [jnp.full((32, 16), -1, jnp.int32)], 0)
    own_spot = lax.broadcasted_iota(jnp.int32, (128, 16), 0) & 15
    own_spot = own_spot == lax.broadcasted_iota(jnp.int32, (128, 16), 1)
    entry = jnp.sum(jnp.where(own_spot, spots, 0).astype(jnp.float32), 1, keepdims=True)
    entry = jnp.broadcast_to(entry, (128, 128)).astype(jnp.int32)
    held = entry >= 0
    away = (entry >> (SLOTS * n_gz).bit_length() - 1) - me + 3
    kind = jnp.minimum(away & (n_gx - 1), 7)
    remote = jnp.logical_and(held, kind != 3)
    face = ((square_rows >> 4) ^ 1) * 16 + (entry & 15)
    mine = as_one(jnp.logical_and(remote, kind == square_lanes))
    before = dot(as_one(square_lanes < square_rows), mine)
    rank = dot((before * mine.astype(jnp.float32)).astype(jnp.bfloat16), jnp.ones((128, 128), jnp.bfloat16))
    slot = kind.astype(jnp.float32) * 8.0 + rank
    slot = jnp.where(remote, slot, -16.0)
    lane_ids = square_lanes.astype(jnp.float32)
    face = face.astype(jnp.float32)
    chosen = as_one(slot == lane_ids)
    asked = dot_rows(chosen, face.astype(jnp.bfloat16))
    asked = asked + dot_rows(as_one(slot + 4.0 == lane_ids), (face + 128.0).astype(jnp.bfloat16))
    request[...] = asked[:64].reshape(8, 8, 128)
    far_col[...] = slot[:96]
    take[...] = dot_rows(chosen, as_one(square_rows == square_lanes))[56:64]
    near_col[...] = jnp.where(jnp.logical_and(held, kind == 3), face, -16.0)[:96]
    missing[...] = jnp.where(held, 0.0, 1.0)[:96]
    faces[96:, :] = jnp.zeros((32, 1536), jnp.float32)

    pl.semaphore_wait(barrier, len(PEERS) + n_gz - 1)
    for peer in PEERS:
        pltpu.make_async_remote_copy(
            src_ref=request.at[peer], dst_ref=heard.at[facing(peer)],
            send_sem=request_sent.at[peer], recv_sem=request_got.at[facing(peer)],
            device_id=peer_id(peer), device_id_type=MESH).start()

    coarse_masks = lane_masks(16, 16, 3)
    fine_masks = lane_masks(16, 1, 4)

    def rows_of(axis, position, tile):
        return pl.ds(axis * AXIS_ROWS + position * 32 + tile * 16, 16)

    def keep_face(axis, position, tile, value):
        depth = min(position, 15 - position)
        if depth < 6:
            side = 2 * axis + (position >= 8)
            at = (depth * 2 + tile) * 128
            faces[side * 16:side * 16 + 16, at:at + 128] = value

    def spread(tile, x_of):
        ys = []
        for ytile in range(2):
            ys += exchange([x_of(i, ytile) for i in range(8)], 16, coarse_masks)
        for y in range(16):
            u[rows_of(1, y, tile), :] = ys[y]
            keep_face(1, y, tile, ys[y])
        zs = exchange(ys, 1, fine_masks)
        for z in range(16):
            u[rows_of(2, z, tile), :] = zs[z]
            keep_face(2, z, tile, zs[z])
        return ys, zs

    load_target.wait()
    load.wait()
    for tile in range(2):
        tops = {}
        for i in range(8):
            for ytile in range(2):
                x = tile * 8 + i
                value = start[:, x * 256 + ytile * 128:x * 256 + ytile * 128 + 128]
                u[rows_of(0, x, ytile), :] = value
                keep_face(0, x, ytile, value)
                sigma[rows_of(0, x, ytile), :] = jnp.where(value > 0.0, 1.0, -1.0)
                speed[rows_of(0, x, ytile), :] = 0.1 * value * lax.rsqrt(value * value + 1.0)
                tops[i, ytile] = value
        ys, zs = spread(tile, lambda i, ytile: tops[i, ytile])
        for p in range(16):
            sigma[rows_of(1, p, tile), :] = jnp.where(ys[p] > 0.0, 1.0, -1.0)
            sigma[rows_of(2, p, tile), :] = jnp.where(zs[p] > 0.0, 1.0, -1.0)

    for peer in PEERS:
        pltpu.make_async_remote_copy(
            src_ref=request.at[peer], dst_ref=heard.at[peer],
            send_sem=request_sent.at[peer], recv_sem=request_got.at[peer],
            device_id=peer_id(peer), device_id_type=MESH).wait()

    def copy_of(turn, peer, into):
        return pltpu.make_async_remote_copy(
            src_ref=sends.at[turn, peer], dst_ref=recvs.at[turn, into],
            send_sem=sent.at[turn, peer], recv_sem=got.at[turn, into],
            device_id=peer_id(peer), device_id_type=MESH)

    def serve(turn):
        hi, mid, low = split3(faces[:, :768])
        cols = heard[...].reshape(64, 128)
        left = as_one(cols == lane_ids[:64])
        right = as_one(cols == lane_ids[:64] + 128.0)
        both = jnp.concatenate([left, left], 1)
        out = dot(both, jnp.concatenate([hi[:, :384], mid[:, :384]], 0))
        both = jnp.concatenate([right, right], 1)
        out = out + dot(both, jnp.concatenate([hi[:, 384:], mid[:, 384:]], 0))
        both = jnp.concatenate([left, right], 1)
        out = out + dot(both, jnp.concatenate([low[:, :384], low[:, 384:]], 0))
        sends[turn] = out.reshape(8, 8, 384)
        for peer in PEERS:
            copy_of(turn, peer, facing(peer)).start()
        near = as_one(near_col[...] == lane_ids[:96])
        out = dot(jnp.concatenate([near, near], 1), jnp.concatenate([hi, mid], 0)) + dot(near, low)
        for side in range(6):
            for part in range(6):
                at = (side * 6 + part) * 16
                ghost[at:at + 16, :] = out[side * 16:side * 16 + 16, part * 128:part * 128 + 128]

    def fetch_near(turn):
        for peer in NEAR:
            copy_of(turn, peer, peer).wait()
        none = jnp.zeros((8, 384), jnp.float32)
        hi, mid, low = split3(jnp.concatenate([recvs[turn, c] if c in NEAR else none for c in range(8)], 0))
        arrived = jnp.concatenate([hi, mid, low, jnp.zeros_like(low)], 0)
        fold = jnp.where(lane_ids[:96] >= 64.0, lane_ids[:96] - 64.0, lane_ids[:96])
        for half in range(2):
            pick = as_one(far_col[...] + 4.0 * half == fold)
            out = dot(jnp.concatenate([pick, pick], 1), arrived)
            for side in range(6):
                for part in range(3):
                    at = (side * 6 + half * 3 + part) * 16
                    ghost[at:at + 16, :] += out[side * 16:side * 16 + 16, part * 128:part * 128 + 128]

    def own_cells():
        hi, mid, low = split3(faces[...])
        one = take[...].astype(jnp.bfloat16)
        return dot(jnp.concatenate([one, one], 1), jnp.concatenate([hi, mid], 0)) + dot(one, low)

    def put_far(values):
        parts = [part.astype(jnp.float32) for part in split3(values)]
        parts = jnp.concatenate(parts + [jnp.zeros_like(values)], 0).astype(jnp.bfloat16)
        lanes = lax.broadcasted_iota(jnp.int32, (96, 32), 1)
        rows = jnp.where(lanes < 24, (lanes & 7) + 56, -1).astype(jnp.float32)
        return dot(as_one(far_col[:, :32] == rows), parts)

    def is_far(side):
        return far_col[side * 16:side * 16 + 16, :] >= 56.0

    def far_weno(turn, own):
        copy_of(turn, FAR, FAR).wait()
        came = recvs[turn, FAR]
        other = pltpu.roll(came, 4, 0)
        result = {}
        for tile in range(2):
            values = {}
            for depth in range(3):
                part = depth * 2 + tile
                from_ = came if part < 3 else other
                values[-1 - depth] = from_[:, part % 3 * 128:part % 3 * 128 + 128]
            for depth in range(6):
                at = (depth * 2 + tile) * 128
                values[depth] = own[:, at:at + 128]

            def signs(i):
                return far_sigma[:, (i * 2 + tile) * 128:(i * 2 + tile) * 128 + 128]

            def store(i, value):
                result[i * 2 + tile] = value

            weno_axis(values, 0, 3, signs, store)
        return put_far(jnp.concatenate([result[part] for part in range(6)], 1))

    def column_rows(axis, position, column):
        return pl.ds(axis * AXIS_ROWS + position * 32 + column * 8, 8)

    def ghosts_at(axis, high, depth, column, edge):
        values = ghost[pl.ds((2 * axis + high) * 96 + depth * 32 + column * 8, 8), :]
        gone = missing[pl.ds((2 * axis + high) * 16 + (column % 2) * 8, 8), :]
        return jnp.where(gone > 0.0, edge, values)

    def weno_part(index, low, high):
        axis, column = index // 4, index % 4
        load = lambda i: u[column_rows(axis, i, column), :]
        signs = lambda i: sigma[column_rows(axis, i, column), :]

        def store(i, value):
            grad[column_rows(axis, i, column), :] = value

        if low == 3:
            values = {i: load(i) for i in range(16)}
            weno_axis(values, 3, 13, signs, store)
            return
        values = {i: load(i) for i in range(6)}
        for i in range(3):
            values[-1 - i] = ghosts_at(axis, 0, i, column, values[0])
        weno_axis(values, 0, 3, signs, store)
        values = {i: load(i) for i in range(10, 16)}
        for i in range(3):
            values[16 + i] = ghosts_at(axis, 1, i, column, values[15])
        weno_axis(values, 13, 16, signs, store)

    first = own_cells()[:, :768]
    far_sigma[...] = jnp.where(first > 0.0, 1.0, -1.0)

    def step(turn, carry):
        serve(turn)

        def inner(index, c):
            weno_part(index, 3, 13)
            return c

        def outer(index, c):
            weno_part(index, 0, 16)
            return c

        lax.fori_loop(0, 12, inner, 0)
        own = own_cells()
        fetch_near(turn)
        lax.fori_loop(0, 12, outer, 0)
        fixed = far_weno(turn, own)

        def grad_at(axis, position, tile):
            value = grad[rows_of(axis, position, tile), :]
            depth = min(position, 15 - position)
            if depth >= 3:
                return value
            side = 2 * axis + (position >= 8)
            at = (depth * 2 + tile) * 128
            return jnp.where(is_far(side), fixed[side * 16:side * 16 + 16, at:at + 128], value)

        for tile in range(2):
            sums = exchange([grad_at(2, z, tile) for z in range(16)], 1, fine_masks)
            sums = [sums[y] + grad_at(1, y, tile) for y in range(16)]
            fresh = {}
            for ytile in range(2):
                xs = exchange(sums[ytile * 8:ytile * 8 + 8], 16, coarse_masks)
                for i in range(8):
                    rows = rows_of(0, tile * 8 + i, ytile)
                    steep = jnp.sqrt(xs[i] + grad_at(0, tile * 8 + i, ytile))
                    value = u[rows, :] - speed[rows, :] * (steep - 3.0)
                    u[rows, :] = value
                    keep_face(0, tile * 8 + i, ytile, value)
                    fresh[i, ytile] = value
            spread(tile, lambda i, ytile: fresh[i, ytile])
        return carry

    lax.fori_loop(0, STEPS, step, 0)

    serve(STEPS)
    keep = lax.broadcasted_iota(jnp.int32, (16, 128), 0) < live[0]
    for x in range(16):
        for ytile in range(2):
            at = x * 256 + ytile * 128
            level_out[:, at:at + 128] = jnp.where(keep, u[rows_of(0, x, ytile), :], 0.0)
    fetch_near(STEPS)
    copy_of(STEPS, FAR, FAR).wait()
    far_rim = put_far(recvs[STEPS, FAR, :, :256])

    def rim(axis, high, tile, edge):
        side = 2 * axis + high
        values = ghost[side * 96 + tile * 16:side * 96 + tile * 16 + 16, :]
        values = jnp.where(is_far(side), far_rim[side * 16:side * 16 + 16, tile * 128:tile * 128 + 128], values)
        return jnp.where(missing[side * 16:side * 16 + 16, :] > 0.0, edge, values)

    def beside(axis, position, tile):
        here = u[rows_of(axis, position, tile), :]
        low = rim(axis, 0, tile, here) if position == 0 else u[rows_of(axis, position - 1, tile), :]
        high = rim(axis, 1, tile, here) if position == 15 else u[rows_of(axis, position + 1, tile), :]
        return (high + low) - (here + here), high - low, here

    for tile in range(2):
        lap_y, grad_x = [], []
        for ytile in range(2):
            parts = [beside(0, tile * 8 + i, ytile) for i in range(8)]
            lap_y += exchange([p[0] for p in parts], 16, coarse_masks)
            grad_x += exchange([p[1] for p in parts], 16, coarse_masks)
        parts = [beside(1, y, tile) for y in range(16)]
        laps = exchange([lap_y[y] + parts[y][0] for y in range(16)], 1, fine_masks)
        grad_x = exchange(grad_x, 1, fine_masks)
        grad_y = exchange([p[1] for p in parts], 1, fine_masks)
        held = None
        for z in range(16):
            lap, grad_z, here = beside(2, z, tile)
            lap = lap + laps[z]
            v2 = jnp.minimum(here * here, BAND_WIDTH * BAND_WIDTH) * ((math.pi / 3.0) ** 2)
            wave = 1.0 / 479001600.0
            for power in (-1.0 / 3628800.0, 1.0 / 40320.0, -1.0 / 720.0, 1.0 / 24.0, -0.5, 1.0):
                wave = wave * v2 + power
            lap = jnp.where(jnp.abs(here) < BAND_WIDTH, lap * (wave * wave * (2.0 / 3.0)), 0.0)
            forces = [lap * grad_x[z], lap * grad_y[z], lap * grad_z]
            if z % 2 == 0:
                held = forces
            else:
                for a in range(3):
                    force[a, pl.ds(z // 2 * 16, 16), tile * 128:tile * 128 + 128] = held[a] + forces[a]

    r = lax.broadcasted_iota(jnp.int32, (256, 256), 0)
    l = lax.broadcasted_iota(jnp.int32, (256, 256), 1)
    same = jnp.logical_and((r >> 5) == ((l >> 4) & 7), ((r >> 1) & 7) == (l & 7))
    average = jnp.where(same, 1.0 / 16.0, 0.0).astype(jnp.bfloat16)
    lanes = lax.broadcasted_iota(jnp.int32, (16, 256), 1)
    brick_rows = lax.broadcasted_iota(jnp.int32, (16, 256), 0)
    lane_bricks = lax.broadcasted_iota(jnp.int32, (64, 128), 1)
    by_row = jnp.zeros((16, 256), jnp.int32)
    by_lane = jnp.full((64, 128), -1, jnp.int32)
    for b in range(16):
        by_row = jnp.where(brick_rows == b, target[b], by_row)
        by_lane = jnp.where((lane_bricks & 15) == b, target[b], by_lane)
    octant = jnp.logical_and(((by_row >> 2) & 1) == (lanes >> 7), ((by_row >> 1) & 1) == ((lanes >> 3) & 1))
    octant = jnp.where(octant, 1.0, 0.0)
    out_rows = lax.broadcasted_iota(jnp.int32, (64, 128), 0)
    pick = jnp.logical_and((by_lane >> 3) == (out_rows & 3), (by_lane & 1) == (out_rows >> 5))
    pick = jnp.logical_and(pick, (lane_bricks >> 4) == ((out_rows >> 2) & 7))
    pick = jnp.where(pick, 1.0, 0.0).astype(jnp.bfloat16)
    share = 64 // n_gz
    turns = sorted(range(1, n_gz), key=lambda turn: abs(2 * turn - n_gz))

    def part_copy(a, turn):
        to = lax.rem(layer + turn, n_gz)
        return pltpu.make_async_remote_copy(
            src_ref=fsend.at[to, a], dst_ref=frecv.at[turn - 1, a],
            send_sem=fsent.at[turn - 1, a], recv_sem=fgot.at[turn - 1, a],
            device_id={"gz": to}, device_id_type=MESH)

    for a in range(3):
        hi, mid, low = split3(force[a])
        block = dot(hi, average) + (dot(mid, average) + dot(low, average))
        block = (block.reshape(8, 16, 256) * octant[None]).reshape(128, 256)
        hi, mid, low = split3(block)
        result = dot(pick, hi) + (dot(pick, mid) + dot(pick, low))
        for g in range(n_gz):
            fsend[g, a] = result[g * share:(g + 1) * share]
        for turn in turns:
            part_copy(a, turn).start()
    for a in range(3):
        total = fsend[layer, a]
        for turn in turns:
            part_copy(a, turn).wait()
            total = total + frecv[turn - 1, a]
        part_out[a] = total


def shards(n_gx, n_gz, level_set, neighbours, live_count, dense_target):
    share = 64 // n_gz
    vmem = pl.BlockSpec(memory_space=pltpu.VMEM)
    anywhere = pl.BlockSpec(memory_space=pl.ANY)
    dma, f32 = pltpu.SemaphoreType.DMA, jnp.float32
    def far_memory(array):
        return pltpu.with_memory_space_constraint(array, pltpu.HBM)

    level, part = pl.pallas_call(
        functools.partial(kernel, n_gx, n_gz),
        out_shape=(jax.ShapeDtypeStruct(level_set.shape, f32), jax.ShapeDtypeStruct((3, share, 256), f32)),
        in_specs=[anywhere, pl.BlockSpec(memory_space=pltpu.SMEM), anywhere, anywhere],
        out_specs=(vmem, vmem),
        scratch_shapes=[
            pltpu.VMEM((6, SLOTS), jnp.int32),
            pltpu.SMEM((SLOTS,), jnp.int32),
            pltpu.VMEM(level_set.shape, f32),
            pltpu.VMEM((3 * AXIS_ROWS, 128), f32),
            pltpu.VMEM((128, 1536), f32),
            pltpu.VMEM((36 * 16, 128), f32),
            pltpu.VMEM((3 * AXIS_ROWS, 128), f32),
            pltpu.VMEM((3 * AXIS_ROWS, 128), f32),
            pltpu.VMEM((AXIS_ROWS, 128), f32),
            pltpu.VMEM((96, 128), f32),
            pltpu.VMEM((96, 128), f32),
            pltpu.VMEM((96, 128), f32),
            pltpu.VMEM((8, 128), f32),
            pltpu.VMEM((8, 768), f32),
            pltpu.VMEM((3, 128, 256), f32),
            pltpu.VMEM((8, 8, 128), f32),
            pltpu.VMEM((8, 8, 128), f32),
            pltpu.VMEM((ROUNDS, 8, 8, 384), f32),
            pltpu.VMEM((ROUNDS, 8, 8, 384), f32),
            pltpu.VMEM((n_gz, 3, share, 256), f32),
            pltpu.VMEM((n_gz - 1, 3, share, 256), f32),
            dma(()), dma(()), dma(()), dma((8,)), dma((8,)), dma((ROUNDS, 8)), dma((ROUNDS, 8)), dma((n_gz - 1, 3)), dma((n_gz - 1, 3)),
        ],
        compiler_params=pltpu.CompilerParams(
            collective_id=0, has_side_effects=True, vmem_limit_bytes=24 << 20),
    )(far_memory(neighbours.T), live_count, far_memory(dense_target), far_memory(level_set))
    part = part.reshape(3, SIDE // n_gz, DENSE, 256)
    return level, jnp.transpose(part, (2, 0, 1, 3))


def solution(mesh):
    placed = (P(("gx", "gz"), None), P(("gx", "gz"), None), P(("gx", "gz")), P(("gx", "gz")))
    return jax.shard_map(
        functools.partial(shards, mesh.shape["gx"], mesh.shape["gz"]),
        mesh=mesh,
        in_specs=placed,
        out_specs=(P(("gx", "gz"), None), P("gx", None, "gz", None)),
        check_vma=False,
    )
```

```python
import functools
import math

import jax
import jax.numpy as jnp
from jax import lax
from jax.experimental import pallas as pl
from jax.experimental.pallas import tpu as pltpu
from jax.sharding import PartitionSpec as P

SIDE = 16
SLOTS = 16
DENSE = 4
STEPS = 3
ROUNDS = STEPS + 1
BAND_WIDTH = 1.5
MESH = pl.DeviceIdType.MESH

PEERS = (7, 0, 6, 1, 5, 2, 4)
NEAR = (0, 6, 1, 5, 2, 4)
FAR = 7
AXIS_ROWS = 512


def facing(peer):
    return 7 if peer == 7 else 6 - peer


def exchange(values, width, masks):
    count = len(values)
    bits = count.bit_length() - 1
    rolled = [v if j == 0 else pltpu.roll(v, j * width, 1) for j, v in enumerate(values)]
    moved = [rolled[-i % count] for i in range(count)]
    for bit in range(bits):
        moved = [jnp.where(masks[bit], moved[(i - (1 << bit)) % count], moved[i]) for i in range(count)]
    return [v if i == 0 else pltpu.roll(v, 128 - i * width, 1) for i, v in enumerate(moved)]


def lane_masks(rows, width, bits):
    lanes = lax.broadcasted_iota(jnp.int32, (rows, 128), 1)
    return [(lanes & (width << bit)) != 0 for bit in range(bits)]


def weno_axis(u, first, last, sigma, store):
    d = {j: u[j] - u[j - 1] for j in range(first - 2, last + 3)}
    e = {j: d[j + 1] - d[j] for j in range(first - 2, last + 2)}
    s = {j: e[j] - e[j - 1] for j in range(first - 1, last + 2)}
    t = {j: s[j + 1] - s[j] for j in range(first - 1, last + 1)}
    r1, r2, r3 = {}, {}, {}
    for j in range(first - 1, last + 2):
        base = (13.0 / 3.0) * (s[j] * s[j]) + 4e-6
        if j <= last - 1:
            lean = (e[j] + e[j]) + s[j]
            r = pltpu.reciprocal(base + lean * lean, approx=True)
            r1[j] = r * r
        if first <= j <= last:
            lean = e[j] + e[j - 1]
            r = pltpu.reciprocal(base + lean * lean, approx=True)
            r2[j] = 6.0 * (r * r)
        if j >= first + 1:
            lean = s[j] - (e[j - 1] + e[j - 1])
            r = pltpu.reciprocal(base + lean * lean, approx=True)
            r3[j] = r * r
    for i in range(first, last):
        half = 0.5 * t[i]
        left = 3.0 * d[i] + (e[i] + 0.5 * e[i - 1])
        right = left - half
        w3 = 3.0 * r3[i + 1]
        den = (r1[i - 1] + r2[i]) + w3
        num = r1[i - 1] * t[i - 1] + w3 * half
        left = left - num * pltpu.reciprocal(den, approx=True)
        w3 = 3.0 * r1[i]
        den = (r3[i + 2] + r2[i + 1]) + w3
        num = r3[i + 2] * t[i + 1] + w3 * half
        right = right + num * pltpu.reciprocal(den, approx=True)
        m = jnp.maximum(jnp.maximum(sigma(i) * left, -sigma(i) * right), 0.0)
        store(i, m * m)


def split3(x):
    hi = x.astype(jnp.bfloat16)
    rest = x - hi.astype(jnp.float32)
    mid = rest.astype(jnp.bfloat16)
    low = (rest - mid.astype(jnp.float32)).astype(jnp.bfloat16)
    return hi, mid, low


def as_one(mask):
    return jnp.where(mask, 1.0, 0.0).astype(jnp.bfloat16)


def dot_rows(a, b):
    return lax.dot_general(a, b, (((0,), (0,)), ((), ())), preferred_element_type=jnp.float32)


def dot(a, b):
    return lax.dot_general(a, b, (((1,), (0,)), ((), ())), preferred_element_type=jnp.float32)


def kernel(n_gx, n_gz, table, live, target_in, level, level_out, part_out,
           nb, target, start, u, faces, ghost, sigma, grad, speed, missing, near_col, far_col, take, far_sigma, force, request, heard,
           sends, recvs, fsend, frecv,
           table_loaded, target_loaded, loaded, request_sent, request_got, sent, got, fsent, fgot):
    me = lax.axis_index("gx")
    layer = lax.axis_index("gz")

    def peer_id(peer):
        step = n_gx // 2 if peer == 7 else peer - 3
        return {"gx": lax.rem(me + step + n_gx, n_gx)}

    load = pltpu.make_async_copy(level, start, loaded)
    load.start()
    load_table = pltpu.make_async_copy(table, nb, table_loaded)
    load_table.start()
    load_target = pltpu.make_async_copy(target_in, target, target_loaded)
    load_target.start()
    barrier = pltpu.get_barrier_semaphore()
    for peer in PEERS:
        pl.semaphore_signal(barrier, inc=1, device_id=peer_id(peer), device_id_type=MESH)
    for turn in range(1, n_gz):
        pl.semaphore_signal(barrier, inc=1, device_id={"gz": lax.rem(layer + turn, n_gz)}, device_id_type=MESH)

    square_rows = lax.broadcasted_iota(jnp.int32, (128, 128), 0)
    square_lanes = lax.broadcasted_iota(jnp.int32, (128, 128), 1)
    load_table.wait()
    spots = [jnp.broadcast_to(nb[side:side + 1, :], (16, 16)) for side in range(6)]
    spots = jnp.concatenate(spots + [jnp.full((32, 16), -1, jnp.int32)], 0)
    own_spot = lax.broadcasted_iota(jnp.int32, (128, 16), 0) & 15
    own_spot = own_spot == lax.broadcasted_iota(jnp.int32, (128, 16), 1)
    entry = jnp.sum(jnp.where(own_spot, spots, 0).astype(jnp.float32), 1, keepdims=True)
    entry = jnp.broadcast_to(entry, (128, 128)).astype(jnp.int32)
    held = entry >= 0
    away = (entry >> (SLOTS * n_gz).bit_length() - 1) - me + 3
    kind = jnp.minimum(away & (n_gx - 1), 7)
    remote = jnp.logical_and(held, kind != 3)
    face = ((square_rows >> 4) ^ 1) * 16 + (entry & 15)
    mine = as_one(jnp.logical_and(remote, kind == square_lanes))
    before = dot(as_one(square_lanes < square_rows), mine)
    rank = dot((before * mine.astype(jnp.float32)).astype(jnp.bfloat16), jnp.ones((128, 128), jnp.bfloat16))
    slot = kind.astype(jnp.float32) * 8.0 + rank
    slot = jnp.where(remote, slot, -16.0)
    lane_ids = square_lanes.astype(jnp.float32)
    face = face.astype(jnp.float32)
    chosen = as_one(slot == lane_ids)
    asked = dot_rows(chosen, face.astype(jnp.bfloat16))
    asked = asked + dot_rows(as_one(slot + 4.0 == lane_ids), (face + 128.0).astype(jnp.bfloat16))
    request[...] = asked[:64].reshape(8, 8, 128)
    far_col[...] = slot[:96]
    take[...] = dot_rows(chosen, as_one(square_rows == square_lanes))[56:64]
    near_col[...] = jnp.where(jnp.logical_and(held, kind == 3), face, -16.0)[:96]
    missing[...] = jnp.where(held, 0.0, 1.0)[:96]
    faces[96:, :] = jnp.zeros((32, 1536), jnp.float32)

    pl.semaphore_wait(barrier, len(PEERS) + n_gz - 1)
    for peer in PEERS:
        pltpu.make_async_remote_copy(
            src_ref=request.at[peer], dst_ref=heard.at[facing(peer)],
            send_sem=request_sent.at[peer], recv_sem=request_got.at[facing(peer)],
            device_id=peer_id(peer), device_id_type=MESH).start()

    coarse_masks = lane_masks(16, 16, 3)
    fine_masks = lane_masks(16, 1, 4)

    def rows_of(axis, position, tile):
        return pl.ds(axis * AXIS_ROWS + position * 32 + tile * 16, 16)

    def keep_face(axis, position, tile, value):
        depth = min(position, 15 - position)
        if depth < 6:
            side = 2 * axis + (position >= 8)
            at = (depth * 2 + tile) * 128
            faces[side * 16:side * 16 + 16, at:at + 128] = value

    def spread(tile, x_of):
        ys = []
        for ytile in range(2):
            ys += exchange([x_of(i, ytile) for i in range(8)], 16, coarse_masks)
        for y in range(16):
            u[rows_of(1, y, tile), :] = ys[y]
            keep_face(1, y, tile, ys[y])
        zs = exchange(ys, 1, fine_masks)
        for z in range(16):
            u[rows_of(2, z, tile), :] = zs[z]
            keep_face(2, z, tile, zs[z])
        return ys, zs

    load_target.wait()
    load.wait()
    for tile in range(2):
        tops = {}
        for i in range(8):
            for ytile in range(2):
                x = tile * 8 + i
                value = start[:, x * 256 + ytile * 128:x * 256 + ytile * 128 + 128]
                u[rows_of(0, x, ytile), :] = value
                keep_face(0, x, ytile, value)
                sigma[rows_of(0, x, ytile), :] = jnp.where(value > 0.0, 1.0, -1.0)
                speed[rows_of(0, x, ytile), :] = 0.1 * value * lax.rsqrt(value * value + 1.0)
                tops[i, ytile] = value
        ys, zs = spread(tile, lambda i, ytile: tops[i, ytile])
        for p in range(16):
            sigma[rows_of(1, p, tile), :] = jnp.where(ys[p] > 0.0, 1.0, -1.0)
            sigma[rows_of(2, p, tile), :] = jnp.where(zs[p] > 0.0, 1.0, -1.0)

    for peer in PEERS:
        pltpu.make_async_remote_copy(
            src_ref=request.at[peer], dst_ref=heard.at[peer],
            send_sem=request_sent.at[peer], recv_sem=request_got.at[peer],
            device_id=peer_id(peer), device_id_type=MESH).wait()

    def copy_of(turn, peer, into):
        return pltpu.make_async_remote_copy(
            src_ref=sends.at[turn, peer], dst_ref=recvs.at[turn, into],
            send_sem=sent.at[turn, peer], recv_sem=got.at[turn, into],
            device_id=peer_id(peer), device_id_type=MESH)

    def serve(turn):
        hi, mid, low = split3(faces[:, :768])
        cols = heard[...].reshape(64, 128)
        left = as_one(cols == lane_ids[:64])
        right = as_one(cols == lane_ids[:64] + 128.0)
        both = jnp.concatenate([left, left], 1)
        out = dot(both, jnp.concatenate([hi[:, :384], mid[:, :384]], 0))
        both = jnp.concatenate([right, right], 1)
        out = out + dot(both, jnp.concatenate([hi[:, 384:], mid[:, 384:]], 0))
        both = jnp.concatenate([left, right], 1)
        out = out + dot(both, jnp.concatenate([low[:, :384], low[:, 384:]], 0))
        sends[turn] = out.reshape(8, 8, 384)
        for peer in PEERS:
            copy_of(turn, peer, facing(peer)).start()
        near = as_one(near_col[...] == lane_ids[:96])
        out = dot(jnp.concatenate([near, near], 1), jnp.concatenate([hi, mid], 0)) + dot(near, low)
        for side in range(6):
            for part in range(6):
                at = (side * 6 + part) * 16
                ghost[at:at + 16, :] = out[side * 16:side * 16 + 16, part * 128:part * 128 + 128]

    def fetch_near(turn):
        for peer in NEAR:
            copy_of(turn, peer, peer).wait()
        none = jnp.zeros((8, 384), jnp.float32)
        hi, mid, low = split3(jnp.concatenate([recvs[turn, c] if c in NEAR else none for c in range(8)], 0))
        arrived = jnp.concatenate([hi, mid, low, jnp.zeros_like(low)], 0)
        fold = jnp.where(lane_ids[:96] >= 64.0, lane_ids[:96] - 64.0, lane_ids[:96])
        for half in range(2):
            pick = as_one(far_col[...] + 4.0 * half == fold)
            out = dot(jnp.concatenate([pick, pick], 1), arrived)
            for side in range(6):
                for part in range(3):
                    at = (side * 6 + half * 3 + part) * 16
                    ghost[at:at + 16, :] += out[side * 16:side * 16 + 16, part * 128:part * 128 + 128]

    def own_cells():
        hi, mid, low = split3(faces[...])
        one = take[...].astype(jnp.bfloat16)
        return dot(jnp.concatenate([one, one], 1), jnp.concatenate([hi, mid], 0)) + dot(one, low)

    def put_far(values):
        parts = [part.astype(jnp.float32) for part in split3(values)]
        parts = jnp.concatenate(parts + [jnp.zeros_like(values)], 0).astype(jnp.bfloat16)
        lanes = lax.broadcasted_iota(jnp.int32, (96, 32), 1)
        rows = jnp.where(lanes < 24, (lanes & 7) + 56, -1).astype(jnp.float32)
        return dot(as_one(far_col[:, :32] == rows), parts)

    def is_far(side):
        return far_col[side * 16:side * 16 + 16, :] >= 56.0

    def far_weno(turn, own):
        copy_of(turn, FAR, FAR).wait()
        came = recvs[turn, FAR]
        other = pltpu.roll(came, 4, 0)
        result = {}
        for tile in range(2):
            values = {}
            for depth in range(3):
                part = depth * 2 + tile
                from_ = came if part < 3 else other
                values[-1 - depth] = from_[:, part % 3 * 128:part % 3 * 128 + 128]
            for depth in range(6):
                at = (depth * 2 + tile) * 128
                values[depth] = own[:, at:at + 128]

            def signs(i):
                return far_sigma[:, (i * 2 + tile) * 128:(i * 2 + tile) * 128 + 128]

            def store(i, value):
                result[i * 2 + tile] = value

            weno_axis(values, 0, 3, signs, store)
        return put_far(jnp.concatenate([result[part] for part in range(6)], 1))

    def column_rows(axis, position, column):
        return pl.ds(axis * AXIS_ROWS + position * 32 + column * 8, 8)

    def ghosts_at(axis, high, depth, column, edge):
        values = ghost[pl.ds((2 * axis + high) * 96 + depth * 32 + column * 8, 8), :]
        gone = missing[pl.ds((2 * axis + high) * 16 + (column % 2) * 8, 8), :]
        return jnp.where(gone > 0.0, edge, values)

    def weno_part(index, low, high):
        axis, column = index // 4, index % 4
        load = lambda i: u[column_rows(axis, i, column), :]
        signs = lambda i: sigma[column_rows(axis, i, column), :]

        def store(i, value):
            grad[column_rows(axis, i, column), :] = value

        if low == 3:
            values = {i: load(i) for i in range(16)}
            weno_axis(values, 3, 13, signs, store)
            return
        values = {i: load(i) for i in range(6)}
        for i in range(3):
            values[-1 - i] = ghosts_at(axis, 0, i, column, values[0])
        weno_axis(values, 0, 3, signs, store)
        values = {i: load(i) for i in range(10, 16)}
        for i in range(3):
            values[16 + i] = ghosts_at(axis, 1, i, column, values[15])
        weno_axis(values, 13, 16, signs, store)

    first = own_cells()[:, :768]
    far_sigma[...] = jnp.where(first > 0.0, 1.0, -1.0)

    def step(turn, carry):
        serve(turn)

        def inner(index, c):
            weno_part(index, 3, 13)
            return c

        def outer(index, c):
            weno_part(index, 0, 16)
            return c

        lax.fori_loop(0, 12, inner, 0)
        own = own_cells()
        fetch_near(turn)
        lax.fori_loop(0, 12, outer, 0)
        fixed = far_weno(turn, own)

        def grad_at(axis, position, tile):
            value = grad[rows_of(axis, position, tile), :]
            depth = min(position, 15 - position)
            if depth >= 3:
                return value
            side = 2 * axis + (position >= 8)
            at = (depth * 2 + tile) * 128
            return jnp.where(is_far(side), fixed[side * 16:side * 16 + 16, at:at + 128], value)

        for tile in range(2):
            sums = exchange([grad_at(2, z, tile) for z in range(16)], 1, fine_masks)
            sums = [sums[y] + grad_at(1, y, tile) for y in range(16)]
            fresh = {}
            for ytile in range(2):
                xs = exchange(sums[ytile * 8:ytile * 8 + 8], 16, coarse_masks)
                for i in range(8):
                    rows = rows_of(0, tile * 8 + i, ytile)
                    steep = jnp.sqrt(xs[i] + grad_at(0, tile * 8 + i, ytile))
                    value = u[rows, :] - speed[rows, :] * (steep - 3.0)
                    u[rows, :] = value
                    keep_face(0, tile * 8 + i, ytile, value)
                    fresh[i, ytile] = value
            spread(tile, lambda i, ytile: fresh[i, ytile])
        return carry

    lax.fori_loop(0, STEPS, step, 0)

    serve(STEPS)
    keep = lax.broadcasted_iota(jnp.int32, (16, 128), 0) < live[0]
    for x in range(16):
        for ytile in range(2):
            at = x * 256 + ytile * 128
            level_out[:, at:at + 128] = jnp.where(keep, u[rows_of(0, x, ytile), :], 0.0)

    r = lax.broadcasted_iota(jnp.int32, (256, 256), 0)
    l = lax.broadcasted_iota(jnp.int32, (256, 256), 1)
    same = jnp.logical_and((r >> 5) == ((l >> 4) & 7), ((r >> 1) & 7) == (l & 7))
    average = jnp.where(same, 1.0 / 16.0, 0.0).astype(jnp.bfloat16)
    average = jnp.concatenate([average, average], 0)
    swap = as_one(l == (r & 15) * 16 + (r >> 4))
    swap = jnp.concatenate([swap, swap, swap], 0)
    lanes = lax.broadcasted_iota(jnp.int32, (16, 256), 1)
    brick_rows = lax.broadcasted_iota(jnp.int32, (16, 256), 0)
    lane_bricks = lax.broadcasted_iota(jnp.int32, (64, 128), 1)
    by_row = jnp.zeros((16, 256), jnp.int32)
    by_lane = jnp.full((64, 128), -1, jnp.int32)
    for b in range(16):
        by_row = jnp.where(brick_rows == b, target[b], by_row)
        by_lane = jnp.where((lane_bricks & 15) == b, target[b], by_lane)
    octant = jnp.logical_and(((by_row >> 2) & 1) == (lanes >> 7), ((by_row >> 1) & 1) == ((lanes >> 3) & 1))
    octant = jnp.where(octant, 1.0, 0.0)
    share, deep = 64 // n_gz, SIDE // n_gz
    out_rows = lax.broadcasted_iota(jnp.int32, (64, 128), 0)
    out_z = (out_rows // share) * deep + (out_rows & (deep - 1))
    pick = jnp.logical_and((by_lane >> 3) == (out_rows & (share - 1)) // deep, (by_lane & 1) == (out_z >> 3))
    pick = as_one(jnp.logical_and(pick, (lane_bricks >> 4) == (out_z & 7)))
    turns = sorted(range(1, n_gz), key=lambda turn: abs(2 * turn - n_gz))

    fetch_near(STEPS)

    def rim(axis, high, tile, edge):
        side = 2 * axis + high
        values = ghost[side * 96 + tile * 16:side * 96 + tile * 16 + 16, :]
        return jnp.where(missing[side * 16:side * 16 + 16, :] > 0.0, edge, values)

    def beside(axis, position, tile):
        here = u[rows_of(axis, position, tile), :]
        low = rim(axis, 0, tile, here) if position == 0 else u[rows_of(axis, position - 1, tile), :]
        high = rim(axis, 1, tile, here) if position == 15 else u[rows_of(axis, position + 1, tile), :]
        return (high + low) - (here + here), high - low, here

    for tile in range(2):
        lap_y, grad_x = [], []
        for ytile in range(2):
            parts = [beside(0, tile * 8 + i, ytile) for i in range(8)]
            lap_y += exchange([p[0] for p in parts], 16, coarse_masks)
            grad_x += exchange([p[1] for p in parts], 16, coarse_masks)
        parts = [beside(1, y, tile) for y in range(16)]
        laps = exchange([lap_y[y] + parts[y][0] for y in range(16)], 1, fine_masks)
        grad_x = exchange(grad_x, 1, fine_masks)
        grad_y = exchange([p[1] for p in parts], 1, fine_masks)
        for z in range(16):
            lap, grad_z, here = beside(2, z, tile)
            v2 = jnp.minimum(here * here, BAND_WIDTH * BAND_WIDTH) * ((math.pi / 3.0) ** 2)
            wave = 1.0 / 479001600.0
            for power in (-1.0 / 3628800.0, 1.0 / 40320.0, -1.0 / 720.0, 1.0 / 24.0, -0.5, 1.0):
                wave = wave * v2 + power
            grad[rows_of(0, z, tile), :] = lap + laps[z]
            grad[rows_of(1, z, tile), :] = grad_x[z]
            grad[rows_of(2, z, tile), :] = grad_y[z]
            sigma[rows_of(0, z, tile), :] = grad_z
            sigma[rows_of(1, z, tile), :] = jnp.where(jnp.abs(here) < BAND_WIDTH, wave * wave * (2.0 / 3.0), 0.0)

    copy_of(STEPS, FAR, FAR).wait()
    far_rim = put_far(recvs[STEPS, FAR, :, :256])
    turned = dot(jnp.concatenate(split3(far_rim[:32]), 1), swap)
    groups = lax.broadcasted_iota(jnp.int32, (16, 128), 1)
    y_ids, x_ids = groups & 15, groups >> 4

    def moved_to(mask, values, by):
        return jnp.where(mask, pltpu.roll(values, by % 128, 1) if by % 128 else values, 0.0)

    for tile in range(2):
        edge = 7 * tile
        held = None
        for z in range(16):
            at = z // 8 * 128
            add_x = moved_to(x_ids == edge, turned[tile * 16:tile * 16 + 16, at:at + 128], 16 * (edge - z % 8))
            at = tile * 128
            low_y = moved_to(y_ids == 0, far_rim[32:48, at:at + 128], -z)
            high_y = moved_to(y_ids == 15, far_rim[48:64, at:at + 128], 15 - z)
            lap = (grad[rows_of(0, z, tile), :] + add_x) + (low_y + high_y)
            grad_x = grad[rows_of(1, z, tile), :] + (add_x if tile else -add_x)
            grad_y = grad[rows_of(2, z, tile), :] + (high_y - low_y)
            grad_z = sigma[rows_of(0, z, tile), :]
            if z == 0:
                lap = lap + far_rim[64:80, at:at + 128]
                grad_z = grad_z - far_rim[64:80, at:at + 128]
            if z == 15:
                lap = lap + far_rim[80:96, at:at + 128]
                grad_z = grad_z + far_rim[80:96, at:at + 128]
            lap = lap * sigma[rows_of(1, z, tile), :]
            forces = [lap * grad_x, lap * grad_y, lap * grad_z]
            if z % 2 == 0:
                held = forces
            else:
                for a in range(3):
                    force[a, pl.ds(z // 2 * 16, 16), at:at + 128] = held[a] + forces[a]

    def part_copy(a, turn):
        to = lax.rem(layer + turn, n_gz)
        return pltpu.make_async_remote_copy(
            src_ref=fsend.at[to, a], dst_ref=frecv.at[turn - 1, a],
            send_sem=fsent.at[turn - 1, a], recv_sem=fgot.at[turn - 1, a],
            device_id={"gz": to}, device_id_type=MESH)

    for a in range(3):
        block = dot(jnp.concatenate(split3(force[a])[:2], 1), average)
        block = (block.reshape(8, 16, 256) * octant[None]).reshape(128, 256)
        hi, mid, _ = split3(block)
        result = dot(pick, hi) + dot(pick, mid)
        for g in range(n_gz):
            fsend[g, a] = result[g * share:(g + 1) * share]
        for turn in turns:
            part_copy(a, turn).start()
    for a in range(3):
        total = fsend[layer, a]
        for turn in turns:
            part_copy(a, turn).wait()
            total = total + frecv[turn - 1, a]
        for s in range(DENSE):
            part_out[s, a] = total[s * deep:(s + 1) * deep]


def finish(level, force, level_out, force_out, level_sem, force_sem):
    level_copy = pltpu.make_async_copy(level, level_out, level_sem)
    force_copy = pltpu.make_async_copy(force, force_out, force_sem)
    level_copy.start()
    force_copy.start()
    force_copy.wait()
    level_copy.wait()


def shards(n_gx, n_gz, level_set, neighbours, live_count, dense_target):
    share = 64 // n_gz
    vmem = pl.BlockSpec(memory_space=pltpu.VMEM)
    anywhere = pl.BlockSpec(memory_space=pl.ANY)
    dma, f32 = pltpu.SemaphoreType.DMA, jnp.float32
    def far_memory(array):
        return pltpu.with_memory_space_constraint(array, pltpu.HBM)

    level, part = pl.pallas_call(
        functools.partial(kernel, n_gx, n_gz),
        out_shape=(jax.ShapeDtypeStruct(level_set.shape, f32), jax.ShapeDtypeStruct((DENSE, 3, SIDE // n_gz, 256), f32)),
        in_specs=[anywhere, pl.BlockSpec(memory_space=pltpu.SMEM), anywhere, anywhere],
        out_specs=(vmem, vmem),
        scratch_shapes=[
            pltpu.VMEM((6, SLOTS), jnp.int32),
            pltpu.SMEM((SLOTS,), jnp.int32),
            pltpu.VMEM(level_set.shape, f32),
            pltpu.VMEM((3 * AXIS_ROWS, 128), f32),
            pltpu.VMEM((128, 1536), f32),
            pltpu.VMEM((36 * 16, 128), f32),
            pltpu.VMEM((3 * AXIS_ROWS, 128), f32),
            pltpu.VMEM((3 * AXIS_ROWS, 128), f32),
            pltpu.VMEM((AXIS_ROWS, 128), f32),
            pltpu.VMEM((96, 128), f32),
            pltpu.VMEM((96, 128), f32),
            pltpu.VMEM((96, 128), f32),
            pltpu.VMEM((8, 128), f32),
            pltpu.VMEM((8, 768), f32),
            pltpu.VMEM((3, 128, 256), f32),
            pltpu.VMEM((8, 8, 128), f32),
            pltpu.VMEM((8, 8, 128), f32),
            pltpu.VMEM((ROUNDS, 8, 8, 384), f32),
            pltpu.VMEM((ROUNDS, 8, 8, 384), f32),
            pltpu.VMEM((n_gz, 3, share, 256), f32),
            pltpu.VMEM((n_gz - 1, 3, share, 256), f32),
            dma(()), dma(()), dma(()), dma((8,)), dma((8,)), dma((ROUNDS, 8)), dma((ROUNDS, 8)), dma((n_gz - 1, 3)), dma((n_gz - 1, 3)),
        ],
        compiler_params=pltpu.CompilerParams(
            collective_id=0, has_side_effects=True, vmem_limit_bytes=24 << 20),
    )(far_memory(neighbours.T), live_count, far_memory(dense_target), far_memory(level_set))
    results = (level, part)
    return pl.pallas_call(
        finish,
        out_shape=tuple(jax.ShapeDtypeStruct(r.shape, f32) for r in results),
        in_specs=[anywhere] * 2,
        out_specs=(anywhere,) * 2,
        scratch_shapes=[dma(()), dma(())],
    )(*results)


def solution(mesh):
    placed = (P(("gx", "gz"), None), P(("gx", "gz"), None), P(("gx", "gz")), P(("gx", "gz")))
    return jax.shard_map(
        functools.partial(shards, mesh.shape["gx"], mesh.shape["gz"]),
        mesh=mesh,
        in_specs=placed,
        out_specs=(P(("gx", "gz"), None), P("gx", None, "gz", None)),
        check_vma=False,
    )
```

```python
import functools
import math

import jax
import jax.numpy as jnp
from jax import lax
from jax.experimental import pallas as pl
from jax.experimental.pallas import tpu as pltpu
from jax.sharding import PartitionSpec as P

SIDE = 16
SLOTS = 16
DENSE = 4
STEPS = 3
ROUNDS = STEPS + 1
BAND_WIDTH = 1.5
MESH = pl.DeviceIdType.MESH

PEERS = (7, 0, 6, 1, 5, 2, 4)
NEAR = (0, 6, 1, 5, 2, 4)
FAR = 7
AXIS_ROWS = 512


def facing(peer):
    return 7 if peer == 7 else 6 - peer


def exchange(values, width, masks):
    count = len(values)
    bits = count.bit_length() - 1
    rolled = [v if j == 0 else pltpu.roll(v, j * width, 1) for j, v in enumerate(values)]
    moved = [rolled[-i % count] for i in range(count)]
    for bit in range(bits):
        moved = [jnp.where(masks[bit], moved[(i - (1 << bit)) % count], moved[i]) for i in range(count)]
    return [v if i == 0 else pltpu.roll(v, 128 - i * width, 1) for i, v in enumerate(moved)]


def lane_masks(rows, width, bits):
    lanes = lax.broadcasted_iota(jnp.int32, (rows, 128), 1)
    return [(lanes & (width << bit)) != 0 for bit in range(bits)]


def weno_axis(u, first, last, sigma, store):
    d = {j: u[j] - u[j - 1] for j in range(first - 2, last + 3)}
    e = {j: d[j + 1] - d[j] for j in range(first - 2, last + 2)}
    s = {j: e[j] - e[j - 1] for j in range(first - 1, last + 2)}
    t = {j: s[j + 1] - s[j] for j in range(first - 1, last + 1)}
    r1, r2, r3 = {}, {}, {}
    for j in range(first - 1, last + 2):
        base = (13.0 / 3.0) * (s[j] * s[j]) + 4e-6
        if j <= last - 1:
            lean = (e[j] + e[j]) + s[j]
            r = pltpu.reciprocal(base + lean * lean, approx=True)
            r1[j] = r * r
        if first <= j <= last:
            lean = e[j] + e[j - 1]
            r = pltpu.reciprocal(base + lean * lean, approx=True)
            r2[j] = 6.0 * (r * r)
        if j >= first + 1:
            lean = s[j] - (e[j - 1] + e[j - 1])
            r = pltpu.reciprocal(base + lean * lean, approx=True)
            r3[j] = r * r
    for i in range(first, last):
        half = 0.5 * t[i]
        left = 3.0 * d[i] + (e[i] + 0.5 * e[i - 1])
        right = left - half
        w3 = 3.0 * r3[i + 1]
        den = (r1[i - 1] + r2[i]) + w3
        num = r1[i - 1] * t[i - 1] + w3 * half
        left = left - num * pltpu.reciprocal(den, approx=True)
        w3 = 3.0 * r1[i]
        den = (r3[i + 2] + r2[i + 1]) + w3
        num = r3[i + 2] * t[i + 1] + w3 * half
        right = right + num * pltpu.reciprocal(den, approx=True)
        m = jnp.maximum(jnp.maximum(sigma(i) * left, -sigma(i) * right), 0.0)
        store(i, m * m)


def split3(x):
    hi = x.astype(jnp.bfloat16)
    rest = x - hi.astype(jnp.float32)
    mid = rest.astype(jnp.bfloat16)
    low = (rest - mid.astype(jnp.float32)).astype(jnp.bfloat16)
    return hi, mid, low


def as_one(mask):
    return jnp.where(mask, 1.0, 0.0).astype(jnp.bfloat16)


def dot_rows(a, b):
    return lax.dot_general(a, b, (((0,), (0,)), ((), ())), preferred_element_type=jnp.float32)


def dot(a, b):
    return lax.dot_general(a, b, (((1,), (0,)), ((), ())), preferred_element_type=jnp.float32)


def kernel(n_gx, n_gz, table, live, target_in, level, level_out, part_out,
           nb, target, start, u, faces, ghost, sigma, grad, speed, missing, near_col, far_col, take, far_sigma, force, request, heard,
           sends, recvs, fsend, frecv,
           table_loaded, target_loaded, loaded, request_sent, request_got, sent, got, fsent, fgot):
    me = lax.axis_index("gx")
    layer = lax.axis_index("gz")

    def peer_id(peer):
        step = n_gx // 2 if peer == 7 else peer - 3
        return {"gx": lax.rem(me + step + n_gx, n_gx)}

    load = pltpu.make_async_copy(level, start, loaded)
    load.start()
    load_table = pltpu.make_async_copy(table, nb, table_loaded)
    load_table.start()
    load_target = pltpu.make_async_copy(target_in, target, target_loaded)
    load_target.start()
    barrier = pltpu.get_barrier_semaphore()
    for peer in PEERS:
        pl.semaphore_signal(barrier, inc=1, device_id=peer_id(peer), device_id_type=MESH)
    for turn in range(1, n_gz):
        pl.semaphore_signal(barrier, inc=1, device_id={"gz": lax.rem(layer + turn, n_gz)}, device_id_type=MESH)

    square_rows = lax.broadcasted_iota(jnp.int32, (128, 128), 0)
    square_lanes = lax.broadcasted_iota(jnp.int32, (128, 128), 1)
    load_table.wait()
    spots = [jnp.broadcast_to(nb[side:side + 1, :], (16, 16)) for side in range(6)]
    spots = jnp.concatenate(spots + [jnp.full((32, 16), -1, jnp.int32)], 0)
    own_spot = lax.broadcasted_iota(jnp.int32, (128, 16), 0) & 15
    own_spot = own_spot == lax.broadcasted_iota(jnp.int32, (128, 16), 1)
    entry = jnp.sum(jnp.where(own_spot, spots, 0).astype(jnp.float32), 1, keepdims=True)
    entry = jnp.broadcast_to(entry, (128, 128)).astype(jnp.int32)
    held = entry >= 0
    away = (entry >> (SLOTS * n_gz).bit_length() - 1) - me + 3
    kind = jnp.minimum(away & (n_gx - 1), 7)
    remote = jnp.logical_and(held, kind != 3)
    face = ((square_rows >> 4) ^ 1) * 16 + (entry & 15)
    mine = as_one(jnp.logical_and(remote, kind == square_lanes))
    before = dot(as_one(square_lanes < square_rows), mine)
    rank = dot((before * mine.astype(jnp.float32)).astype(jnp.bfloat16), jnp.ones((128, 128), jnp.bfloat16))
    slot = kind.astype(jnp.float32) * 8.0 + rank
    slot = jnp.where(remote, slot, -16.0)
    lane_ids = square_lanes.astype(jnp.float32)
    face = face.astype(jnp.float32)
    chosen = as_one(slot == lane_ids)
    asked = dot_rows(chosen, face.astype(jnp.bfloat16))
    asked = asked + dot_rows(as_one(slot + 4.0 == lane_ids), (face + 128.0).astype(jnp.bfloat16))
    request[...] = asked[:64].reshape(8, 8, 128)
    far_col[...] = slot[:96]
    take[...] = dot_rows(chosen, as_one(square_rows == square_lanes))[56:64]
    near_col[...] = jnp.where(jnp.logical_and(held, kind == 3), face, -16.0)[:96]
    missing[...] = jnp.where(held, 0.0, 1.0)[:96]
    faces[96:, :] = jnp.zeros((32, 1536), jnp.float32)

    pl.semaphore_wait(barrier, len(PEERS) + n_gz - 1)
    for peer in PEERS:
        pltpu.make_async_remote_copy(
            src_ref=request.at[peer], dst_ref=heard.at[facing(peer)],
            send_sem=request_sent.at[peer], recv_sem=request_got.at[facing(peer)],
            device_id=peer_id(peer), device_id_type=MESH).start()

    coarse_masks = lane_masks(16, 16, 3)
    fine_masks = lane_masks(16, 1, 4)

    def rows_of(axis, position, tile):
        return pl.ds(axis * AXIS_ROWS + position * 32 + tile * 16, 16)

    def keep_face(axis, position, tile, value):
        depth = min(position, 15 - position)
        if depth < 6:
            side = 2 * axis + (position >= 8)
            at = (depth * 2 + tile) * 128
            faces[side * 16:side * 16 + 16, at:at + 128] = value

    def spread(tile, x_of):
        ys = []
        for ytile in range(2):
            ys += exchange([x_of(i, ytile) for i in range(8)], 16, coarse_masks)
        for y in range(16):
            u[rows_of(1, y, tile), :] = ys[y]
            keep_face(1, y, tile, ys[y])
        zs = exchange(ys, 1, fine_masks)
        for z in range(16):
            u[rows_of(2, z, tile), :] = zs[z]
            keep_face(2, z, tile, zs[z])
        return ys, zs

    load_target.wait()
    load.wait()
    for tile in range(2):
        tops = {}
        for i in range(8):
            for ytile in range(2):
                x = tile * 8 + i
                value = start[:, x * 256 + ytile * 128:x * 256 + ytile * 128 + 128]
                u[rows_of(0, x, ytile), :] = value
                keep_face(0, x, ytile, value)
                sigma[rows_of(0, x, ytile), :] = jnp.where(value > 0.0, 1.0, -1.0)
                speed[rows_of(0, x, ytile), :] = 0.1 * value * lax.rsqrt(value * value + 1.0)
                tops[i, ytile] = value
        ys, zs = spread(tile, lambda i, ytile: tops[i, ytile])
        for p in range(16):
            sigma[rows_of(1, p, tile), :] = jnp.where(ys[p] > 0.0, 1.0, -1.0)
            sigma[rows_of(2, p, tile), :] = jnp.where(zs[p] > 0.0, 1.0, -1.0)

    for peer in PEERS:
        pltpu.make_async_remote_copy(
            src_ref=request.at[peer], dst_ref=heard.at[peer],
            send_sem=request_sent.at[peer], recv_sem=request_got.at[peer],
            device_id=peer_id(peer), device_id_type=MESH).wait()

    def copy_of(turn, peer, into):
        return pltpu.make_async_remote_copy(
            src_ref=sends.at[turn, peer], dst_ref=recvs.at[turn, into],
            send_sem=sent.at[turn, peer], recv_sem=got.at[turn, into],
            device_id=peer_id(peer), device_id_type=MESH)

    def serve(turn):
        hi, mid, low = split3(faces[:, :768])
        cols = heard[...].reshape(64, 128)
        left = as_one(cols == lane_ids[:64])
        right = as_one(cols == lane_ids[:64] + 128.0)
        both = jnp.concatenate([left, left], 1)
        out = dot(both, jnp.concatenate([hi[:, :384], mid[:, :384]], 0))
        both = jnp.concatenate([right, right], 1)
        out = out + dot(both, jnp.concatenate([hi[:, 384:], mid[:, 384:]], 0))
        both = jnp.concatenate([left, right], 1)
        out = out + dot(both, jnp.concatenate([low[:, :384], low[:, 384:]], 0))
        sends[turn] = out.reshape(8, 8, 384)
        for peer in PEERS:
            copy_of(turn, peer, facing(peer)).start()
        near = as_one(near_col[...] == lane_ids[:96])
        out = dot(jnp.concatenate([near, near], 1), jnp.concatenate([hi, mid], 0)) + dot(near, low)
        for side in range(6):
            for part in range(6):
                at = (side * 6 + part) * 16
                ghost[at:at + 16, :] = out[side * 16:side * 16 + 16, part * 128:part * 128 + 128]

    def fetch_near(turn):
        for peer in NEAR:
            copy_of(turn, peer, peer).wait()
        none = jnp.zeros((8, 384), jnp.float32)
        hi, mid, low = split3(jnp.concatenate([recvs[turn, c] if c in NEAR else none for c in range(8)], 0))
        arrived = jnp.concatenate([hi, mid, low, jnp.zeros_like(low)], 0)
        fold = jnp.where(lane_ids[:96] >= 64.0, lane_ids[:96] - 64.0, lane_ids[:96])
        for half in range(2):
            pick = as_one(far_col[...] + 4.0 * half == fold)
            out = dot(jnp.concatenate([pick, pick], 1), arrived)
            for side in range(6):
                for part in range(3):
                    at = (side * 6 + half * 3 + part) * 16
                    ghost[at:at + 16, :] += out[side * 16:side * 16 + 16, part * 128:part * 128 + 128]

    def own_cells():
        hi, mid, low = split3(faces[...])
        one = take[...].astype(jnp.bfloat16)
        return dot(jnp.concatenate([one, one], 1), jnp.concatenate([hi, mid], 0)) + dot(one, low)

    def put_far(values):
        parts = [part.astype(jnp.float32) for part in split3(values)]
        parts = jnp.concatenate(parts + [jnp.zeros_like(values)], 0).astype(jnp.bfloat16)
        lanes = lax.broadcasted_iota(jnp.int32, (96, 32), 1)
        rows = jnp.where(lanes < 24, (lanes & 7) + 56, -1).astype(jnp.float32)
        return dot(as_one(far_col[:, :32] == rows), parts)

    def is_far(side):
        return far_col[side * 16:side * 16 + 16, :] >= 56.0

    def far_weno(turn, own):
        copy_of(turn, FAR, FAR).wait()
        came = recvs[turn, FAR]
        other = pltpu.roll(came, 4, 0)
        result = {}
        for tile in range(2):
            values = {}
            for depth in range(3):
                part = depth * 2 + tile
                from_ = came if part < 3 else other
                values[-1 - depth] = from_[:, part % 3 * 128:part % 3 * 128 + 128]
            for depth in range(6):
                at = (depth * 2 + tile) * 128
                values[depth] = own[:, at:at + 128]

            def signs(i):
                return far_sigma[:, (i * 2 + tile) * 128:(i * 2 + tile) * 128 + 128]

            def store(i, value):
                result[i * 2 + tile] = value

            weno_axis(values, 0, 3, signs, store)
        return put_far(jnp.concatenate([result[part] for part in range(6)], 1))

    def column_rows(axis, position, column):
        return pl.ds(axis * AXIS_ROWS + position * 32 + column * 8, 8)

    def ghosts_at(axis, high, depth, column, edge):
        values = ghost[pl.ds((2 * axis + high) * 96 + depth * 32 + column * 8, 8), :]
        gone = missing[pl.ds((2 * axis + high) * 16 + (column % 2) * 8, 8), :]
        return jnp.where(gone > 0.0, edge, values)

    def weno_part(index, low, high):
        axis, column = index // 4, index % 4
        load = lambda i: u[column_rows(axis, i, column), :]
        signs = lambda i: sigma[column_rows(axis, i, column), :]

        def store(i, value):
            grad[column_rows(axis, i, column), :] = value

        if low == 3:
            values = {i: load(i) for i in range(16)}
            weno_axis(values, 3, 13, signs, store)
            return
        values = {i: load(i) for i in range(6)}
        for i in range(3):
            values[-1 - i] = ghosts_at(axis, 0, i, column, values[0])
        weno_axis(values, 0, 3, signs, store)
        values = {i: load(i) for i in range(10, 16)}
        for i in range(3):
            values[16 + i] = ghosts_at(axis, 1, i, column, values[15])
        weno_axis(values, 13, 16, signs, store)

    first = own_cells()[:, :768]
    far_sigma[...] = jnp.where(first > 0.0, 1.0, -1.0)

    def step(turn, carry):
        serve(turn)

        def inner(index, c):
            weno_part(index, 3, 13)
            return c

        def outer(index, c):
            weno_part(index, 0, 16)
            return c

        lax.fori_loop(0, 12, inner, 0)
        own = own_cells()
        fetch_near(turn)
        lax.fori_loop(0, 12, outer, 0)
        fixed = far_weno(turn, own)

        def grad_at(axis, position, tile):
            value = grad[rows_of(axis, position, tile), :]
            depth = min(position, 15 - position)
            if depth >= 3:
                return value
            side = 2 * axis + (position >= 8)
            at = (depth * 2 + tile) * 128
            return jnp.where(is_far(side), fixed[side * 16:side * 16 + 16, at:at + 128], value)

        for tile in range(2):
            sums = exchange([grad_at(2, z, tile) for z in range(16)], 1, fine_masks)
            sums = [sums[y] + grad_at(1, y, tile) for y in range(16)]
            fresh = {}
            for ytile in range(2):
                xs = exchange(sums[ytile * 8:ytile * 8 + 8], 16, coarse_masks)
                for i in range(8):
                    rows = rows_of(0, tile * 8 + i, ytile)
                    steep = jnp.sqrt(xs[i] + grad_at(0, tile * 8 + i, ytile))
                    value = u[rows, :] - speed[rows, :] * (steep - 3.0)
                    u[rows, :] = value
                    keep_face(0, tile * 8 + i, ytile, value)
                    fresh[i, ytile] = value
            spread(tile, lambda i, ytile: fresh[i, ytile])
        return carry

    lax.fori_loop(0, STEPS, step, 0)

    serve(STEPS)
    keep = lax.broadcasted_iota(jnp.int32, (16, 128), 0) < live[0]
    for x in range(16):
        for ytile in range(2):
            at = x * 256 + ytile * 128
            level_out[:, at:at + 128] = jnp.where(keep, u[rows_of(0, x, ytile), :], 0.0)

    r = lax.broadcasted_iota(jnp.int32, (256, 256), 0)
    l = lax.broadcasted_iota(jnp.int32, (256, 256), 1)
    same = jnp.logical_and((r >> 5) == ((l >> 4) & 7), ((r >> 1) & 7) == (l & 7))
    average = jnp.where(same, 1.0 / 16.0, 0.0).astype(jnp.bfloat16)
    average = jnp.concatenate([average, average], 0)
    swap = as_one(l == (r & 15) * 16 + (r >> 4))
    swap = jnp.concatenate([swap, swap, swap], 0)
    lanes = lax.broadcasted_iota(jnp.int32, (16, 256), 1)
    brick_rows = lax.broadcasted_iota(jnp.int32, (16, 256), 0)
    lane_bricks = lax.broadcasted_iota(jnp.int32, (64, 128), 1)
    by_row = jnp.zeros((16, 256), jnp.int32)
    by_lane = jnp.full((64, 128), -1, jnp.int32)
    for b in range(16):
        by_row = jnp.where(brick_rows == b, target[b], by_row)
        by_lane = jnp.where((lane_bricks & 15) == b, target[b], by_lane)
    octant = jnp.logical_and(((by_row >> 2) & 1) == (lanes >> 7), ((by_row >> 1) & 1) == ((lanes >> 3) & 1))
    octant = jnp.where(octant, 1.0, 0.0)
    share, deep = 64 // n_gz, SIDE // n_gz
    out_rows = lax.broadcasted_iota(jnp.int32, (64, 128), 0)
    out_z = (out_rows // share) * deep + (out_rows & (deep - 1))
    pick = jnp.logical_and((by_lane >> 3) == (out_rows & (share - 1)) // deep, (by_lane & 1) == (out_z >> 3))
    pick = as_one(jnp.logical_and(pick, (lane_bricks >> 4) == (out_z & 7)))
    turns = sorted(range(1, n_gz), key=lambda turn: abs(2 * turn - n_gz))

    fetch_near(STEPS)

    def rim(axis, high, tile, edge):
        side = 2 * axis + high
        values = ghost[side * 96 + tile * 16:side * 96 + tile * 16 + 16, :]
        return jnp.where(missing[side * 16:side * 16 + 16, :] > 0.0, edge, values)

    def beside(axis, position, tile):
        here = u[rows_of(axis, position, tile), :]
        low = rim(axis, 0, tile, here) if position == 0 else u[rows_of(axis, position - 1, tile), :]
        high = rim(axis, 1, tile, here) if position == 15 else u[rows_of(axis, position + 1, tile), :]
        return (high + low) - (here + here), high - low, here

    for tile in range(2):
        lap_y, grad_x = [], []
        for ytile in range(2):
            parts = [beside(0, tile * 8 + i, ytile) for i in range(8)]
            lap_y += exchange([p[0] for p in parts], 16, coarse_masks)
            grad_x += exchange([p[1] for p in parts], 16, coarse_masks)
        parts = [beside(1, y, tile) for y in range(16)]
        laps = exchange([lap_y[y] + parts[y][0] for y in range(16)], 1, fine_masks)
        grad_x = exchange(grad_x, 1, fine_masks)
        grad_y = exchange([p[1] for p in parts], 1, fine_masks)
        for z in range(16):
            lap, grad_z, here = beside(2, z, tile)
            v2 = jnp.minimum(here * here, BAND_WIDTH * BAND_WIDTH) * ((math.pi / 3.0) ** 2)
            wave = 1.0 / 479001600.0
            for power in (-1.0 / 3628800.0, 1.0 / 40320.0, -1.0 / 720.0, 1.0 / 24.0, -0.5, 1.0):
                wave = wave * v2 + power
            grad[rows_of(0, z, tile), :] = lap + laps[z]
            grad[rows_of(1, z, tile), :] = grad_x[z]
            grad[rows_of(2, z, tile), :] = grad_y[z]
            sigma[rows_of(0, z, tile), :] = grad_z
            sigma[rows_of(1, z, tile), :] = jnp.where(jnp.abs(here) < BAND_WIDTH, wave * wave * (2.0 / 3.0), 0.0)

    copy_of(STEPS, FAR, FAR).wait()
    far_rim = put_far(recvs[STEPS, FAR, :, :256])
    turned = dot(jnp.concatenate(split3(far_rim[:32]), 1), swap)
    groups = lax.broadcasted_iota(jnp.int32, (16, 128), 1)
    y_ids, x_ids = groups & 15, groups >> 4

    def moved_to(mask, values, by):
        return jnp.where(mask, pltpu.roll(values, by % 128, 1) if by % 128 else values, 0.0)

    for tile in range(2):
        edge = 7 * tile
        held = None
        for z in range(16):
            at = z // 8 * 128
            add_x = moved_to(x_ids == edge, turned[tile * 16:tile * 16 + 16, at:at + 128], 16 * (edge - z % 8))
            at = tile * 128
            low_y = moved_to(y_ids == 0, far_rim[32:48, at:at + 128], -z)
            high_y = moved_to(y_ids == 15, far_rim[48:64, at:at + 128], 15 - z)
            lap = (grad[rows_of(0, z, tile), :] + add_x) + (low_y + high_y)
            grad_x = grad[rows_of(1, z, tile), :] + (add_x if tile else -add_x)
            grad_y = grad[rows_of(2, z, tile), :] + (high_y - low_y)
            grad_z = sigma[rows_of(0, z, tile), :]
            if z == 0:
                lap = lap + far_rim[64:80, at:at + 128]
                grad_z = grad_z - far_rim[64:80, at:at + 128]
            if z == 15:
                lap = lap + far_rim[80:96, at:at + 128]
                grad_z = grad_z + far_rim[80:96, at:at + 128]
            lap = lap * sigma[rows_of(1, z, tile), :]
            forces = [lap * grad_x, lap * grad_y, lap * grad_z]
            if z % 2 == 0:
                held = forces
            else:
                for a in range(3):
                    force[a, pl.ds(z // 2 * 16, 16), at:at + 128] = held[a] + forces[a]

    def part_copy(a, turn):
        to = lax.rem(layer + turn, n_gz)
        return pltpu.make_async_remote_copy(
            src_ref=fsend.at[to, a], dst_ref=frecv.at[turn - 1, a],
            send_sem=fsent.at[turn - 1, a], recv_sem=fgot.at[turn - 1, a],
            device_id={"gz": to}, device_id_type=MESH)

    for a in range(3):
        block = dot(jnp.concatenate(split3(force[a])[:2], 1), average)
        block = (block.reshape(8, 16, 256) * octant[None]).reshape(128, 256)
        hi, mid, _ = split3(block)
        result = dot(pick, hi) + dot(pick, mid)
        for g in range(n_gz):
            fsend[g, a] = result[g * share:(g + 1) * share]
        for turn in turns:
            part_copy(a, turn).start()
    for a in range(3):
        total = fsend[layer, a]
        for turn in turns:
            part_copy(a, turn).wait()
            total = total + frecv[turn - 1, a]
        for s in range(DENSE):
            part_out[s, a] = total[s * deep:(s + 1) * deep]


def finish(level, force, level_out, force_out, level_sem, force_sem):
    level_copy = pltpu.make_async_copy(level, level_out, level_sem)
    force_copy = pltpu.make_async_copy(force, force_out, force_sem)
    level_copy.start()
    force_copy.start()
    force_copy.wait()
    level_copy.wait()


def shards(n_gx, n_gz, level_set, neighbours, live_count, dense_target):
    share = 64 // n_gz
    vmem = pl.BlockSpec(memory_space=pltpu.VMEM)
    anywhere = pl.BlockSpec(memory_space=pl.ANY)
    dma, f32 = pltpu.SemaphoreType.DMA, jnp.float32
    def far_memory(array):
        return pltpu.with_memory_space_constraint(array, pltpu.HBM)

    level, part = pl.pallas_call(
        functools.partial(kernel, n_gx, n_gz),
        out_shape=(jax.ShapeDtypeStruct(level_set.shape, f32), jax.ShapeDtypeStruct((DENSE, 3, SIDE // n_gz, 256), f32)),
        in_specs=[anywhere, pl.BlockSpec(memory_space=pltpu.SMEM), anywhere, anywhere],
        out_specs=(vmem, vmem),
        scratch_shapes=[
            pltpu.VMEM((6, SLOTS), jnp.int32),
            pltpu.SMEM((SLOTS,), jnp.int32),
            pltpu.VMEM(level_set.shape, f32),
            pltpu.VMEM((3 * AXIS_ROWS, 128), f32),
            pltpu.VMEM((128, 1536), f32),
            pltpu.VMEM((36 * 16, 128), f32),
            pltpu.VMEM((3 * AXIS_ROWS, 128), f32),
            pltpu.VMEM((3 * AXIS_ROWS, 128), f32),
            pltpu.VMEM((AXIS_ROWS, 128), f32),
            pltpu.VMEM((96, 128), f32),
            pltpu.VMEM((96, 128), f32),
            pltpu.VMEM((96, 128), f32),
            pltpu.VMEM((8, 128), f32),
            pltpu.VMEM((8, 768), f32),
            pltpu.VMEM((3, 128, 256), f32),
            pltpu.VMEM((8, 8, 128), f32),
            pltpu.VMEM((8, 8, 128), f32),
            pltpu.VMEM((ROUNDS, 8, 8, 384), f32),
            pltpu.VMEM((ROUNDS, 8, 8, 384), f32),
            pltpu.VMEM((n_gz, 3, share, 256), f32),
            pltpu.VMEM((n_gz - 1, 3, share, 256), f32),
            dma(()), dma(()), dma(()), dma((8,)), dma((8,)), dma((ROUNDS, 8)), dma((ROUNDS, 8)), dma((n_gz - 1, 3)), dma((n_gz - 1, 3)),
        ],
        compiler_params=pltpu.CompilerParams(
            collective_id=0, has_side_effects=True, vmem_limit_bytes=24 << 20),
    )(far_memory(neighbours.T), live_count, far_memory(dense_target), far_memory(level_set))
    results = tuple(pltpu.with_memory_space_constraint(r, pltpu.VMEM) for r in (level, part))
    return pl.pallas_call(
        finish,
        out_shape=tuple(jax.ShapeDtypeStruct(r.shape, f32) for r in results),
        in_specs=[anywhere] * 2,
        out_specs=(anywhere,) * 2,
        scratch_shapes=[dma(()), dma(())],
    )(*results)


def solution(mesh):
    placed = (P(("gx", "gz"), None), P(("gx", "gz"), None), P(("gx", "gz")), P(("gx", "gz")))
    return jax.shard_map(
        functools.partial(shards, mesh.shape["gx"], mesh.shape["gz"]),
        mesh=mesh,
        in_specs=placed,
        out_specs=(P(("gx", "gz"), None), P("gx", None, "gz", None)),
        check_vma=False,
    )
```

```python
import functools
import math

import jax
import jax.numpy as jnp
from jax import lax
from jax.experimental import pallas as pl
from jax.experimental.pallas import tpu as pltpu
from jax.sharding import PartitionSpec as P

SIDE = 16
SLOTS = 16
DENSE = 4
STEPS = 3
ROUNDS = STEPS + 1
BAND_WIDTH = 1.5
MESH = pl.DeviceIdType.MESH

PEERS = (7, 0, 6, 1, 5, 2, 4)
NEAR = (0, 6, 1, 5, 2, 4)
FAR = 7
AXIS_ROWS = 512


def facing(peer):
    return 7 if peer == 7 else 6 - peer


def exchange(values, width, masks):
    count = len(values)
    bits = count.bit_length() - 1
    rolled = [v if j == 0 else pltpu.roll(v, j * width, 1) for j, v in enumerate(values)]
    moved = [rolled[-i % count] for i in range(count)]
    for bit in range(bits):
        moved = [jnp.where(masks[bit], moved[(i - (1 << bit)) % count], moved[i]) for i in range(count)]
    return [v if i == 0 else pltpu.roll(v, 128 - i * width, 1) for i, v in enumerate(moved)]


def lane_masks(rows, width, bits):
    lanes = lax.broadcasted_iota(jnp.int32, (rows, 128), 1)
    return [(lanes & (width << bit)) != 0 for bit in range(bits)]


def weno_axis(u, first, last, sigma, store):
    d = {j: u[j] - u[j - 1] for j in range(first - 2, last + 3)}
    e = {j: d[j + 1] - d[j] for j in range(first - 2, last + 2)}
    s = {j: e[j] - e[j - 1] for j in range(first - 1, last + 2)}
    t = {j: s[j + 1] - s[j] for j in range(first - 1, last + 1)}
    r1, r2, r3 = {}, {}, {}
    for j in range(first - 1, last + 2):
        base = (13.0 / 3.0) * (s[j] * s[j]) + 4e-6
        if j <= last - 1:
            lean = (e[j] + e[j]) + s[j]
            r = pltpu.reciprocal(base + lean * lean, approx=True)
            r1[j] = r * r
        if first <= j <= last:
            lean = e[j] + e[j - 1]
            r = pltpu.reciprocal(base + lean * lean, approx=True)
            r2[j] = 6.0 * (r * r)
        if j >= first + 1:
            lean = s[j] - (e[j - 1] + e[j - 1])
            r = pltpu.reciprocal(base + lean * lean, approx=True)
            r3[j] = r * r
    for i in range(first, last):
        half = 0.5 * t[i]
        left = 3.0 * d[i] + (e[i] + 0.5 * e[i - 1])
        right = left - half
        w3 = 3.0 * r3[i + 1]
        den = (r1[i - 1] + r2[i]) + w3
        num = r1[i - 1] * t[i - 1] + w3 * half
        left = left - num * pltpu.reciprocal(den, approx=True)
        w3 = 3.0 * r1[i]
        den = (r3[i + 2] + r2[i + 1]) + w3
        num = r3[i + 2] * t[i + 1] + w3 * half
        right = right + num * pltpu.reciprocal(den, approx=True)
        m = jnp.maximum(jnp.maximum(sigma(i) * left, -sigma(i) * right), 0.0)
        store(i, m * m)


def split3(x):
    hi = x.astype(jnp.bfloat16)
    rest = x - hi.astype(jnp.float32)
    mid = rest.astype(jnp.bfloat16)
    low = (rest - mid.astype(jnp.float32)).astype(jnp.bfloat16)
    return hi, mid, low


def as_one(mask):
    return jnp.where(mask, 1.0, 0.0).astype(jnp.bfloat16)


def dot_rows(a, b):
    return lax.dot_general(a, b, (((0,), (0,)), ((), ())), preferred_element_type=jnp.float32)


def dot(a, b):
    return lax.dot_general(a, b, (((1,), (0,)), ((), ())), preferred_element_type=jnp.float32)


def kernel(n_gx, n_gz, table, live, target_in, level, level_out, part_out,
           nb, target, start, u, faces, ghost, sigma, grad, speed, missing, near_col, far_col, take, far_sigma, force, request, heard,
           sends, recvs, fsend, frecv,
           table_loaded, target_loaded, loaded, request_sent, request_got, sent, got, fsent, fgot):
    me = lax.axis_index("gx")
    layer = lax.axis_index("gz")

    def peer_id(peer):
        step = n_gx // 2 if peer == 7 else peer - 3
        return {"gx": lax.rem(me + step + n_gx, n_gx)}

    load = pltpu.make_async_copy(level, start, loaded)
    load.start()
    load_table = pltpu.make_async_copy(table, nb, table_loaded)
    load_table.start()
    load_target = pltpu.make_async_copy(target_in, target, target_loaded)
    load_target.start()
    barrier = pltpu.get_barrier_semaphore()
    for peer in PEERS:
        pl.semaphore_signal(barrier, inc=1, device_id=peer_id(peer), device_id_type=MESH)
    for turn in range(1, n_gz):
        pl.semaphore_signal(barrier, inc=1, device_id={"gz": lax.rem(layer + turn, n_gz)}, device_id_type=MESH)

    square_rows = lax.broadcasted_iota(jnp.int32, (128, 128), 0)
    square_lanes = lax.broadcasted_iota(jnp.int32, (128, 128), 1)
    load_table.wait()
    spots = [jnp.broadcast_to(nb[side:side + 1, :], (16, 16)) for side in range(6)]
    spots = jnp.concatenate(spots + [jnp.full((32, 16), -1, jnp.int32)], 0)
    own_spot = lax.broadcasted_iota(jnp.int32, (128, 16), 0) & 15
    own_spot = own_spot == lax.broadcasted_iota(jnp.int32, (128, 16), 1)
    entry = jnp.sum(jnp.where(own_spot, spots, 0).astype(jnp.float32), 1, keepdims=True)
    entry = jnp.broadcast_to(entry, (128, 128)).astype(jnp.int32)
    held = entry >= 0
    away = (entry >> (SLOTS * n_gz).bit_length() - 1) - me + 3
    kind = jnp.minimum(away & (n_gx - 1), 7)
    remote = jnp.logical_and(held, kind != 3)
    face = ((square_rows >> 4) ^ 1) * 16 + (entry & 15)
    mine = as_one(jnp.logical_and(remote, kind == square_lanes))
    before = dot(as_one(square_lanes < square_rows), mine)
    rank = dot((before * mine.astype(jnp.float32)).astype(jnp.bfloat16), jnp.ones((128, 128), jnp.bfloat16))
    slot = kind.astype(jnp.float32) * 8.0 + rank
    slot = jnp.where(remote, slot, -16.0)
    lane_ids = square_lanes.astype(jnp.float32)
    face = face.astype(jnp.float32)
    chosen = as_one(slot == lane_ids)
    asked = dot_rows(chosen, face.astype(jnp.bfloat16))
    asked = asked + dot_rows(as_one(slot + 4.0 == lane_ids), (face + 128.0).astype(jnp.bfloat16))
    request[...] = asked[:64].reshape(8, 8, 128)
    far_col[...] = slot[:96]
    take[...] = dot_rows(chosen, as_one(square_rows == square_lanes))[56:64]
    near_col[...] = jnp.where(jnp.logical_and(held, kind == 3), face, -16.0)[:96]
    missing[...] = jnp.where(held, 0.0, 1.0)[:96]
    faces[96:, :] = jnp.zeros((32, 1536), jnp.float32)

    pl.semaphore_wait(barrier, len(PEERS) + n_gz - 1)
    for peer in PEERS:
        pltpu.make_async_remote_copy(
            src_ref=request.at[peer], dst_ref=heard.at[facing(peer)],
            send_sem=request_sent.at[peer], recv_sem=request_got.at[facing(peer)],
            device_id=peer_id(peer), device_id_type=MESH).start()

    coarse_masks = lane_masks(16, 16, 3)
    fine_masks = lane_masks(16, 1, 4)

    def rows_of(axis, position, tile):
        return pl.ds(axis * AXIS_ROWS + position * 32 + tile * 16, 16)

    def keep_face(axis, position, tile, value):
        depth = min(position, 15 - position)
        if depth < 6:
            side = 2 * axis + (position >= 8)
            at = (depth * 2 + tile) * 128
            faces[side * 16:side * 16 + 16, at:at + 128] = value

    def spread(tile, x_of):
        ys = []
        for ytile in range(2):
            ys += exchange([x_of(i, ytile) for i in range(8)], 16, coarse_masks)
        for y in range(16):
            u[rows_of(1, y, tile), :] = ys[y]
            keep_face(1, y, tile, ys[y])
        zs = exchange(ys, 1, fine_masks)
        for z in range(16):
            u[rows_of(2, z, tile), :] = zs[z]
            keep_face(2, z, tile, zs[z])
        return ys, zs

    load_target.wait()
    load.wait()
    for tile in range(2):
        tops = {}
        for i in range(8):
            for ytile in range(2):
                x = tile * 8 + i
                value = start[:, x * 256 + ytile * 128:x * 256 + ytile * 128 + 128]
                u[rows_of(0, x, ytile), :] = value
                keep_face(0, x, ytile, value)
                sigma[rows_of(0, x, ytile), :] = jnp.where(value > 0.0, 1.0, -1.0)
                speed[rows_of(0, x, ytile), :] = 0.1 * value * lax.rsqrt(value * value + 1.0)
                tops[i, ytile] = value
        ys, zs = spread(tile, lambda i, ytile: tops[i, ytile])
        for p in range(16):
            sigma[rows_of(1, p, tile), :] = jnp.where(ys[p] > 0.0, 1.0, -1.0)
            sigma[rows_of(2, p, tile), :] = jnp.where(zs[p] > 0.0, 1.0, -1.0)

    for peer in PEERS:
        pltpu.make_async_remote_copy(
            src_ref=request.at[peer], dst_ref=heard.at[peer],
            send_sem=request_sent.at[peer], recv_sem=request_got.at[peer],
            device_id=peer_id(peer), device_id_type=MESH).wait()

    def copy_of(turn, peer, into):
        return pltpu.make_async_remote_copy(
            src_ref=sends.at[turn, peer], dst_ref=recvs.at[turn, into],
            send_sem=sent.at[turn, peer], recv_sem=got.at[turn, into],
            device_id=peer_id(peer), device_id_type=MESH)

    def serve(turn):
        hi, mid, low = split3(faces[:, :768])
        cols = heard[...].reshape(64, 128)
        left = as_one(cols == lane_ids[:64])
        right = as_one(cols == lane_ids[:64] + 128.0)
        both = jnp.concatenate([left, left], 1)
        out = dot(both, jnp.concatenate([hi[:, :384], mid[:, :384]], 0))
        both = jnp.concatenate([right, right], 1)
        out = out + dot(both, jnp.concatenate([hi[:, 384:], mid[:, 384:]], 0))
        both = jnp.concatenate([left, right], 1)
        out = out + dot(both, jnp.concatenate([low[:, :384], low[:, 384:]], 0))
        sends[turn] = out.reshape(8, 8, 384)
        for peer in PEERS:
            copy_of(turn, peer, facing(peer)).start()
        near = as_one(near_col[...] == lane_ids[:96])
        out = dot(jnp.concatenate([near, near], 1), jnp.concatenate([hi, mid], 0)) + dot(near, low)
        for side in range(6):
            for part in range(6):
                at = (side * 6 + part) * 16
                ghost[at:at + 16, :] = out[side * 16:side * 16 + 16, part * 128:part * 128 + 128]

    def near_faces(turn):
        for peer in NEAR:
            copy_of(turn, peer, peer).wait()
        none = jnp.zeros((8, 384), jnp.float32)
        hi, mid, low = split3(jnp.concatenate([recvs[turn, c] if c in NEAR else none for c in range(8)], 0))
        return jnp.concatenate([hi, mid, low, jnp.zeros_like(low)], 0)

    def put_near(arrived, half):
        fold = jnp.where(lane_ids[:96] >= 64.0, lane_ids[:96] - 64.0, lane_ids[:96])
        pick = as_one(far_col[...] + 4.0 * half == fold)
        return dot(jnp.concatenate([pick, pick], 1), arrived)

    def fetch_near(turn):
        arrived = near_faces(turn)
        for half in range(2):
            out = put_near(arrived, half)
            for side in range(6):
                for part in range(3):
                    at = (side * 6 + half * 3 + part) * 16
                    ghost[at:at + 16, :] += out[side * 16:side * 16 + 16, part * 128:part * 128 + 128]

    def own_cells():
        hi, mid, low = split3(faces[...])
        one = take[...].astype(jnp.bfloat16)
        return dot(jnp.concatenate([one, one], 1), jnp.concatenate([hi, mid], 0)) + dot(one, low)

    def put_far(values):
        parts = [part.astype(jnp.float32) for part in split3(values)]
        parts = jnp.concatenate(parts + [jnp.zeros_like(values)], 0).astype(jnp.bfloat16)
        lanes = lax.broadcasted_iota(jnp.int32, (96, 32), 1)
        rows = jnp.where(lanes < 24, (lanes & 7) + 56, -1).astype(jnp.float32)
        return dot(as_one(far_col[:, :32] == rows), parts)

    def is_far(side):
        return far_col[side * 16:side * 16 + 16, :] >= 56.0

    def far_weno(turn, own):
        copy_of(turn, FAR, FAR).wait()
        came = recvs[turn, FAR]
        other = pltpu.roll(came, 4, 0)
        result = {}
        for tile in range(2):
            values = {}
            for depth in range(3):
                part = depth * 2 + tile
                from_ = came if part < 3 else other
                values[-1 - depth] = from_[:, part % 3 * 128:part % 3 * 128 + 128]
            for depth in range(6):
                at = (depth * 2 + tile) * 128
                values[depth] = own[:, at:at + 128]

            def signs(i):
                return far_sigma[:, (i * 2 + tile) * 128:(i * 2 + tile) * 128 + 128]

            def store(i, value):
                result[i * 2 + tile] = value

            weno_axis(values, 0, 3, signs, store)
        return put_far(jnp.concatenate([result[part] for part in range(6)], 1))

    def column_rows(axis, position, column):
        return pl.ds(axis * AXIS_ROWS + position * 32 + column * 8, 8)

    def ghosts_at(axis, high, depth, column, edge):
        values = ghost[pl.ds((2 * axis + high) * 96 + depth * 32 + column * 8, 8), :]
        gone = missing[pl.ds((2 * axis + high) * 16 + (column % 2) * 8, 8), :]
        return jnp.where(gone > 0.0, edge, values)

    def weno_part(index, low, high):
        axis, column = index // 4, index % 4
        load = lambda i: u[column_rows(axis, i, column), :]
        signs = lambda i: sigma[column_rows(axis, i, column), :]

        def store(i, value):
            grad[column_rows(axis, i, column), :] = value

        if low == 3:
            values = {i: load(i) for i in range(16)}
            weno_axis(values, 3, 13, signs, store)
            return
        values = {i: load(i) for i in range(6)}
        for i in range(3):
            values[-1 - i] = ghosts_at(axis, 0, i, column, values[0])
        weno_axis(values, 0, 3, signs, store)
        values = {i: load(i) for i in range(10, 16)}
        for i in range(3):
            values[16 + i] = ghosts_at(axis, 1, i, column, values[15])
        weno_axis(values, 13, 16, signs, store)

    first = own_cells()[:, :768]
    far_sigma[...] = jnp.where(first > 0.0, 1.0, -1.0)

    def step(turn, carry):
        serve(turn)

        def inner(index, c):
            weno_part(index, 3, 13)
            return c

        def outer(index, c):
            weno_part(index, 0, 16)
            return c

        lax.fori_loop(0, 12, inner, 0)
        own = own_cells()
        fetch_near(turn)
        lax.fori_loop(0, 12, outer, 0)
        fixed = far_weno(turn, own)

        def grad_at(axis, position, tile):
            value = grad[rows_of(axis, position, tile), :]
            depth = min(position, 15 - position)
            if depth >= 3:
                return value
            side = 2 * axis + (position >= 8)
            at = (depth * 2 + tile) * 128
            return jnp.where(is_far(side), fixed[side * 16:side * 16 + 16, at:at + 128], value)

        for tile in range(2):
            sums = exchange([grad_at(2, z, tile) for z in range(16)], 1, fine_masks)
            sums = [sums[y] + grad_at(1, y, tile) for y in range(16)]
            fresh = {}
            for ytile in range(2):
                xs = exchange(sums[ytile * 8:ytile * 8 + 8], 16, coarse_masks)
                for i in range(8):
                    rows = rows_of(0, tile * 8 + i, ytile)
                    steep = jnp.sqrt(xs[i] + grad_at(0, tile * 8 + i, ytile))
                    value = u[rows, :] - speed[rows, :] * (steep - 3.0)
                    u[rows, :] = value
                    keep_face(0, tile * 8 + i, ytile, value)
                    fresh[i, ytile] = value
            spread(tile, lambda i, ytile: fresh[i, ytile])
        return carry

    lax.fori_loop(0, STEPS, step, 0)

    serve(STEPS)
    keep = lax.broadcasted_iota(jnp.int32, (16, 128), 0) < live[0]
    for x in range(16):
        for ytile in range(2):
            at = x * 256 + ytile * 128
            level_out[:, at:at + 128] = jnp.where(keep, u[rows_of(0, x, ytile), :], 0.0)

    r = lax.broadcasted_iota(jnp.int32, (256, 256), 0)
    l = lax.broadcasted_iota(jnp.int32, (256, 256), 1)
    same = jnp.logical_and((r >> 5) == ((l >> 4) & 7), ((r >> 1) & 7) == (l & 7))
    average = jnp.where(same, 1.0 / 16.0, 0.0).astype(jnp.bfloat16)
    average = jnp.concatenate([average, average], 0)
    swap = as_one(l == (r & 15) * 16 + (r >> 4))
    swap = jnp.concatenate([swap, swap, swap], 0)
    lanes = lax.broadcasted_iota(jnp.int32, (16, 256), 1)
    brick_rows = lax.broadcasted_iota(jnp.int32, (16, 256), 0)
    lane_bricks = lax.broadcasted_iota(jnp.int32, (64, 128), 1)
    by_row = jnp.zeros((16, 256), jnp.int32)
    by_lane = jnp.full((64, 128), -1, jnp.int32)
    for b in range(16):
        by_row = jnp.where(brick_rows == b, target[b], by_row)
        by_lane = jnp.where((lane_bricks & 15) == b, target[b], by_lane)
    octant = jnp.logical_and(((by_row >> 2) & 1) == (lanes >> 7), ((by_row >> 1) & 1) == ((lanes >> 3) & 1))
    octant = jnp.where(octant, 1.0, 0.0)
    share, deep = 64 // n_gz, SIDE // n_gz
    out_rows = lax.broadcasted_iota(jnp.int32, (64, 128), 0)
    out_z = (out_rows // share) * deep + (out_rows & (deep - 1))
    pick = jnp.logical_and((by_lane >> 3) == (out_rows & (share - 1)) // deep, (by_lane & 1) == (out_z >> 3))
    pick = as_one(jnp.logical_and(pick, (lane_bricks >> 4) == (out_z & 7)))
    turns = sorted(range(1, n_gz), key=lambda turn: abs(2 * turn - n_gz))


    def rim(axis, high, tile, edge):
        side = 2 * axis + high
        values = ghost[side * 96 + tile * 16:side * 96 + tile * 16 + 16, :]
        return jnp.where(missing[side * 16:side * 16 + 16, :] > 0.0, edge, values)

    def beside(axis, position, tile):
        here = u[rows_of(axis, position, tile), :]
        low = rim(axis, 0, tile, here) if position == 0 else u[rows_of(axis, position - 1, tile), :]
        high = rim(axis, 1, tile, here) if position == 15 else u[rows_of(axis, position + 1, tile), :]
        return (high + low) - (here + here), high - low, here

    for tile in range(2):
        lap_y, grad_x = [], []
        for ytile in range(2):
            parts = [beside(0, tile * 8 + i, ytile) for i in range(8)]
            lap_y += exchange([p[0] for p in parts], 16, coarse_masks)
            grad_x += exchange([p[1] for p in parts], 16, coarse_masks)
        parts = [beside(1, y, tile) for y in range(16)]
        laps = exchange([lap_y[y] + parts[y][0] for y in range(16)], 1, fine_masks)
        grad_x = exchange(grad_x, 1, fine_masks)
        grad_y = exchange([p[1] for p in parts], 1, fine_masks)
        for z in range(16):
            lap, grad_z, here = beside(2, z, tile)
            v2 = jnp.minimum(here * here, BAND_WIDTH * BAND_WIDTH) * ((math.pi / 3.0) ** 2)
            wave = 1.0 / 479001600.0
            for power in (-1.0 / 3628800.0, 1.0 / 40320.0, -1.0 / 720.0, 1.0 / 24.0, -0.5, 1.0):
                wave = wave * v2 + power
            grad[rows_of(0, z, tile), :] = lap + laps[z]
            grad[rows_of(1, z, tile), :] = grad_x[z]
            grad[rows_of(2, z, tile), :] = grad_y[z]
            sigma[rows_of(0, z, tile), :] = grad_z
            sigma[rows_of(1, z, tile), :] = jnp.where(jnp.abs(here) < BAND_WIDTH, wave * wave * (2.0 / 3.0), 0.0)

    rims = put_near(near_faces(STEPS)[:, :256], 0)
    copy_of(STEPS, FAR, FAR).wait()
    rims = rims + put_far(recvs[STEPS, FAR, :, :256])
    turned = dot(jnp.concatenate(split3(rims[:32]), 1), swap)
    groups = lax.broadcasted_iota(jnp.int32, (16, 128), 1)
    y_ids, x_ids = groups & 15, groups >> 4

    def moved(values, by):
        return pltpu.roll(values, by % 128, 1) if by % 128 else values

    for tile in range(2):
        edge = 7 * tile
        held = None
        low_y = rims[32:48, tile * 128:tile * 128 + 128]
        high_y = moved(rims[48:64, tile * 128:tile * 128 + 128], 15)
        for z in range(16):
            at = z // 8 * 128
            add_x = moved(turned[tile * 16:tile * 16 + 16, at:at + 128], 16 * (edge - z % 8))
            add_x = jnp.where(x_ids == edge, add_x, 0.0)
            add_y = moved(jnp.where(y_ids == z, low_y, high_y), -z)
            add_y = jnp.where(jnp.logical_or(y_ids == 0, y_ids == 15), add_y, 0.0)
            at = tile * 128
            lap = grad[rows_of(0, z, tile), :] + (add_x + add_y)
            grad_x = grad[rows_of(1, z, tile), :] + (add_x if tile else -add_x)
            grad_y = grad[rows_of(2, z, tile), :] + jnp.where(y_ids == 0, -add_y, add_y)
            grad_z = sigma[rows_of(0, z, tile), :]
            if z == 0:
                lap = lap + rims[64:80, at:at + 128]
                grad_z = grad_z - rims[64:80, at:at + 128]
            if z == 15:
                lap = lap + rims[80:96, at:at + 128]
                grad_z = grad_z + rims[80:96, at:at + 128]
            lap = lap * sigma[rows_of(1, z, tile), :]
            forces = [lap * grad_x, lap * grad_y, lap * grad_z]
            if z % 2 == 0:
                held = forces
            else:
                for a in range(3):
                    force[a, pl.ds(z // 2 * 16, 16), at:at + 128] = held[a] + forces[a]

    def part_copy(a, turn):
        to = lax.rem(layer + turn, n_gz)
        return pltpu.make_async_remote_copy(
            src_ref=fsend.at[to, a], dst_ref=frecv.at[turn - 1, a],
            send_sem=fsent.at[turn - 1, a], recv_sem=fgot.at[turn - 1, a],
            device_id={"gz": to}, device_id_type=MESH)

    for a in range(3):
        block = dot(jnp.concatenate(split3(force[a])[:2], 1), average)
        block = (block.reshape(8, 16, 256) * octant[None]).reshape(128, 256)
        hi, mid, _ = split3(block)
        result = dot(pick, hi) + dot(pick, mid)
        for g in range(n_gz):
            fsend[g, a] = result[g * share:(g + 1) * share]
        for turn in turns:
            part_copy(a, turn).start()
    for a in range(3):
        total = fsend[layer, a]
        for turn in turns:
            part_copy(a, turn).wait()
            total = total + frecv[turn - 1, a]
        for s in range(DENSE):
            part_out[s, a] = total[s * deep:(s + 1) * deep]


def finish(level, force, level_out, force_out, level_sem, force_sem):
    level_copy = pltpu.make_async_copy(level, level_out, level_sem)
    force_copy = pltpu.make_async_copy(force, force_out, force_sem)
    level_copy.start()
    force_copy.start()
    force_copy.wait()
    level_copy.wait()


def shards(n_gx, n_gz, level_set, neighbours, live_count, dense_target):
    share = 64 // n_gz
    vmem = pl.BlockSpec(memory_space=pltpu.VMEM)
    anywhere = pl.BlockSpec(memory_space=pl.ANY)
    dma, f32 = pltpu.SemaphoreType.DMA, jnp.float32
    def far_memory(array):
        return pltpu.with_memory_space_constraint(array, pltpu.HBM)

    level, part = pl.pallas_call(
        functools.partial(kernel, n_gx, n_gz),
        out_shape=(jax.ShapeDtypeStruct(level_set.shape, f32), jax.ShapeDtypeStruct((DENSE, 3, SIDE // n_gz, 256), f32)),
        in_specs=[anywhere, pl.BlockSpec(memory_space=pltpu.SMEM), anywhere, anywhere],
        out_specs=(vmem, vmem),
        scratch_shapes=[
            pltpu.VMEM((6, SLOTS), jnp.int32),
            pltpu.SMEM((SLOTS,), jnp.int32),
            pltpu.VMEM(level_set.shape, f32),
            pltpu.VMEM((3 * AXIS_ROWS, 128), f32),
            pltpu.VMEM((128, 1536), f32),
            pltpu.VMEM((36 * 16, 128), f32),
            pltpu.VMEM((3 * AXIS_ROWS, 128), f32),
            pltpu.VMEM((3 * AXIS_ROWS, 128), f32),
            pltpu.VMEM((AXIS_ROWS, 128), f32),
            pltpu.VMEM((96, 128), f32),
            pltpu.VMEM((96, 128), f32),
            pltpu.VMEM((96, 128), f32),
            pltpu.VMEM((8, 128), f32),
            pltpu.VMEM((8, 768), f32),
            pltpu.VMEM((3, 128, 256), f32),
            pltpu.VMEM((8, 8, 128), f32),
            pltpu.VMEM((8, 8, 128), f32),
            pltpu.VMEM((ROUNDS, 8, 8, 384), f32),
            pltpu.VMEM((ROUNDS, 8, 8, 384), f32),
            pltpu.VMEM((n_gz, 3, share, 256), f32),
            pltpu.VMEM((n_gz - 1, 3, share, 256), f32),
            dma(()), dma(()), dma(()), dma((8,)), dma((8,)), dma((ROUNDS, 8)), dma((ROUNDS, 8)), dma((n_gz - 1, 3)), dma((n_gz - 1, 3)),
        ],
        compiler_params=pltpu.CompilerParams(
            collective_id=0, has_side_effects=True, vmem_limit_bytes=24 << 20),
    )(far_memory(neighbours.T), live_count, far_memory(dense_target), far_memory(level_set))
    results = tuple(pltpu.with_memory_space_constraint(r, pltpu.VMEM) for r in (level, part))
    return pl.pallas_call(
        finish,
        out_shape=tuple(jax.ShapeDtypeStruct(r.shape, f32) for r in results),
        in_specs=[anywhere] * 2,
        out_specs=(anywhere,) * 2,
        scratch_shapes=[dma(()), dma(())],
    )(*results)


def solution(mesh):
    placed = (P(("gx", "gz"), None), P(("gx", "gz"), None), P(("gx", "gz")), P(("gx", "gz")))
    return jax.shard_map(
        functools.partial(shards, mesh.shape["gx"], mesh.shape["gz"]),
        mesh=mesh,
        in_specs=placed,
        out_specs=(P(("gx", "gz"), None), P("gx", None, "gz", None)),
        check_vma=False,
    )
```

```python
import functools
import math

import jax
import jax.numpy as jnp
from jax import lax
from jax.experimental import pallas as pl
from jax.experimental.pallas import tpu as pltpu
from jax.sharding import PartitionSpec as P

SIDE = 16
SLOTS = 16
DENSE = 4
STEPS = 3
ROUNDS = STEPS + 1
BAND_WIDTH = 1.5
MESH = pl.DeviceIdType.MESH

PEERS = (7, 0, 6, 1, 5, 2, 4)
NEAR = (0, 6, 1, 5, 2, 4)
FAR = 7
AXIS_ROWS = 512


def facing(peer):
    return 7 if peer == 7 else 6 - peer


def roll_by(values, by):
    return pltpu.roll(values, by % 128, 1) if by % 128 else values


def pick_tree(rolled, masks):
    count = len(rolled)
    moved = [rolled[-i % count] for i in range(count)]
    for bit, mask in enumerate(masks):
        moved = [jnp.where(mask, moved[(i - (1 << bit)) % count], moved[i]) for i in range(count)]
    return moved


def exchange(values, width, masks):
    moved = pick_tree([roll_by(v, j * width) for j, v in enumerate(values)], masks)
    return [roll_by(v, -i * width) for i, v in enumerate(moved)]


def is_edge(position):
    return min(position, 15 - position) < 3


def lane_masks(rows, width, bits):
    lanes = lax.broadcasted_iota(jnp.int32, (rows, 128), 1)
    return [(lanes & (width << bit)) != 0 for bit in range(bits)]


def weno_axis(u, first, last, sigma, store):
    d = {j: u[j] - u[j - 1] for j in range(first - 2, last + 3)}
    e = {j: d[j + 1] - d[j] for j in range(first - 2, last + 2)}
    s = {j: e[j] - e[j - 1] for j in range(first - 1, last + 2)}
    t = {j: s[j + 1] - s[j] for j in range(first - 1, last + 1)}
    r1, r2, r3 = {}, {}, {}
    for j in range(first - 1, last + 2):
        base = (13.0 / 3.0) * (s[j] * s[j]) + 4e-6
        if j <= last - 1:
            lean = (e[j] + e[j]) + s[j]
            r = pltpu.reciprocal(base + lean * lean, approx=True)
            r1[j] = r * r
        if first <= j <= last:
            lean = e[j] + e[j - 1]
            r = pltpu.reciprocal(base + lean * lean, approx=True)
            r2[j] = 6.0 * (r * r)
        if j >= first + 1:
            lean = s[j] - (e[j - 1] + e[j - 1])
            r = pltpu.reciprocal(base + lean * lean, approx=True)
            r3[j] = r * r
    for i in range(first, last):
        half = 0.5 * t[i]
        left = 3.0 * d[i] + (e[i] + 0.5 * e[i - 1])
        right = left - half
        w3 = 3.0 * r3[i + 1]
        den = (r1[i - 1] + r2[i]) + w3
        num = r1[i - 1] * t[i - 1] + w3 * half
        left = left - num * pltpu.reciprocal(den, approx=True)
        w3 = 3.0 * r1[i]
        den = (r3[i + 2] + r2[i + 1]) + w3
        num = r3[i + 2] * t[i + 1] + w3 * half
        right = right + num * pltpu.reciprocal(den, approx=True)
        m = jnp.maximum(jnp.maximum(sigma(i) * left, -sigma(i) * right), 0.0)
        store(i, m * m)


def split3(x):
    hi = x.astype(jnp.bfloat16)
    rest = x - hi.astype(jnp.float32)
    mid = rest.astype(jnp.bfloat16)
    low = (rest - mid.astype(jnp.float32)).astype(jnp.bfloat16)
    return hi, mid, low


def as_one(mask):
    return jnp.where(mask, 1.0, 0.0).astype(jnp.bfloat16)


def dot_rows(a, b):
    return lax.dot_general(a, b, (((0,), (0,)), ((), ())), preferred_element_type=jnp.float32)


def dot(a, b):
    return lax.dot_general(a, b, (((1,), (0,)), ((), ())), preferred_element_type=jnp.float32)


def kernel(n_gx, n_gz, table, live, target_in, level, level_out, part_out,
           nb, target, start, u, faces, ghost, sigma, grad, speed, missing, near_col, far_col, take, far_sigma, force, request, heard,
           sends, recvs, fsend, frecv,
           table_loaded, target_loaded, loaded, request_sent, request_got, sent, got, fsent, fgot):
    me = lax.axis_index("gx")
    layer = lax.axis_index("gz")

    def peer_id(peer):
        step = n_gx // 2 if peer == 7 else peer - 3
        return {"gx": lax.rem(me + step + n_gx, n_gx)}

    load = pltpu.make_async_copy(level, start, loaded)
    load.start()
    load_table = pltpu.make_async_copy(table, nb, table_loaded)
    load_table.start()
    load_target = pltpu.make_async_copy(target_in, target, target_loaded)
    load_target.start()
    barrier = pltpu.get_barrier_semaphore()
    for peer in PEERS:
        pl.semaphore_signal(barrier, inc=1, device_id=peer_id(peer), device_id_type=MESH)
    for turn in range(1, n_gz):
        pl.semaphore_signal(barrier, inc=1, device_id={"gz": lax.rem(layer + turn, n_gz)}, device_id_type=MESH)

    square_rows = lax.broadcasted_iota(jnp.int32, (128, 128), 0)
    square_lanes = lax.broadcasted_iota(jnp.int32, (128, 128), 1)
    load_table.wait()
    spots = [jnp.broadcast_to(nb[side:side + 1, :], (16, 16)) for side in range(6)]
    spots = jnp.concatenate(spots + [jnp.full((32, 16), -1, jnp.int32)], 0)
    own_spot = lax.broadcasted_iota(jnp.int32, (128, 16), 0) & 15
    own_spot = own_spot == lax.broadcasted_iota(jnp.int32, (128, 16), 1)
    entry = jnp.sum(jnp.where(own_spot, spots, 0).astype(jnp.float32), 1, keepdims=True)
    entry = jnp.broadcast_to(entry, (128, 128)).astype(jnp.int32)
    held = entry >= 0
    away = (entry >> (SLOTS * n_gz).bit_length() - 1) - me + 3
    kind = jnp.minimum(away & (n_gx - 1), 7)
    remote = jnp.logical_and(held, kind != 3)
    face = ((square_rows >> 4) ^ 1) * 16 + (entry & 15)
    mine = as_one(jnp.logical_and(remote, kind == square_lanes))
    before = dot(as_one(square_lanes < square_rows), mine)
    rank = dot((before * mine.astype(jnp.float32)).astype(jnp.bfloat16), jnp.ones((128, 128), jnp.bfloat16))
    slot = kind.astype(jnp.float32) * 8.0 + rank
    slot = jnp.where(remote, slot, -16.0)
    lane_ids = square_lanes.astype(jnp.float32)
    face = face.astype(jnp.float32)
    chosen = as_one(slot == lane_ids)
    asked = dot_rows(chosen, face.astype(jnp.bfloat16))
    asked = asked + dot_rows(as_one(slot + 4.0 == lane_ids), (face + 128.0).astype(jnp.bfloat16))
    request[...] = asked[:64].reshape(8, 8, 128)
    far_col[...] = slot[:96]
    take[...] = dot_rows(chosen, as_one(square_rows == square_lanes))[56:64]
    near_col[...] = jnp.where(jnp.logical_and(held, kind == 3), face, -16.0)[:96]
    missing[...] = jnp.where(held, 0.0, 1.0)[:96]
    faces[96:, :] = jnp.zeros((32, 1536), jnp.float32)

    pl.semaphore_wait(barrier, len(PEERS) + n_gz - 1)
    for peer in PEERS:
        pltpu.make_async_remote_copy(
            src_ref=request.at[peer], dst_ref=heard.at[facing(peer)],
            send_sem=request_sent.at[peer], recv_sem=request_got.at[facing(peer)],
            device_id=peer_id(peer), device_id_type=MESH).start()

    coarse_masks = lane_masks(16, 16, 3)
    fine_masks = lane_masks(16, 1, 4)

    def rows_of(axis, position, tile):
        return pl.ds(axis * AXIS_ROWS + position * 32 + tile * 16, 16)

    def keep_face(axis, position, tile, value):
        depth = min(position, 15 - position)
        if depth < 6:
            side = 2 * axis + (position >= 8)
            at = (depth * 2 + tile) * 128
            faces[side * 16:side * 16 + 16, at:at + 128] = value

    def spread(tile, x_of):
        halves = []
        for ytile in range(2):
            halves += pick_tree([roll_by(x_of(i, ytile), 16 * i) for i in range(8)], coarse_masks)
        zs = pick_tree([roll_by(halves[y], y - 16 * (y % 8)) for y in range(16)], fine_masks)
        for axis, values, width in ((1, halves, 16), (2, zs, 1)):
            for p in range(16):
                value = values[p]
                if is_edge(p):
                    value = roll_by(value, -(p * width))
                    keep_face(axis, p, tile, value)
                u[rows_of(axis, p, tile), :] = value

    def settle():
        for tile in range(2):
            for p in range(3, 13):
                for axis, width in ((1, 16), (2, 1)):
                    value = roll_by(u[rows_of(axis, p, tile), :], -(p * width))
                    u[rows_of(axis, p, tile), :] = value
                    keep_face(axis, p, tile, value)

    load_target.wait()
    load.wait()
    for tile in range(2):
        tops = {}
        for i in range(8):
            for ytile in range(2):
                x = tile * 8 + i
                value = start[:, x * 256 + ytile * 128:x * 256 + ytile * 128 + 128]
                u[rows_of(0, x, ytile), :] = value
                keep_face(0, x, ytile, value)
                sigma[rows_of(0, x, ytile), :] = jnp.where(value > 0.0, 1.0, -1.0)
                speed[rows_of(0, x, ytile), :] = 0.1 * value * lax.rsqrt(value * value + 1.0)
                tops[i, ytile] = value
        spread(tile, lambda i, ytile: tops[i, ytile])
    settle()
    for axis in (1, 2):
        rows = pl.ds(axis * AXIS_ROWS, AXIS_ROWS)
        sigma[rows, :] = jnp.where(u[rows, :] > 0.0, 1.0, -1.0)

    for peer in PEERS:
        pltpu.make_async_remote_copy(
            src_ref=request.at[peer], dst_ref=heard.at[peer],
            send_sem=request_sent.at[peer], recv_sem=request_got.at[peer],
            device_id=peer_id(peer), device_id_type=MESH).wait()

    def copy_of(turn, peer, into):
        return pltpu.make_async_remote_copy(
            src_ref=sends.at[turn, peer], dst_ref=recvs.at[turn, into],
            send_sem=sent.at[turn, peer], recv_sem=got.at[turn, into],
            device_id=peer_id(peer), device_id_type=MESH)

    def serve(turn):
        hi, mid, low = split3(faces[:, :768])
        cols = heard[...].reshape(64, 128)
        left = as_one(cols == lane_ids[:64])
        right = as_one(cols == lane_ids[:64] + 128.0)
        both = jnp.concatenate([left, left], 1)
        out = dot(both, jnp.concatenate([hi[:, :384], mid[:, :384]], 0))
        both = jnp.concatenate([right, right], 1)
        out = out + dot(both, jnp.concatenate([hi[:, 384:], mid[:, 384:]], 0))
        both = jnp.concatenate([left, right], 1)
        out = out + dot(both, jnp.concatenate([low[:, :384], low[:, 384:]], 0))
        sends[turn] = out.reshape(8, 8, 384)
        for peer in PEERS:
            copy_of(turn, peer, facing(peer)).start()
        near = as_one(near_col[...] == lane_ids[:96])
        out = dot(jnp.concatenate([near, near], 1), jnp.concatenate([hi, mid], 0)) + dot(near, low)
        for side in range(6):
            for part in range(6):
                at = (side * 6 + part) * 16
                ghost[at:at + 16, :] = out[side * 16:side * 16 + 16, part * 128:part * 128 + 128]

    def near_faces(turn):
        for peer in NEAR:
            copy_of(turn, peer, peer).wait()
        none = jnp.zeros((8, 384), jnp.float32)
        hi, mid, low = split3(jnp.concatenate([recvs[turn, c] if c in NEAR else none for c in range(8)], 0))
        return jnp.concatenate([hi, mid, low, jnp.zeros_like(low)], 0)

    def put_near(arrived, half):
        fold = jnp.where(lane_ids[:96] >= 64.0, lane_ids[:96] - 64.0, lane_ids[:96])
        pick = as_one(far_col[...] + 4.0 * half == fold)
        return dot(jnp.concatenate([pick, pick], 1), arrived)

    def fetch_near(turn):
        arrived = near_faces(turn)
        for half in range(2):
            out = put_near(arrived, half)
            for side in range(6):
                for part in range(3):
                    at = (side * 6 + half * 3 + part) * 16
                    ghost[at:at + 16, :] += out[side * 16:side * 16 + 16, part * 128:part * 128 + 128]

    def own_cells():
        hi, mid, low = split3(faces[...])
        one = take[...].astype(jnp.bfloat16)
        return dot(jnp.concatenate([one, one], 1), jnp.concatenate([hi, mid], 0)) + dot(one, low)

    def put_far(values):
        parts = [part.astype(jnp.float32) for part in split3(values)]
        parts = jnp.concatenate(parts + [jnp.zeros_like(values)], 0).astype(jnp.bfloat16)
        lanes = lax.broadcasted_iota(jnp.int32, (96, 32), 1)
        rows = jnp.where(lanes < 24, (lanes & 7) + 56, -1).astype(jnp.float32)
        return dot(as_one(far_col[:, :32] == rows), parts)

    def is_far(side):
        return far_col[side * 16:side * 16 + 16, :] >= 56.0

    def far_weno(turn, own):
        copy_of(turn, FAR, FAR).wait()
        came = recvs[turn, FAR]
        other = pltpu.roll(came, 4, 0)
        result = {}
        for tile in range(2):
            values = {}
            for depth in range(3):
                part = depth * 2 + tile
                from_ = came if part < 3 else other
                values[-1 - depth] = from_[:, part % 3 * 128:part % 3 * 128 + 128]
            for depth in range(6):
                at = (depth * 2 + tile) * 128
                values[depth] = own[:, at:at + 128]

            def signs(i):
                return far_sigma[:, (i * 2 + tile) * 128:(i * 2 + tile) * 128 + 128]

            def store(i, value):
                result[i * 2 + tile] = value

            weno_axis(values, 0, 3, signs, store)
        return put_far(jnp.concatenate([result[part] for part in range(6)], 1))

    def column_rows(axis, position, column):
        return pl.ds(axis * AXIS_ROWS + position * 32 + column * 8, 8)

    def ghosts_at(axis, high, depth, column, edge):
        values = ghost[pl.ds((2 * axis + high) * 96 + depth * 32 + column * 8, 8), :]
        gone = missing[pl.ds((2 * axis + high) * 16 + (column % 2) * 8, 8), :]
        return jnp.where(gone > 0.0, edge, values)

    def weno_part(index, low, high):
        axis, column = index // 4, index % 4
        load = lambda i: u[column_rows(axis, i, column), :]
        signs = lambda i: sigma[column_rows(axis, i, column), :]

        def store(i, value):
            grad[column_rows(axis, i, column), :] = value

        if low == 3:
            values = {i: load(i) for i in range(16)}
            weno_axis(values, 3, 13, signs, store)
            return
        values = {i: load(i) for i in range(6)}
        for i in range(3):
            values[-1 - i] = ghosts_at(axis, 0, i, column, values[0])
        weno_axis(values, 0, 3, signs, store)
        values = {i: load(i) for i in range(10, 16)}
        for i in range(3):
            values[16 + i] = ghosts_at(axis, 1, i, column, values[15])
        weno_axis(values, 13, 16, signs, store)

    serve(0)
    first = own_cells()[:, :768]
    far_sigma[...] = jnp.where(first > 0.0, 1.0, -1.0)

    def step(turn, carry):

        def inner(index, c):
            weno_part(index, 3, 13)
            return c

        def outer(index, c):
            weno_part(index, 0, 16)
            return c

        lax.fori_loop(0, 12, inner, 0)
        for tile in range(2):
            for p in range(3, 13):
                for axis, width in ((1, 16), (2, 1)):
                    if p * width % 128:
                        rows = rows_of(axis, p, tile)
                        grad[rows, :] = roll_by(grad[rows, :], p * width)
        own = own_cells()
        fetch_near(turn)
        lax.fori_loop(0, 12, outer, 0)
        fixed = far_weno(turn, own)

        def grad_at(axis, position, tile):
            value = grad[rows_of(axis, position, tile), :]
            depth = min(position, 15 - position)
            if depth >= 3:
                return value
            side = 2 * axis + (position >= 8)
            at = (depth * 2 + tile) * 128
            return jnp.where(is_far(side), fixed[side * 16:side * 16 + 16, at:at + 128], value)

        for tile in range(2):
            zs = [grad_at(2, z, tile) for z in range(16)]
            zs = pick_tree([roll_by(v, z) if is_edge(z) else v for z, v in enumerate(zs)], fine_masks)
            sums = []
            for y in range(16):
                value = grad_at(1, y, tile)
                value = roll_by(value, 16 * y) if is_edge(y) else value
                sums.append(roll_by(zs[y], 16 * y - y) + value)
            fresh = {}
            for ytile in range(2):
                xs = pick_tree(sums[ytile * 8:ytile * 8 + 8], coarse_masks)
                for i in range(8):
                    rows = rows_of(0, tile * 8 + i, ytile)
                    steep = jnp.sqrt(roll_by(xs[i], -16 * i) + grad_at(0, tile * 8 + i, ytile))
                    value = u[rows, :] - speed[rows, :] * (steep - 3.0)
                    u[rows, :] = value
                    keep_face(0, tile * 8 + i, ytile, value)
                    fresh[i, ytile] = value
            spread(tile, lambda i, ytile: fresh[i, ytile])
        serve(turn + 1)
        settle()
        return carry

    lax.fori_loop(0, STEPS, step, 0)

    keep = lax.broadcasted_iota(jnp.int32, (16, 128), 0) < live[0]
    for x in range(16):
        for ytile in range(2):
            at = x * 256 + ytile * 128
            level_out[:, at:at + 128] = jnp.where(keep, u[rows_of(0, x, ytile), :], 0.0)

    r = lax.broadcasted_iota(jnp.int32, (256, 256), 0)
    l = lax.broadcasted_iota(jnp.int32, (256, 256), 1)
    same = jnp.logical_and((r >> 5) == ((l >> 4) & 7), ((r >> 1) & 7) == (l & 7))
    average = jnp.where(same, 1.0 / 16.0, 0.0).astype(jnp.bfloat16)
    average = jnp.concatenate([average, average], 0)
    swap = as_one(l == (r & 15) * 16 + (r >> 4))
    swap = jnp.concatenate([swap, swap, swap], 0)
    lanes = lax.broadcasted_iota(jnp.int32, (16, 256), 1)
    brick_rows = lax.broadcasted_iota(jnp.int32, (16, 256), 0)
    lane_bricks = lax.broadcasted_iota(jnp.int32, (64, 128), 1)
    by_row = jnp.zeros((16, 256), jnp.int32)
    by_lane = jnp.full((64, 128), -1, jnp.int32)
    for b in range(16):
        by_row = jnp.where(brick_rows == b, target[b], by_row)
        by_lane = jnp.where((lane_bricks & 15) == b, target[b], by_lane)
    octant = jnp.logical_and(((by_row >> 2) & 1) == (lanes >> 7), ((by_row >> 1) & 1) == ((lanes >> 3) & 1))
    octant = jnp.where(octant, 1.0, 0.0)
    share, deep = 64 // n_gz, SIDE // n_gz
    out_rows = lax.broadcasted_iota(jnp.int32, (64, 128), 0)
    out_z = (out_rows // share) * deep + (out_rows & (deep - 1))
    pick = jnp.logical_and((by_lane >> 3) == (out_rows & (share - 1)) // deep, (by_lane & 1) == (out_z >> 3))
    pick = as_one(jnp.logical_and(pick, (lane_bricks >> 4) == (out_z & 7)))
    turns = sorted(range(1, n_gz), key=lambda turn: abs(2 * turn - n_gz))


    def rim(axis, high, tile, edge):
        side = 2 * axis + high
        values = ghost[side * 96 + tile * 16:side * 96 + tile * 16 + 16, :]
        return jnp.where(missing[side * 16:side * 16 + 16, :] > 0.0, edge, values)

    def beside(axis, position, tile):
        here = u[rows_of(axis, position, tile), :]
        low = rim(axis, 0, tile, here) if position == 0 else u[rows_of(axis, position - 1, tile), :]
        high = rim(axis, 1, tile, here) if position == 15 else u[rows_of(axis, position + 1, tile), :]
        return (high + low) - (here + here), high - low, here

    for tile in range(2):
        lap_y, grad_x = [], []
        for ytile in range(2):
            parts = [beside(0, tile * 8 + i, ytile) for i in range(8)]
            lap_y += exchange([p[0] for p in parts], 16, coarse_masks)
            grad_x += exchange([p[1] for p in parts], 16, coarse_masks)
        parts = [beside(1, y, tile) for y in range(16)]
        laps = exchange([lap_y[y] + parts[y][0] for y in range(16)], 1, fine_masks)
        grad_x = exchange(grad_x, 1, fine_masks)
        grad_y = exchange([p[1] for p in parts], 1, fine_masks)
        for z in range(16):
            lap, grad_z, here = beside(2, z, tile)
            v2 = jnp.minimum(here * here, BAND_WIDTH * BAND_WIDTH) * ((math.pi / 3.0) ** 2)
            wave = 1.0 / 479001600.0
            for power in (-1.0 / 3628800.0, 1.0 / 40320.0, -1.0 / 720.0, 1.0 / 24.0, -0.5, 1.0):
                wave = wave * v2 + power
            grad[rows_of(0, z, tile), :] = lap + laps[z]
            grad[rows_of(1, z, tile), :] = grad_x[z]
            grad[rows_of(2, z, tile), :] = grad_y[z]
            sigma[rows_of(0, z, tile), :] = grad_z
            sigma[rows_of(1, z, tile), :] = jnp.where(jnp.abs(here) < BAND_WIDTH, wave * wave * (2.0 / 3.0), 0.0)

    rims = put_near(near_faces(STEPS)[:, :256], 0)
    copy_of(STEPS, FAR, FAR).wait()
    rims = rims + put_far(recvs[STEPS, FAR, :, :256])
    turned = dot(jnp.concatenate(split3(rims[:32]), 1), swap)
    groups = lax.broadcasted_iota(jnp.int32, (16, 128), 1)
    y_ids, x_ids = groups & 15, groups >> 4

    for tile in range(2):
        edge = 7 * tile
        held = None
        low_y = rims[32:48, tile * 128:tile * 128 + 128]
        high_y = roll_by(rims[48:64, tile * 128:tile * 128 + 128], 15)
        for z in range(16):
            at = z // 8 * 128
            add_x = roll_by(turned[tile * 16:tile * 16 + 16, at:at + 128], 16 * (edge - z % 8))
            add_x = jnp.where(x_ids == edge, add_x, 0.0)
            add_y = roll_by(jnp.where(y_ids == z, low_y, high_y), -z)
            add_y = jnp.where(jnp.logical_or(y_ids == 0, y_ids == 15), add_y, 0.0)
            at = tile * 128
            lap = grad[rows_of(0, z, tile), :] + (add_x + add_y)
            grad_x = grad[rows_of(1, z, tile), :] + (add_x if tile else -add_x)
            grad_y = grad[rows_of(2, z, tile), :] + jnp.where(y_ids == 0, -add_y, add_y)
            grad_z = sigma[rows_of(0, z, tile), :]
            if z == 0:
                lap = lap + rims[64:80, at:at + 128]
                grad_z = grad_z - rims[64:80, at:at + 128]
            if z == 15:
                lap = lap + rims[80:96, at:at + 128]
                grad_z = grad_z + rims[80:96, at:at + 128]
            lap = lap * sigma[rows_of(1, z, tile), :]
            forces = [lap * grad_x, lap * grad_y, lap * grad_z]
            if z % 2 == 0:
                held = forces
            else:
                for a in range(3):
                    force[a, pl.ds(z // 2 * 16, 16), at:at + 128] = held[a] + forces[a]

    def part_copy(a, turn):
        to = lax.rem(layer + turn, n_gz)
        return pltpu.make_async_remote_copy(
            src_ref=fsend.at[to, a], dst_ref=frecv.at[turn - 1, a],
            send_sem=fsent.at[turn - 1, a], recv_sem=fgot.at[turn - 1, a],
            device_id={"gz": to}, device_id_type=MESH)

    for a in range(3):
        block = dot(jnp.concatenate(split3(force[a])[:2], 1), average)
        block = (block.reshape(8, 16, 256) * octant[None]).reshape(128, 256)
        hi, mid, _ = split3(block)
        result = dot(pick, hi) + dot(pick, mid)
        for g in range(n_gz):
            fsend[g, a] = result[g * share:(g + 1) * share]
        for turn in turns:
            part_copy(a, turn).start()
    for a in range(3):
        total = fsend[layer, a]
        for turn in turns:
            part_copy(a, turn).wait()
            total = total + frecv[turn - 1, a]
        for s in range(DENSE):
            part_out[s, a] = total[s * deep:(s + 1) * deep]


def finish(level, force, level_out, force_out, level_sem, force_sem):
    level_copy = pltpu.make_async_copy(level, level_out, level_sem)
    force_copy = pltpu.make_async_copy(force, force_out, force_sem)
    level_copy.start()
    force_copy.start()
    force_copy.wait()
    level_copy.wait()


def shards(n_gx, n_gz, level_set, neighbours, live_count, dense_target):
    share = 64 // n_gz
    vmem = pl.BlockSpec(memory_space=pltpu.VMEM)
    anywhere = pl.BlockSpec(memory_space=pl.ANY)
    dma, f32 = pltpu.SemaphoreType.DMA, jnp.float32
    def far_memory(array):
        return pltpu.with_memory_space_constraint(array, pltpu.HBM)

    level, part = pl.pallas_call(
        functools.partial(kernel, n_gx, n_gz),
        out_shape=(jax.ShapeDtypeStruct(level_set.shape, f32), jax.ShapeDtypeStruct((DENSE, 3, SIDE // n_gz, 256), f32)),
        in_specs=[anywhere, pl.BlockSpec(memory_space=pltpu.SMEM), anywhere, anywhere],
        out_specs=(vmem, vmem),
        scratch_shapes=[
            pltpu.VMEM((6, SLOTS), jnp.int32),
            pltpu.SMEM((SLOTS,), jnp.int32),
            pltpu.VMEM(level_set.shape, f32),
            pltpu.VMEM((3 * AXIS_ROWS, 128), f32),
            pltpu.VMEM((128, 1536), f32),
            pltpu.VMEM((36 * 16, 128), f32),
            pltpu.VMEM((3 * AXIS_ROWS, 128), f32),
            pltpu.VMEM((3 * AXIS_ROWS, 128), f32),
            pltpu.VMEM((AXIS_ROWS, 128), f32),
            pltpu.VMEM((96, 128), f32),
            pltpu.VMEM((96, 128), f32),
            pltpu.VMEM((96, 128), f32),
            pltpu.VMEM((8, 128), f32),
            pltpu.VMEM((8, 768), f32),
            pltpu.VMEM((3, 128, 256), f32),
            pltpu.VMEM((8, 8, 128), f32),
            pltpu.VMEM((8, 8, 128), f32),
            pltpu.VMEM((ROUNDS, 8, 8, 384), f32),
            pltpu.VMEM((ROUNDS, 8, 8, 384), f32),
            pltpu.VMEM((n_gz, 3, share, 256), f32),
            pltpu.VMEM((n_gz - 1, 3, share, 256), f32),
            dma(()), dma(()), dma(()), dma((8,)), dma((8,)), dma((ROUNDS, 8)), dma((ROUNDS, 8)), dma((n_gz - 1, 3)), dma((n_gz - 1, 3)),
        ],
        compiler_params=pltpu.CompilerParams(
            collective_id=0, has_side_effects=True, vmem_limit_bytes=24 << 20),
    )(far_memory(neighbours.T), live_count, far_memory(dense_target), far_memory(level_set))
    results = tuple(pltpu.with_memory_space_constraint(r, pltpu.VMEM) for r in (level, part))
    return pl.pallas_call(
        finish,
        out_shape=tuple(jax.ShapeDtypeStruct(r.shape, f32) for r in results),
        in_specs=[anywhere] * 2,
        out_specs=(anywhere,) * 2,
        scratch_shapes=[dma(()), dma(())],
    )(*results)


def solution(mesh):
    placed = (P(("gx", "gz"), None), P(("gx", "gz"), None), P(("gx", "gz")), P(("gx", "gz")))
    return jax.shard_map(
        functools.partial(shards, mesh.shape["gx"], mesh.shape["gz"]),
        mesh=mesh,
        in_specs=placed,
        out_specs=(P(("gx", "gz"), None), P("gx", None, "gz", None)),
        check_vma=False,
    )
```

```python
import functools
import math

import jax
import jax.numpy as jnp
from jax import lax
from jax.experimental import pallas as pl
from jax.experimental.pallas import tpu as pltpu
from jax.sharding import PartitionSpec as P

SIDE = 16
SLOTS = 16
DENSE = 4
STEPS = 3
ROUNDS = STEPS + 1
BAND_WIDTH = 1.5
MESH = pl.DeviceIdType.MESH

PEERS = (7, 0, 6, 1, 5, 2, 4)
NEAR = (0, 6, 1, 5, 2, 4)
FAR = 7
AXIS_ROWS = 512


def facing(peer):
    return 7 if peer == 7 else 6 - peer


def roll_by(values, by):
    return pltpu.roll(values, by % 128, 1) if by % 128 else values


def pick_tree(rolled, masks):
    count = len(rolled)
    moved = [rolled[-i % count] for i in range(count)]
    for bit, mask in enumerate(masks):
        moved = [jnp.where(mask, moved[(i - (1 << bit)) % count], moved[i]) for i in range(count)]
    return moved


def exchange(values, width, masks):
    moved = pick_tree([roll_by(v, j * width) for j, v in enumerate(values)], masks)
    return [roll_by(v, -i * width) for i, v in enumerate(moved)]


def is_edge(position):
    return min(position, 15 - position) < 3


def lane_masks(rows, width, bits):
    lanes = lax.broadcasted_iota(jnp.int32, (rows, 128), 1)
    return [(lanes & (width << bit)) != 0 for bit in range(bits)]


def weno_axis(u, first, last, sigma, store):
    d = {j: u[j] - u[j - 1] for j in range(first - 2, last + 3)}
    e = {j: d[j + 1] - d[j] for j in range(first - 2, last + 2)}
    s = {j: e[j] - e[j - 1] for j in range(first - 1, last + 2)}
    t = {j: s[j + 1] - s[j] for j in range(first - 1, last + 1)}
    r1, r2, r3 = {}, {}, {}
    for j in range(first - 1, last + 2):
        base = (13.0 / 3.0) * (s[j] * s[j]) + 4e-6
        if j <= last - 1:
            lean = (e[j] + e[j]) + s[j]
            r = pltpu.reciprocal(base + lean * lean, approx=True)
            r1[j] = r * r
        if first <= j <= last:
            lean = e[j] + e[j - 1]
            r = pltpu.reciprocal(base + lean * lean, approx=True)
            r2[j] = 6.0 * (r * r)
        if j >= first + 1:
            lean = s[j] - (e[j - 1] + e[j - 1])
            r = pltpu.reciprocal(base + lean * lean, approx=True)
            r3[j] = r * r
    for i in range(first, last):
        half = 0.5 * t[i]
        left = 3.0 * d[i] + (e[i] + 0.5 * e[i - 1])
        right = left - half
        w3 = 3.0 * r3[i + 1]
        den = (r1[i - 1] + r2[i]) + w3
        num = r1[i - 1] * t[i - 1] + w3 * half
        left = left - num * pltpu.reciprocal(den, approx=True)
        w3 = 3.0 * r1[i]
        den = (r3[i + 2] + r2[i + 1]) + w3
        num = r3[i + 2] * t[i + 1] + w3 * half
        right = right + num * pltpu.reciprocal(den, approx=True)
        m = jnp.maximum(jnp.maximum(sigma(i) * left, -sigma(i) * right), 0.0)
        store(i, m * m)


def split3(x):
    hi = x.astype(jnp.bfloat16)
    rest = x - hi.astype(jnp.float32)
    mid = rest.astype(jnp.bfloat16)
    low = (rest - mid.astype(jnp.float32)).astype(jnp.bfloat16)
    return hi, mid, low


def as_one(mask):
    return jnp.where(mask, 1.0, 0.0).astype(jnp.bfloat16)


def dot_rows(a, b):
    return lax.dot_general(a, b, (((0,), (0,)), ((), ())), preferred_element_type=jnp.float32)


def dot(a, b):
    return lax.dot_general(a, b, (((1,), (0,)), ((), ())), preferred_element_type=jnp.float32)


def kernel(n_gx, n_gz, table, live, target_in, level, level_out, part_out,
           nb, target, start, u, faces, ghost, sigma, grad, speed, lean, missing, near_col, far_col, take, far_sigma, force, request, heard,
           sends, recvs, fsend, frecv,
           table_loaded, target_loaded, loaded, request_sent, request_got, sent, got, fsent, fgot):
    me = lax.axis_index("gx")
    layer = lax.axis_index("gz")

    def peer_id(peer):
        step = n_gx // 2 if peer == 7 else peer - 3
        return {"gx": lax.rem(me + step + n_gx, n_gx)}

    load = pltpu.make_async_copy(level, start, loaded)
    load.start()
    load_table = pltpu.make_async_copy(table, nb, table_loaded)
    load_table.start()
    load_target = pltpu.make_async_copy(target_in, target, target_loaded)
    load_target.start()
    barrier = pltpu.get_barrier_semaphore()
    for peer in PEERS:
        pl.semaphore_signal(barrier, inc=1, device_id=peer_id(peer), device_id_type=MESH)
    for turn in range(1, n_gz):
        pl.semaphore_signal(barrier, inc=1, device_id={"gz": lax.rem(layer + turn, n_gz)}, device_id_type=MESH)

    square_rows = lax.broadcasted_iota(jnp.int32, (128, 128), 0)
    square_lanes = lax.broadcasted_iota(jnp.int32, (128, 128), 1)
    load_table.wait()
    spots = [jnp.broadcast_to(nb[side:side + 1, :], (16, 16)) for side in range(6)]
    spots = jnp.concatenate(spots + [jnp.full((32, 16), -1, jnp.int32)], 0)
    own_spot = lax.broadcasted_iota(jnp.int32, (128, 16), 0) & 15
    own_spot = own_spot == lax.broadcasted_iota(jnp.int32, (128, 16), 1)
    entry = jnp.sum(jnp.where(own_spot, spots, 0).astype(jnp.float32), 1, keepdims=True)
    entry = jnp.broadcast_to(entry, (128, 128)).astype(jnp.int32)
    held = entry >= 0
    away = (entry >> (SLOTS * n_gz).bit_length() - 1) - me + 3
    kind = jnp.minimum(away & (n_gx - 1), 7)
    remote = jnp.logical_and(held, kind != 3)
    face = ((square_rows >> 4) ^ 1) * 16 + (entry & 15)
    mine = as_one(jnp.logical_and(remote, kind == square_lanes))
    before = dot(as_one(square_lanes < square_rows), mine)
    rank = dot((before * mine.astype(jnp.float32)).astype(jnp.bfloat16), jnp.ones((128, 128), jnp.bfloat16))
    slot = kind.astype(jnp.float32) * 8.0 + rank
    slot = jnp.where(remote, slot, -16.0)
    lane_ids = square_lanes.astype(jnp.float32)
    face = face.astype(jnp.float32)
    chosen = as_one(slot == lane_ids)
    asked = dot_rows(chosen, face.astype(jnp.bfloat16))
    asked = asked + dot_rows(as_one(slot + 4.0 == lane_ids), (face + 128.0).astype(jnp.bfloat16))
    request[...] = asked[:64].reshape(8, 8, 128)
    far_col[...] = slot[:96]
    take[...] = dot_rows(chosen, as_one(square_rows == square_lanes))[56:64]
    near_col[...] = jnp.where(jnp.logical_and(held, kind == 3), face, -16.0)[:96]
    missing[...] = jnp.where(held, 0.0, 1.0)[:96]
    faces[96:, :] = jnp.zeros((32, 1536), jnp.float32)

    pl.semaphore_wait(barrier, len(PEERS) + n_gz - 1)
    for peer in PEERS:
        pltpu.make_async_remote_copy(
            src_ref=request.at[peer], dst_ref=heard.at[facing(peer)],
            send_sem=request_sent.at[peer], recv_sem=request_got.at[facing(peer)],
            device_id=peer_id(peer), device_id_type=MESH).start()

    coarse_masks = lane_masks(16, 16, 3)
    fine_masks = lane_masks(16, 1, 4)

    def rows_of(axis, position, tile):
        return pl.ds(axis * AXIS_ROWS + position * 32 + tile * 16, 16)

    def keep_face(axis, position, tile, value):
        depth = min(position, 15 - position)
        if depth < 6:
            side = 2 * axis + (position >= 8)
            at = (depth * 2 + tile) * 128
            faces[side * 16:side * 16 + 16, at:at + 128] = value

    def spread(tile, x_of):
        halves = []
        for ytile in range(2):
            halves += pick_tree([x_of(i, ytile) for i in range(8)], coarse_masks)
        zs = pick_tree([roll_by(halves[y], y - 16 * (y % 8)) for y in range(16)], fine_masks)
        for axis, values, width in ((1, halves, 16), (2, zs, 1)):
            for p in range(16):
                value = values[p]
                if is_edge(p):
                    value = roll_by(value, -(p * width))
                    keep_face(axis, p, tile, value)
                u[rows_of(axis, p, tile), :] = value

    def put_x(x, ytile, rolled):
        rows = rows_of(0, x, ytile)
        lean[rows, :] = rolled
        if is_edge(x):
            value = roll_by(rolled, -16 * x)
            keep_face(0, x, ytile, value)
            u[rows, :] = value
        else:
            u[rows, :] = rolled

    def settle():
        for tile in range(2):
            for p in range(3, 13):
                for axis, width in ((0, 16), (1, 16), (2, 1)):
                    value = roll_by(u[rows_of(axis, p, tile), :], -(p * width))
                    u[rows_of(axis, p, tile), :] = value
                    keep_face(axis, p, tile, value)

    load_target.wait()
    load.wait()
    for tile in range(2):
        tops = {}
        for i in range(8):
            for ytile in range(2):
                x = tile * 8 + i
                value = start[:, x * 256 + ytile * 128:x * 256 + ytile * 128 + 128]
                sigma[rows_of(0, x, ytile), :] = jnp.where(value > 0.0, 1.0, -1.0)
                rolled = roll_by(value, 16 * x)
                speed[rows_of(0, x, ytile), :] = 0.1 * rolled * lax.rsqrt(rolled * rolled + 1.0)
                put_x(x, ytile, rolled)
                tops[i, ytile] = rolled
        spread(tile, lambda i, ytile: tops[i, ytile])
    settle()
    for axis in (1, 2):
        rows = pl.ds(axis * AXIS_ROWS, AXIS_ROWS)
        sigma[rows, :] = jnp.where(u[rows, :] > 0.0, 1.0, -1.0)

    for peer in PEERS:
        pltpu.make_async_remote_copy(
            src_ref=request.at[peer], dst_ref=heard.at[peer],
            send_sem=request_sent.at[peer], recv_sem=request_got.at[peer],
            device_id=peer_id(peer), device_id_type=MESH).wait()

    def copy_of(turn, peer, into):
        return pltpu.make_async_remote_copy(
            src_ref=sends.at[turn, peer], dst_ref=recvs.at[turn, into],
            send_sem=sent.at[turn, peer], recv_sem=got.at[turn, into],
            device_id=peer_id(peer), device_id_type=MESH)

    def serve(turn):
        hi, mid, low = split3(faces[:, :768])
        cols = heard[...].reshape(64, 128)
        left = as_one(cols == lane_ids[:64])
        right = as_one(cols == lane_ids[:64] + 128.0)
        both = jnp.concatenate([left, left], 1)
        out = dot(both, jnp.concatenate([hi[:, :384], mid[:, :384]], 0))
        both = jnp.concatenate([right, right], 1)
        out = out + dot(both, jnp.concatenate([hi[:, 384:], mid[:, 384:]], 0))
        both = jnp.concatenate([left, right], 1)
        out = out + dot(both, jnp.concatenate([low[:, :384], low[:, 384:]], 0))
        sends[turn] = out.reshape(8, 8, 384)
        for peer in PEERS:
            copy_of(turn, peer, facing(peer)).start()
        near = as_one(near_col[...] == lane_ids[:96])
        out = dot(jnp.concatenate([near, near], 1), jnp.concatenate([hi, mid], 0)) + dot(near, low)
        for side in range(6):
            for part in range(6):
                at = (side * 6 + part) * 16
                ghost[at:at + 16, :] = out[side * 16:side * 16 + 16, part * 128:part * 128 + 128]

    def near_faces(turn):
        for peer in NEAR:
            copy_of(turn, peer, peer).wait()
        none = jnp.zeros((8, 384), jnp.float32)
        hi, mid, low = split3(jnp.concatenate([recvs[turn, c] if c in NEAR else none for c in range(8)], 0))
        return jnp.concatenate([hi, mid, low, jnp.zeros_like(low)], 0)

    def put_near(arrived, half):
        fold = jnp.where(lane_ids[:96] >= 64.0, lane_ids[:96] - 64.0, lane_ids[:96])
        pick = as_one(far_col[...] + 4.0 * half == fold)
        return dot(jnp.concatenate([pick, pick], 1), arrived)

    def fetch_near(turn):
        arrived = near_faces(turn)
        for half in range(2):
            out = put_near(arrived, half)
            for side in range(6):
                for part in range(3):
                    at = (side * 6 + half * 3 + part) * 16
                    ghost[at:at + 16, :] += out[side * 16:side * 16 + 16, part * 128:part * 128 + 128]

    def own_cells():
        hi, mid, low = split3(faces[...])
        one = take[...].astype(jnp.bfloat16)
        return dot(jnp.concatenate([one, one], 1), jnp.concatenate([hi, mid], 0)) + dot(one, low)

    def put_far(values):
        parts = [part.astype(jnp.float32) for part in split3(values)]
        parts = jnp.concatenate(parts + [jnp.zeros_like(values)], 0).astype(jnp.bfloat16)
        lanes = lax.broadcasted_iota(jnp.int32, (96, 32), 1)
        rows = jnp.where(lanes < 24, (lanes & 7) + 56, -1).astype(jnp.float32)
        return dot(as_one(far_col[:, :32] == rows), parts)

    def is_far(side):
        return far_col[side * 16:side * 16 + 16, :] >= 56.0

    def far_weno(turn, own):
        copy_of(turn, FAR, FAR).wait()
        came = recvs[turn, FAR]
        other = pltpu.roll(came, 4, 0)
        result = {}
        for tile in range(2):
            values = {}
            for depth in range(3):
                part = depth * 2 + tile
                from_ = came if part < 3 else other
                values[-1 - depth] = from_[:, part % 3 * 128:part % 3 * 128 + 128]
            for depth in range(6):
                at = (depth * 2 + tile) * 128
                values[depth] = own[:, at:at + 128]

            def signs(i):
                return far_sigma[:, (i * 2 + tile) * 128:(i * 2 + tile) * 128 + 128]

            def store(i, value):
                result[i * 2 + tile] = value

            weno_axis(values, 0, 3, signs, store)
        return put_far(jnp.concatenate([result[part] for part in range(6)], 1))

    def column_rows(axis, position, column):
        return pl.ds(axis * AXIS_ROWS + position * 32 + column * 8, 8)

    def ghosts_at(axis, high, depth, column, edge):
        values = ghost[pl.ds((2 * axis + high) * 96 + depth * 32 + column * 8, 8), :]
        gone = missing[pl.ds((2 * axis + high) * 16 + (column % 2) * 8, 8), :]
        return jnp.where(gone > 0.0, edge, values)

    def weno_part(index, low, high):
        axis, column = index // 4, index % 4
        load = lambda i: u[column_rows(axis, i, column), :]
        signs = lambda i: sigma[column_rows(axis, i, column), :]

        def store(i, value):
            grad[column_rows(axis, i, column), :] = value

        if low == 3:
            values = {i: load(i) for i in range(16)}
            weno_axis(values, 3, 13, signs, store)
            return
        values = {i: load(i) for i in range(6)}
        for i in range(3):
            values[-1 - i] = ghosts_at(axis, 0, i, column, values[0])
        weno_axis(values, 0, 3, signs, store)
        values = {i: load(i) for i in range(10, 16)}
        for i in range(3):
            values[16 + i] = ghosts_at(axis, 1, i, column, values[15])
        weno_axis(values, 13, 16, signs, store)

    serve(0)
    first = own_cells()[:, :768]
    far_sigma[...] = jnp.where(first > 0.0, 1.0, -1.0)

    def step(turn, carry):

        def inner(index, c):
            weno_part(index, 3, 13)
            return c

        def outer(index, c):
            weno_part(index, 0, 16)
            return c

        lax.fori_loop(0, 12, inner, 0)
        for tile in range(2):
            for p in range(3, 13):
                for axis, width in ((0, 16), (1, 16), (2, 1)):
                    if p * width % 128:
                        rows = rows_of(axis, p, tile)
                        grad[rows, :] = roll_by(grad[rows, :], p * width)
        own = own_cells()
        fetch_near(turn)
        lax.fori_loop(0, 12, outer, 0)
        fixed = far_weno(turn, own)

        def grad_at(axis, position, tile):
            value = grad[rows_of(axis, position, tile), :]
            depth = min(position, 15 - position)
            if depth >= 3:
                return value
            side = 2 * axis + (position >= 8)
            at = (depth * 2 + tile) * 128
            return jnp.where(is_far(side), fixed[side * 16:side * 16 + 16, at:at + 128], value)

        for tile in range(2):
            zs = [grad_at(2, z, tile) for z in range(16)]
            zs = pick_tree([roll_by(v, z) if is_edge(z) else v for z, v in enumerate(zs)], fine_masks)
            sums = []
            for y in range(16):
                value = grad_at(1, y, tile)
                value = roll_by(value, 16 * y) if is_edge(y) else value
                sums.append(roll_by(zs[y], 16 * y - y) + value)
            fresh = {}
            for ytile in range(2):
                xs = pick_tree(sums[ytile * 8:ytile * 8 + 8], coarse_masks)
                for i in range(8):
                    rows = rows_of(0, tile * 8 + i, ytile)
                    here = grad_at(0, tile * 8 + i, ytile)
                    here = roll_by(here, 16 * i) if is_edge(tile * 8 + i) else here
                    value = lean[rows, :] - speed[rows, :] * (jnp.sqrt(xs[i] + here) - 3.0)
                    put_x(tile * 8 + i, ytile, value)
                    fresh[i, ytile] = value
            spread(tile, lambda i, ytile: fresh[i, ytile])
        serve(turn + 1)
        settle()
        return carry

    lax.fori_loop(0, STEPS, step, 0)

    keep = lax.broadcasted_iota(jnp.int32, (16, 128), 0) < live[0]
    for x in range(16):
        for ytile in range(2):
            at = x * 256 + ytile * 128
            level_out[:, at:at + 128] = jnp.where(keep, u[rows_of(0, x, ytile), :], 0.0)

    r = lax.broadcasted_iota(jnp.int32, (256, 256), 0)
    l = lax.broadcasted_iota(jnp.int32, (256, 256), 1)
    same = jnp.logical_and((r >> 5) == ((l >> 4) & 7), ((r >> 1) & 7) == (l & 7))
    average = jnp.where(same, 1.0 / 16.0, 0.0).astype(jnp.bfloat16)
    average = jnp.concatenate([average, average], 0)
    swap = as_one(l == (r & 15) * 16 + (r >> 4))
    swap = jnp.concatenate([swap, swap, swap], 0)
    lanes = lax.broadcasted_iota(jnp.int32, (16, 256), 1)
    brick_rows = lax.broadcasted_iota(jnp.int32, (16, 256), 0)
    lane_bricks = lax.broadcasted_iota(jnp.int32, (64, 128), 1)
    by_row = jnp.zeros((16, 256), jnp.int32)
    by_lane = jnp.full((64, 128), -1, jnp.int32)
    for b in range(16):
        by_row = jnp.where(brick_rows == b, target[b], by_row)
        by_lane = jnp.where((lane_bricks & 15) == b, target[b], by_lane)
    octant = jnp.logical_and(((by_row >> 2) & 1) == (lanes >> 7), ((by_row >> 1) & 1) == ((lanes >> 3) & 1))
    octant = jnp.where(octant, 1.0, 0.0)
    share, deep = 64 // n_gz, SIDE // n_gz
    out_rows = lax.broadcasted_iota(jnp.int32, (64, 128), 0)
    out_z = (out_rows // share) * deep + (out_rows & (deep - 1))
    pick = jnp.logical_and((by_lane >> 3) == (out_rows & (share - 1)) // deep, (by_lane & 1) == (out_z >> 3))
    pick = as_one(jnp.logical_and(pick, (lane_bricks >> 4) == (out_z & 7)))
    turns = sorted(range(1, n_gz), key=lambda turn: abs(2 * turn - n_gz))


    def rim(axis, high, tile, edge):
        side = 2 * axis + high
        values = ghost[side * 96 + tile * 16:side * 96 + tile * 16 + 16, :]
        return jnp.where(missing[side * 16:side * 16 + 16, :] > 0.0, edge, values)

    def beside(axis, position, tile):
        here = u[rows_of(axis, position, tile), :]
        low = rim(axis, 0, tile, here) if position == 0 else u[rows_of(axis, position - 1, tile), :]
        high = rim(axis, 1, tile, here) if position == 15 else u[rows_of(axis, position + 1, tile), :]
        return (high + low) - (here + here), high - low, here

    for tile in range(2):
        lap_y, grad_x = [], []
        for ytile in range(2):
            parts = [beside(0, tile * 8 + i, ytile) for i in range(8)]
            lap_y += exchange([p[0] for p in parts], 16, coarse_masks)
            grad_x += exchange([p[1] for p in parts], 16, coarse_masks)
        parts = [beside(1, y, tile) for y in range(16)]
        laps = exchange([lap_y[y] + parts[y][0] for y in range(16)], 1, fine_masks)
        grad_x = exchange(grad_x, 1, fine_masks)
        grad_y = exchange([p[1] for p in parts], 1, fine_masks)
        for z in range(16):
            lap, grad_z, here = beside(2, z, tile)
            v2 = jnp.minimum(here * here, BAND_WIDTH * BAND_WIDTH) * ((math.pi / 3.0) ** 2)
            wave = 1.0 / 479001600.0
            for power in (-1.0 / 3628800.0, 1.0 / 40320.0, -1.0 / 720.0, 1.0 / 24.0, -0.5, 1.0):
                wave = wave * v2 + power
            grad[rows_of(0, z, tile), :] = lap + laps[z]
            grad[rows_of(1, z, tile), :] = grad_x[z]
            grad[rows_of(2, z, tile), :] = grad_y[z]
            sigma[rows_of(0, z, tile), :] = grad_z
            sigma[rows_of(1, z, tile), :] = jnp.where(jnp.abs(here) < BAND_WIDTH, wave * wave * (2.0 / 3.0), 0.0)

    rims = put_near(near_faces(STEPS)[:, :256], 0)
    copy_of(STEPS, FAR, FAR).wait()
    rims = rims + put_far(recvs[STEPS, FAR, :, :256])
    turned = dot(jnp.concatenate(split3(rims[:32]), 1), swap)
    groups = lax.broadcasted_iota(jnp.int32, (16, 128), 1)
    y_ids, x_ids = groups & 15, groups >> 4

    for tile in range(2):
        edge = 7 * tile
        held = None
        low_y = rims[32:48, tile * 128:tile * 128 + 128]
        high_y = roll_by(rims[48:64, tile * 128:tile * 128 + 128], 15)
        for z in range(16):
            at = z // 8 * 128
            add_x = roll_by(turned[tile * 16:tile * 16 + 16, at:at + 128], 16 * (edge - z % 8))
            add_x = jnp.where(x_ids == edge, add_x, 0.0)
            add_y = roll_by(jnp.where(y_ids == z, low_y, high_y), -z)
            add_y = jnp.where(jnp.logical_or(y_ids == 0, y_ids == 15), add_y, 0.0)
            at = tile * 128
            lap = grad[rows_of(0, z, tile), :] + (add_x + add_y)
            grad_x = grad[rows_of(1, z, tile), :] + (add_x if tile else -add_x)
            grad_y = grad[rows_of(2, z, tile), :] + jnp.where(y_ids == 0, -add_y, add_y)
            grad_z = sigma[rows_of(0, z, tile), :]
            if z == 0:
                lap = lap + rims[64:80, at:at + 128]
                grad_z = grad_z - rims[64:80, at:at + 128]
            if z == 15:
                lap = lap + rims[80:96, at:at + 128]
                grad_z = grad_z + rims[80:96, at:at + 128]
            lap = lap * sigma[rows_of(1, z, tile), :]
            forces = [lap * grad_x, lap * grad_y, lap * grad_z]
            if z % 2 == 0:
                held = forces
            else:
                for a in range(3):
                    force[a, pl.ds(z // 2 * 16, 16), at:at + 128] = held[a] + forces[a]

    def part_copy(a, turn):
        to = lax.rem(layer + turn, n_gz)
        return pltpu.make_async_remote_copy(
            src_ref=fsend.at[to, a], dst_ref=frecv.at[turn - 1, a],
            send_sem=fsent.at[turn - 1, a], recv_sem=fgot.at[turn - 1, a],
            device_id={"gz": to}, device_id_type=MESH)

    for a in range(3):
        block = dot(jnp.concatenate(split3(force[a])[:2], 1), average)
        block = (block.reshape(8, 16, 256) * octant[None]).reshape(128, 256)
        hi, mid, _ = split3(block)
        result = dot(pick, hi) + dot(pick, mid)
        for g in range(n_gz):
            fsend[g, a] = result[g * share:(g + 1) * share]
        for turn in turns:
            part_copy(a, turn).start()
    for a in range(3):
        total = fsend[layer, a]
        for turn in turns:
            part_copy(a, turn).wait()
            total = total + frecv[turn - 1, a]
        for s in range(DENSE):
            part_out[s, a] = total[s * deep:(s + 1) * deep]


def finish(level, force, level_out, force_out, level_sem, force_sem):
    level_copy = pltpu.make_async_copy(level, level_out, level_sem)
    force_copy = pltpu.make_async_copy(force, force_out, force_sem)
    level_copy.start()
    force_copy.start()
    force_copy.wait()
    level_copy.wait()


def shards(n_gx, n_gz, level_set, neighbours, live_count, dense_target):
    share = 64 // n_gz
    vmem = pl.BlockSpec(memory_space=pltpu.VMEM)
    anywhere = pl.BlockSpec(memory_space=pl.ANY)
    dma, f32 = pltpu.SemaphoreType.DMA, jnp.float32
    def far_memory(array):
        return pltpu.with_memory_space_constraint(array, pltpu.HBM)

    level, part = pl.pallas_call(
        functools.partial(kernel, n_gx, n_gz),
        out_shape=(jax.ShapeDtypeStruct(level_set.shape, f32), jax.ShapeDtypeStruct((DENSE, 3, SIDE // n_gz, 256), f32)),
        in_specs=[anywhere, pl.BlockSpec(memory_space=pltpu.SMEM), anywhere, anywhere],
        out_specs=(vmem, vmem),
        scratch_shapes=[
            pltpu.VMEM((6, SLOTS), jnp.int32),
            pltpu.SMEM((SLOTS,), jnp.int32),
            pltpu.VMEM(level_set.shape, f32),
            pltpu.VMEM((3 * AXIS_ROWS, 128), f32),
            pltpu.VMEM((128, 1536), f32),
            pltpu.VMEM((36 * 16, 128), f32),
            pltpu.VMEM((3 * AXIS_ROWS, 128), f32),
            pltpu.VMEM((3 * AXIS_ROWS, 128), f32),
            pltpu.VMEM((AXIS_ROWS, 128), f32),
            pltpu.VMEM((AXIS_ROWS, 128), f32),
            pltpu.VMEM((96, 128), f32),
            pltpu.VMEM((96, 128), f32),
            pltpu.VMEM((96, 128), f32),
            pltpu.VMEM((8, 128), f32),
            pltpu.VMEM((8, 768), f32),
            pltpu.VMEM((3, 128, 256), f32),
            pltpu.VMEM((8, 8, 128), f32),
            pltpu.VMEM((8, 8, 128), f32),
            pltpu.VMEM((ROUNDS, 8, 8, 384), f32),
            pltpu.VMEM((ROUNDS, 8, 8, 384), f32),
            pltpu.VMEM((n_gz, 3, share, 256), f32),
            pltpu.VMEM((n_gz - 1, 3, share, 256), f32),
            dma(()), dma(()), dma(()), dma((8,)), dma((8,)), dma((ROUNDS, 8)), dma((ROUNDS, 8)), dma((n_gz - 1, 3)), dma((n_gz - 1, 3)),
        ],
        compiler_params=pltpu.CompilerParams(
            collective_id=0, has_side_effects=True, vmem_limit_bytes=24 << 20),
    )(far_memory(neighbours.T), live_count, far_memory(dense_target), far_memory(level_set))
    results = tuple(pltpu.with_memory_space_constraint(r, pltpu.VMEM) for r in (level, part))
    return pl.pallas_call(
        finish,
        out_shape=tuple(jax.ShapeDtypeStruct(r.shape, f32) for r in results),
        in_specs=[anywhere] * 2,
        out_specs=(anywhere,) * 2,
        scratch_shapes=[dma(()), dma(())],
    )(*results)


def solution(mesh):
    placed = (P(("gx", "gz"), None), P(("gx", "gz"), None), P(("gx", "gz")), P(("gx", "gz")))
    return jax.shard_map(
        functools.partial(shards, mesh.shape["gx"], mesh.shape["gz"]),
        mesh=mesh,
        in_specs=placed,
        out_specs=(P(("gx", "gz"), None), P("gx", None, "gz", None)),
        check_vma=False,
    )
```
